32 devices in a mesh: gx: 8 (over y, x, core), gy: 4 (over z).
Axes of the slice: x: 2, y: 2, z: 4, core: 2. Of those that a mesh axis runs over, the one named last changes fastest.
Arguments:
- marker_comp: float32 [16384, 128], P(('gx', 'gy')), may hold values from 0 to 1
- marker_strain: float32 [16384, 128], P(('gx', 'gy')), may hold values from 0.01 to 10
- marker_live: int32 [16384, 128], P(('gx', 'gy')), may hold values 0 or 1
- marker_cell: int32 [16384, 128], P(('gx', 'gy')), may hold values from 0 to 65535, as said below
- block_dest: int32 [16384, 1], P(('gx', 'gy')), may hold values from 0 to 31; in each aligned block of 512 rows (0 to 511, 512 to 1023, ...) at most 32 rows name the same one
- old_logvisc: float32 [128, 128, 128], P('gx', 'gy'), may hold values from -1 to 1
- velocity: float32 [3, 128, 128, 128], P(None, 'gx', 'gy'), may hold values from -6 to 6
Outputs:
- logvisc: float32 [128, 128, 128], P('gx', 'gy')
- density: float32 [128, 128, 128], P('gx', 'gy')
- smoothed: float32 [3, 128, 128, 128], P(None, 'gx', 'gy')
The draws below stay inside these ranges and needn't reach their ends.
Inputs may be any that keep to these rules, and one draw needn't show every extreme that they name: `block_dest`: in the rows of one device no owner is named by more than 32 rows. All markers of one block lie in one column of cells: their marker_cell // 128 are equal.
All inputs are finite; a program needn't handle non-finite values. No bound on the sum of `marker_live` on one device may be relied on, other than what follows from the above.
Results may differ from the reference program's by a relative error of at most 0.0003.
Values sent between devices are 32-bit elements; how exact they have to be, the bound alone decides.
No kernel may reach another device: no remote copies, remote signals or barrier semaphores. Data moves between devices by JAX's collectives and lax.ppermute only.
A program may use at most 64 MiB of HBM per device.

```python
import math
import jax
import jax.numpy as jnp
import numpy as np

CX = 16
CY = 32
NZ = 128
NB_DEV = 512
MARK = 128
SWEEPS = 2
NX = 128
NY = 128
BLOCKS = 16384
CAP = 32
N_GY = 4
DEVICES = 32


def draw_marker_cell(key, part):
    key = jax.random.fold_in(key, 11)
    key_rows, key_depth = jax.random.split(key)
    column_rows = jax.random.randint(key_rows, (BLOCKS, 1), 0, CX * CY, dtype=jnp.int32)
    depth = jax.random.randint(key_depth, (BLOCKS, MARK), 0, NZ, dtype=jnp.int32)
    return column_rows * NZ + depth


def with_ends(array, stream_key, smallest, largest):
    place = [jax.random.randint(jax.random.fold_in(stream_key, axis), (), 0, length) for axis, length in enumerate(array.shape)]
    longest = array.shape.index(max(array.shape))
    next_to = place[:longest] + [(place[longest] + 1) % array.shape[longest]] + place[longest + 1:]
    return array.at[tuple(place)].set(smallest).at[tuple(next_to)].set(largest)


def levels(stream_key, dims, cuts, least, largest):
    def one(axis_at, shards_of):
        heights = jax.random.uniform(jax.random.fold_in(jax.random.fold_in(stream_key, 6), axis_at), (shards_of,), jnp.float32, least / len(cuts), largest / len(cuts))
        return jnp.repeat(jnp.exp(heights), dims[axis_at] // shards_of).reshape((-1,) + (1,) * (len(dims) - axis_at - 1))

    level = one(*cuts[0])
    for cut in cuts[1:]:
        level = level * one(*cut)
    return level


def deal_out(own_key, own, number, rows, count, top, most, skew):
    order = jax.random.permutation(own_key, count)
    heavy_load, common = portions_of(count, rows * top, most, skew, True), portions_of(count, rows * top, most, skew, False)
    places = jnp.arange(count)

    def named(tallies, offset_by):
        used = int((tallies > 0).sum())
        fixed = max(1, used // 4)
        moved = fixed + (places - fixed + offset_by * (used - fixed)) % max(1, count - fixed)
        return jnp.zeros((count,), jnp.int32).at[order[jnp.where(places < fixed, places, moved)]].set(jnp.asarray(tallies, jnp.int32))

    tallies = jnp.where(number % 4 == 0, named(heavy_load, number // 4), named(common, number - number // 4 - 1))
    mixed = jax.random.permutation(jax.random.fold_in(own, 3), count)
    source_of, receiver = mixed[0:count // 2 * 2:2], mixed[1:count // 2 * 2:2]
    room = jnp.minimum(tallies[source_of] - 1, most - tallies[receiver]) // 2
    room = jnp.where((source_of == order[0]) | (receiver == order[0]) | (tallies[receiver] == 0), 0, jnp.maximum(room, 0))
    moved = jax.random.randint(jax.random.fold_in(own, 4), (count // 2,), 0, 1 << 20) % (room + 1)
    tallies = tallies.at[source_of].add(-moved).at[receiver].add(moved)
    members = jnp.searchsorted(jnp.cumsum(tallies), jnp.arange(rows * top), side="right").astype(jnp.int32)
    listing = members.reshape(top, rows).T
    listing = listing[jax.random.permutation(jax.random.fold_in(own, 1), rows)]
    offset_by = jax.random.randint(jax.random.fold_in(own, 2), (rows, 1), 0, top)
    return jnp.take_along_axis(listing, (jnp.arange(top)[None, :] + offset_by) % top, axis=1)


def portions_of(number_of, total, bound, slope, full):
    weights = [(1 << 20) // math.isqrt(grade ** slope) + 1 for grade in range(1, number_of + 1)]
    largest = bound if full else min(bound, max(-(-total // number_of), total * weights[0] // sum(weights)))
    least = 1 if total - largest >= number_of - 1 else 0
    holding, rest = [largest] + [least] * (number_of - 1), total - largest - least * (number_of - 1)
    while rest > 0:
        free = [i for i in range(1, number_of) if holding[i] < largest] or [i for i in range(1, number_of) if holding[i] < bound]
        whole, remaining = sum([weights[i] for i in free]), rest
        for i in free:
            addition = min(bound - holding[i], max(1, remaining * weights[i] // whole), rest)
            holding[i] = holding[i] + addition
            rest = rest - addition
    return np.array(holding)


def scatter_about(stream_key, dims, width, reach, shards=(), kind=jnp.bfloat16):
    array = width * jax.random.normal(stream_key, dims, jnp.float32)
    if shards:
        array = array * levels(stream_key, dims, shards, -0.22, 0.18)
    return jnp.clip(array, -reach, reach).astype(kind)


def setup_inputs(seed: int = 0) -> dict:
    splits = jax.random.split(jax.random.key(seed), 8)
    marker_comp = jnp.clip(1.0 * jax.random.uniform(splits[0], (BLOCKS, MARK), jnp.float32) ** levels(splits[0], (BLOCKS, MARK), ((0, 32),), -0.2, 0.2), 0.0, 1.0)
    marker_strain = jnp.clip(jnp.exp(math.log(10.0) - 6.9077553 * jax.random.uniform(splits[1], (BLOCKS, MARK), jnp.float32) ** levels(splits[1], (BLOCKS, MARK), ((0, 32),), -0.2, 0.2)), 0.01, 10.0)
    marker_live = with_ends((jax.random.randint(splits[2], (BLOCKS, MARK), 0, 4) < 3).astype(jnp.int32), jax.random.fold_in(splits[2], 1), 0, 1)
    marker_cell = draw_marker_cell(jax.random.fold_in(splits[7], 71), 0)
    block_dest_keys = jax.random.split(jax.random.fold_in(splits[4], 1), BLOCKS // NB_DEV)
    block_dest_turns = jax.random.permutation(jax.random.fold_in(splits[4], 3), BLOCKS // NB_DEV)
    block_dest = jax.vmap(lambda own, number: deal_out(jax.random.fold_in(splits[4], 2), own, number, NB_DEV, DEVICES, 1, CAP, 2))(block_dest_keys, block_dest_turns).reshape((BLOCKS, 1))
    old_logvisc = jnp.clip(jax.random.uniform(splits[5], (NX, NY, NZ), jnp.float32, -1.0, 1.0) * levels(splits[5], (NX, NY, NZ), ((0, 8), (1, 4)), -0.4, 0.0), -1.0, 1.0)
    velocity = scatter_about(splits[6], (3, NX, NY, NZ), 1.0, 6.0, ((1, 8), (2, 4)), jnp.float32)
    return dict(marker_comp=marker_comp, marker_strain=marker_strain, marker_live=marker_live, marker_cell=marker_cell, block_dest=block_dest, old_logvisc=old_logvisc, velocity=velocity)


LOG_HIGH = 1.5
LOG_LOW = -1.0
WEAKENING = 1.0
DENSITY_JUMP = 0.4
SOFTENING = 0.1
GRAVITY = 10.0
RELAX = 0.8


def marker_terms(marker_comp, marker_strain, marker_live):
    soften = marker_strain / (1.0 + marker_strain)
    marker_logv = LOG_HIGH * marker_comp + LOG_LOW * (1.0 - marker_comp) - WEAKENING * soften
    marker_rho = 1.0 + DENSITY_JUMP * marker_comp - SOFTENING * soften
    weight = marker_live.astype(jnp.float32)
    return marker_logv, marker_rho, weight


def smooth(viscosity, force_z, velocity, widen_visc, widen_vel):
    padded_visc = widen_visc(viscosity)
    coeffs = [0.5 * (viscosity + padded_visc[2:, 1:-1, 1:-1]),
              0.5 * (viscosity + padded_visc[:-2, 1:-1, 1:-1]),
              0.5 * (viscosity + padded_visc[1:-1, 2:, 1:-1]),
              0.5 * (viscosity + padded_visc[1:-1, :-2, 1:-1]),
              0.5 * (viscosity + padded_visc[1:-1, 1:-1, 2:]),
              0.5 * (viscosity + padded_visc[1:-1, 1:-1, :-2])]
    diag = coeffs[0] + coeffs[1] + coeffs[2] + coeffs[3] + coeffs[4] + coeffs[5]
    zeros_field = jnp.zeros_like(force_z)
    force = jnp.stack([zeros_field, zeros_field, force_z])
    for sweep in range(SWEEPS):
        padded_vel = widen_vel(velocity)
        beside_all = coeffs[0] * padded_vel[:, 2:, 1:-1, 1:-1] + coeffs[1] * padded_vel[:, :-2, 1:-1, 1:-1]
        beside_all = beside_all + coeffs[2] * padded_vel[:, 1:-1, 2:, 1:-1] + coeffs[3] * padded_vel[:, 1:-1, :-2, 1:-1]
        beside_all = beside_all + coeffs[4] * padded_vel[:, 1:-1, 1:-1, 2:] + coeffs[5] * padded_vel[:, 1:-1, 1:-1, :-2]
        operator = diag * velocity - beside_all
        velocity = velocity + RELAX * (force - operator) / diag
    return velocity


def reference(marker_comp, marker_strain, marker_live, marker_cell, block_dest, old_logvisc, velocity):
    marker_logv, marker_rho, weight = marker_terms(marker_comp, marker_strain, marker_live)
    target = block_dest[:, 0].astype(jnp.int32)
    brick_x = (target // N_GY)[:, None]
    brick_y = (target % N_GY)[:, None]
    local_x = marker_cell // (CY * NZ)
    local_y = (marker_cell // NZ) % CY
    local_z = marker_cell % NZ
    flat_index = ((brick_x * CX + local_x) * NY + brick_y * CY + local_y) * NZ + local_z
    flat_index = flat_index.reshape(-1).astype(jnp.int32)
    total_cells = NX * NY * NZ
    sum_logv = jnp.zeros((total_cells,), jnp.float32).at[flat_index].add((weight * marker_logv).reshape(-1))
    sum_rho = jnp.zeros((total_cells,), jnp.float32).at[flat_index].add((weight * marker_rho).reshape(-1))
    count = jnp.zeros((total_cells,), jnp.float32).at[flat_index].add(weight.reshape(-1))
    denominator = count + 1.0
    logvisc = ((sum_logv + old_logvisc.reshape(-1)) / denominator).reshape(NX, NY, NZ)
    density = ((sum_rho + 1.0) / denominator).reshape(NX, NY, NZ)
    viscosity = jnp.exp(logvisc)
    force_z = GRAVITY * (1.0 - density)

    def widen_visc(field):
        return jnp.pad(field, 1)

    def widen_vel(field):
        return jnp.pad(field, ((0, 0), (1, 1), (1, 1), (1, 1)))

    smoothed = smooth(viscosity, force_z, velocity, widen_visc, widen_vel)
    return logvisc, density, smoothed
```

```python
import functools

import jax
import jax.numpy as jnp
from jax import lax
from jax.experimental import pallas as pl
from jax.experimental.pallas import tpu as pltpu
from jax.sharding import PartitionSpec as P

LOG_HIGH = 1.5
LOG_LOW = -1.0
WEAKENING = 1.0
DENSITY_JUMP = 0.4
SOFTENING = 0.1
GRAVITY = 10.0
RELAX = 0.8
BOTH = ("gx", "gy")
F32 = jnp.float32
BF16 = jnp.bfloat16
VMEM = pl.BlockSpec(memory_space=pltpu.VMEM)
SMEM = pl.BlockSpec(memory_space=pltpu.SMEM)
NEAR = 8
FAR = 32
LINE = 48


def split(values):
    high = values.astype(BF16).astype(F32)
    return high, values - high


def pack_kernel(
    slots, chunk, dest_ref, comp_ref, strain_ref, live_ref, cell_ref, out_ref, used_ref
):
    devices = used_ref.shape[0]
    blocks, marks = comp_ref.shape
    shift = marks.bit_length() - 1
    out_ref[...] = jnp.zeros_like(out_ref)
    for owner in range(devices):
        used_ref[owner] = 0
        out_ref[pl.ds(owner * chunk + 3 * slots, 1), :] = jnp.full((1, marks), -1.0, F32)
    depth_ids = lax.broadcasted_iota(jnp.int32, (marks, marks), 0).astype(F32).astype(BF16)
    row_ids = lax.broadcasted_iota(jnp.int32, (48, marks), 0) & 7
    lane_ids = lax.broadcasted_iota(jnp.int32, (1, marks), 1)

    def step(group, carry):
        rows = pl.ds(pl.multiple_of(group * 8, 8), 8)
        comp = comp_ref[rows, :]
        strain = strain_ref[rows, :]
        weight = live_ref[rows, :].astype(F32)
        cell = cell_ref[rows, :]
        soften = strain / (1.0 + strain)
        logv = weight * (LOG_HIGH * comp + LOG_LOW * (1.0 - comp) - WEAKENING * soften)
        rho = weight * (1.0 + DENSITY_JUMP * comp - SOFTENING * soften)
        pieces = [*split(logv), *split(rho), weight, jnp.zeros_like(weight)]
        values = jnp.concatenate(pieces, axis=0)
        depth = (cell & (marks - 1)).astype(F32)
        column = (cell >> shift).astype(F32)
        sums = jnp.zeros((48, marks), F32)
        for pair in range(4):
            left, right = [], []
            for k in (2 * pair, 2 * pair + 1):
                left.append(jnp.where(row_ids == k, values, 0.0).astype(BF16))
                line = jnp.broadcast_to(depth[k : k + 1, :], (16, marks)).astype(BF16)
                line = jnp.concatenate([line] * (marks // 16), axis=0)
                right.append(jnp.where(depth_ids == line, BF16(1.0), BF16(0.0)))
            sums = sums + lax.dot_general(
                jnp.concatenate(left, axis=1),
                jnp.concatenate(right, axis=1),
                (((1,), (1,)), ((), ())),
                preferred_element_type=F32,
            )
        sum_logv = sums[0:8] + sums[8:16]
        sum_rho = sums[16:24] + sums[24:32]
        count = sums[32:40]
        for k in range(8):
            owner = dest_ref[group * 8 + k]
            rank = used_ref[owner]
            used_ref[owner] = rank + 1
            base = owner * chunk
            out_ref[pl.ds(base + rank, 1), :] = sum_logv[k : k + 1]
            out_ref[pl.ds(base + slots + rank, 1), :] = sum_rho[k : k + 1]
            out_ref[pl.ds(base + 2 * slots + rank, 1), :] = count[k : k + 1]
            ids = pl.ds(base + 3 * slots, 1)
            out_ref[ids, :] = jnp.where(lane_ids == rank, column[k : k + 1], out_ref[ids, :])
        return carry

    lax.fori_loop(0, blocks // 8, step, 0)


def average_kernel(
    slots,
    chunk,
    bricks,
    recv_ref,
    old_ref,
    logvisc_ref,
    density_ref,
    visc_ref,
    force_ref,
    x_low_ref,
    x_high_ref,
    y_low_ref,
    y_high_ref,
    hot_ref,
    value_ref,
):
    size_x, size_y = bricks
    columns, depth = old_ref.shape
    total = hot_ref.shape[1]
    per = depth // slots
    lanes = lax.broadcasted_iota(jnp.int32, (1, depth), 1)
    column_ids = lax.broadcasted_iota(jnp.int32, (columns, depth), 0).astype(F32)
    for part in range(total // depth):
        span = slice(part * depth, (part + 1) * depth)
        ids = jnp.full((1, depth), -1.0, F32)
        for k in range(per):
            first = (part * per + k) * chunk
            line = recv_ref[first + 3 * slots : first + 3 * slots + 1, :]
            if k:
                line = pltpu.roll(line, k * slots, 1)
            ids = jnp.where((lanes >= k * slots) & (lanes < (k + 1) * slots), line, ids)
        hot_ref[:, span] = jnp.where(column_ids == ids, 1.0, 0.0).astype(BF16)
        for v in range(3):
            block = jnp.concatenate(
                [
                    recv_ref[pl.ds((part * per + k) * chunk + v * slots, slots), :]
                    for k in range(per)
                ],
                axis=0,
            )
            high, low = split(block)
            value_ref[span, pl.ds(2 * v * depth, depth)] = high.astype(BF16)
            if v < 2:
                value_ref[span, pl.ds((2 * v + 1) * depth, depth)] = low.astype(BF16)
    for tile in range(columns // depth):
        span = slice(tile * depth, (tile + 1) * depth)
        sums = jnp.dot(hot_ref[span, :], value_ref[...], preferred_element_type=F32)
        sum_logv = sums[:, 0:depth] + sums[:, depth : 2 * depth]
        sum_rho = sums[:, 2 * depth : 3 * depth] + sums[:, 3 * depth : 4 * depth]
        count = sums[:, 4 * depth : 5 * depth] + 1.0
        logvisc = (sum_logv + old_ref[span, :]) / count
        density = (sum_rho + 1.0) / count
        logvisc_ref[span, :] = logvisc
        density_ref[span, :] = density
        visc_ref[span, :] = jnp.exp(logvisc)
        force_ref[span, :] = GRAVITY * (1.0 - density)
    near = size_y
    x_low_ref[0 : 2 * near, :] = visc_ref[0 : 2 * near, :]
    x_low_ref[2 * near : 3 * near, :] = force_ref[0:near, :]
    x_high_ref[0 : 2 * near, :] = visc_ref[columns - 2 * near : columns, :]
    x_high_ref[2 * near : 3 * near, :] = force_ref[columns - near : columns, :]
    y_low_ref[...] = jnp.zeros_like(y_low_ref)
    y_high_ref[...] = jnp.zeros_like(y_high_ref)
    for ref, first, second in ((y_low_ref, 0, 1), (y_high_ref, size_y - 1, size_y - 2)):
        ref[NEAR : NEAR + size_x, :] = visc_ref[pl.ds(first, size_x, stride=size_y), :]
        ref[FAR : FAR + size_x, :] = visc_ref[pl.ds(second, size_x, stride=size_y), :]
        ref[LINE : LINE + size_x, :] = force_ref[pl.ds(first, size_x, stride=size_y), :]


def smooth_kernel(
    bricks,
    inside_ref,
    visc_ref,
    force_ref,
    vel_ref,
    vx_low_ref,
    vx_high_ref,
    vy_low_ref,
    vy_high_ref,
    x_low_ref,
    x_high_ref,
    y_low_ref,
    y_high_ref,
    out_ref,
    wide_visc,
    wide_vel,
    wide_next,
    coeff_ref,
):
    size_x, size_y = bricks
    cells, depth = visc_ref.shape
    pitch = size_y + 16
    lanes = lax.broadcasted_iota(jnp.int32, (1, depth), 1)

    def place(ref, offset, core, low, high, near_low, near_high):
        for plane in range(2):
            ref[pl.ds(offset + plane * pitch + 8, size_y), :] = low(plane)
            ref[pl.ds(offset + (size_x + 2 + plane) * pitch + 8, size_y), :] = high(plane)
        for plane in range(size_x):
            ref[pl.ds(offset + (plane + 2) * pitch + 8, size_y), :] = core(plane)
        planes = size_x + 2
        ref[pl.ds(offset + pitch + 7, planes, stride=pitch), :] = near_low
        ref[pl.ds(offset + pitch + 8 + size_y, planes, stride=pitch), :] = near_high

    def block(ref, first, count):
        return ref[pl.ds(first, count), :]

    place(
        wide_visc,
        0,
        lambda p: block(visc_ref, p * size_y, size_y),
        lambda p: block(x_low_ref, p * size_y, size_y),
        lambda p: block(x_high_ref, p * size_y, size_y),
        block(y_low_ref, NEAR - 1, size_x + 2),
        block(y_high_ref, NEAR - 1, size_x + 2),
    )
    field = (size_x + 4) * pitch
    field_next = (size_x + 2) * pitch
    for c in range(3):
        place(
            wide_vel,
            c * field,
            lambda p: block(vel_ref, c * cells + p * size_y, size_y),
            lambda p: block(vx_low_ref, (2 * c + p) * size_y, size_y),
            lambda p: block(vx_high_ref, (2 * c + p) * size_y, size_y),
            block(vy_low_ref, c * LINE + NEAR - 1, size_x + 2),
            block(vy_high_ref, c * LINE + NEAR - 1, size_x + 2),
        )

    def factors(visc, beside, force):
        up = jnp.where(lanes == depth - 1, 0.0, pltpu.roll(visc, depth - 1, 1))
        down = jnp.where(lanes == 0, 0.0, pltpu.roll(visc, 1, 1))
        faces = [visc + other for other in (*beside, up, down)]
        total = ((faces[0] + faces[1]) + (faces[2] + faces[3])) + (faces[4] + faces[5])
        scale = RELAX / total
        faces = [face * scale for face in faces]
        faces[4] = jnp.where(lanes == depth - 1, 0.0, faces[4])
        faces[5] = jnp.where(lanes == 0, 0.0, faces[5])
        return faces, 2.0 * force * scale

    def relax(faces, push, vel, beside):
        up = pltpu.roll(vel, depth - 1, 1)
        down = pltpu.roll(vel, 1, 1)
        terms = [face * other for face, other in zip(faces, (*beside, up, down))]
        result = ((terms[0] + terms[1]) + (terms[2] + terms[3])) + (terms[4] + terms[5])
        result = result + (1.0 - RELAX) * vel
        return result if push is None else result + push

    def around(ref, first):
        return (
            ref[pl.ds(first + pitch, size_y), :],
            ref[pl.ds(first - pitch, size_y), :],
            ref[pl.ds(first + 1, size_y), :],
            ref[pl.ds(first - 1, size_y), :],
        )

    def first_sweep(plane, force):
        at = (plane + 2) * pitch + 8
        faces, push = factors(wide_visc[pl.ds(at, size_y), :], around(wide_visc, at), force)
        results = []
        for c in range(3):
            vel = wide_vel[pl.ds(c * field + at, size_y), :]
            beside = around(wide_vel, c * field + at)
            results.append(relax(faces, push if c == 2 else None, vel, beside))
        return faces, push, results

    def put(plane, results):
        for c in range(3):
            at = c * field_next + (plane + 1) * pitch + 8
            wide_next[pl.ds(at, size_y), :] = results[c]

    for plane, ref, side in ((-1, x_low_ref, 0), (size_x, x_high_ref, 1)):
        _, _, results = first_sweep(plane, ref[pl.ds(2 * size_y, size_y), :])
        put(plane, [jnp.where(inside_ref[side] > 0, value, 0.0) for value in results])

    for row, near_row, visc_lines, vel_lines, side in (
        (7, 0, y_low_ref, vy_low_ref, 2),
        (8 + size_y, size_y - 1, y_high_ref, vy_high_ref, 3),
    ):

        def around_line(ref, first, inner):
            return (
                ref[pl.ds(first + NEAR + 1, size_x), :],
                ref[pl.ds(first + NEAR - 1, size_x), :],
                inner,
                ref[pl.ds(first + FAR, size_x), :],
            )

        inner = visc_ref[pl.ds(near_row, size_x, stride=size_y), :]
        faces, push = factors(
            visc_lines[pl.ds(NEAR, size_x), :],
            around_line(visc_lines, 0, inner),
            visc_lines[pl.ds(LINE, size_x), :],
        )
        for c in range(3):
            inner = vel_ref[pl.ds(c * cells + near_row, size_x, stride=size_y), :]
            value = relax(
                faces,
                push if c == 2 else None,
                vel_lines[pl.ds(c * LINE + NEAR, size_x), :],
                around_line(vel_lines, c * LINE, inner),
            )
            value = jnp.where(inside_ref[side] > 0, value, 0.0)
            at = c * field_next + pitch + row
            wide_next[pl.ds(at, size_x, stride=pitch), :] = value

    for plane in range(size_x):
        faces, push, results = first_sweep(plane, force_ref[pl.ds(plane * size_y, size_y), :])
        put(plane, results)
        for k, value in enumerate((*faces, push)):
            coeff_ref[pl.ds(k * cells + plane * size_y, size_y), :] = value

    for plane in range(size_x):
        faces = [coeff_ref[pl.ds(k * cells + plane * size_y, size_y), :] for k in range(6)]
        push = coeff_ref[pl.ds(6 * cells + plane * size_y, size_y), :]
        for c in range(3):
            at = c * field_next + (plane + 1) * pitch + 8
            vel = wide_next[pl.ds(at, size_y), :]
            value = relax(faces, push if c == 2 else None, vel, around(wide_next, at))
            out_ref[pl.ds(c * cells + plane * size_y, size_y), :] = value


def shifted(value, axis, step):
    count = lax.axis_size(axis)
    pairs = [(i, i + step) for i in range(count) if 0 <= i + step < count]
    return lax.ppermute(value, axis, pairs)


def per_device(
    marker_comp, marker_strain, marker_live, marker_cell, block_dest, old_logvisc, velocity
):
    count_x = lax.axis_size("gx")
    count_y = lax.axis_size("gy")
    devices = count_x * count_y
    blocks, marks = marker_comp.shape
    size_x, size_y, depth = old_logvisc.shape
    columns = size_x * size_y
    slots = 2 * blocks // devices
    chunk = -(-(3 * slots + 1) // 8) * 8
    total = devices * slots

    payload = pl.pallas_call(
        functools.partial(pack_kernel, slots, chunk),
        out_shape=jax.ShapeDtypeStruct((devices * chunk, marks), F32),
        in_specs=[SMEM, VMEM, VMEM, VMEM, VMEM],
        out_specs=VMEM,
        scratch_shapes=[pltpu.SMEM((devices,), jnp.int32)],
        name="pack",
    )(block_dest.reshape(blocks), marker_comp, marker_strain, marker_live, marker_cell)
    received = lax.all_to_all(payload, BOTH, split_axis=0, concat_axis=0, tiled=True)

    vx_low = shifted(velocity[:, size_x - 2 :], "gx", 1)
    vx_high = shifted(velocity[:, :2], "gx", -1)

    def vel_lines(near, far):
        blank = jnp.zeros((3, 7, depth), F32)
        parts = [blank, vx_low[:, 1, near][:, None], velocity[:, :, near]]
        parts += [vx_high[:, 0, near][:, None], blank, velocity[:, :, far]]
        return jnp.concatenate(parts, axis=1)

    vy_low = shifted(vel_lines(size_y - 1, size_y - 2), "gy", 1)
    vy_high = shifted(vel_lines(0, 1), "gy", -1)

    field = jax.ShapeDtypeStruct((columns, depth), F32)
    x_side = jax.ShapeDtypeStruct((3 * size_y, depth), F32)
    y_side = jax.ShapeDtypeStruct((LINE + size_x, depth), F32)
    logvisc, density, visc, force, x_first, x_last, y_first, y_last = pl.pallas_call(
        functools.partial(average_kernel, slots, chunk, (size_x, size_y)),
        out_shape=(field, field, field, field, x_side, x_side, y_side, y_side),
        in_specs=[VMEM, VMEM],
        out_specs=(VMEM,) * 8,
        scratch_shapes=[pltpu.VMEM((columns, total), BF16), pltpu.VMEM((total, 5 * depth), BF16)],
        name="average",
    )(received, old_logvisc.reshape(columns, depth))

    x_low = shifted(x_last, "gx", 1)
    x_high = shifted(x_first, "gx", -1)

    def with_corners(lines, near):
        parts = [lines[:7], x_low[size_y + near][None], lines[8 : 8 + size_x]]
        parts += [x_high[near][None], lines[9 + size_x :]]
        return jnp.concatenate(parts, axis=0)

    y_low = shifted(with_corners(y_last, size_y - 1), "gy", 1)
    y_high = shifted(with_corners(y_first, 0), "gy", -1)

    at_x = lax.axis_index("gx")
    at_y = lax.axis_index("gy")
    inside = jnp.stack([at_x > 0, at_x < count_x - 1, at_y > 0, at_y < count_y - 1])
    pitch = size_y + 16
    smoothed = pl.pallas_call(
        functools.partial(smooth_kernel, (size_x, size_y)),
        out_shape=jax.ShapeDtypeStruct((3 * columns, depth), F32),
        in_specs=[SMEM] + [VMEM] * 11,
        out_specs=VMEM,
        scratch_shapes=[
            pltpu.VMEM(((size_x + 4) * pitch, depth), F32),
            pltpu.VMEM((3 * (size_x + 4) * pitch, depth), F32),
            pltpu.VMEM((3 * (size_x + 2) * pitch, depth), F32),
            pltpu.VMEM((7 * columns, depth), F32),
        ],
        name="smooth",
    )(
        inside.astype(jnp.int32),
        visc,
        force,
        velocity.reshape(3 * columns, depth),
        vx_low.reshape(-1, depth),
        vx_high.reshape(-1, depth),
        vy_low.reshape(-1, depth),
        vy_high.reshape(-1, depth),
        x_low,
        x_high,
        y_low,
        y_high,
    )
    return (
        logvisc.reshape(old_logvisc.shape),
        density.reshape(old_logvisc.shape),
        smoothed.reshape(velocity.shape),
    )


def solution(mesh):
    return jax.shard_map(
        per_device,
        mesh=mesh,
        in_specs=(
            P(("gx", "gy"), None),
            P(("gx", "gy"), None),
            P(("gx", "gy"), None),
            P(("gx", "gy"), None),
            P(("gx", "gy"), None),
            P("gx", "gy", None),
            P(None, "gx", "gy", None),
        ),
        out_specs=(P("gx", "gy", None), P("gx", "gy", None), P(None, "gx", "gy", None)),
        check_vma=False,
    )
```

```python
import functools

import jax
import jax.numpy as jnp
from jax import lax
from jax.experimental import pallas as pl
from jax.experimental.pallas import tpu as pltpu
from jax.sharding import PartitionSpec as P

LOG_HIGH = 1.5
LOG_LOW = -1.0
WEAKENING = 1.0
DENSITY_JUMP = 0.4
SOFTENING = 0.1
GRAVITY = 10.0
RELAX = 0.8
BOTH = ("gx", "gy")
F32 = jnp.float32
BF16 = jnp.bfloat16
VMEM = pl.BlockSpec(memory_space=pltpu.VMEM)
SMEM = pl.BlockSpec(memory_space=pltpu.SMEM)
HBM = pl.BlockSpec(memory_space=pltpu.HBM)
BY_LANES = (((1,), (1,)), ((), ()))
WAYS = 4
BATCH = 32
NEAR = 8
FAR = 32
LINE = 48


def split(values):
    high = values.astype(BF16).astype(F32)
    return high, values - high


def pack_kernel(
    slots,
    chunk,
    dest_hbm,
    comp_hbm,
    strain_hbm,
    live_hbm,
    cell_hbm,
    out_ref,
    place_ref,
    line_ref,
    sums_ref,
    place_sem,
    dest_ref,
    comp_ref,
    strain_ref,
    live_ref,
    cell_ref,
    load_sem,
):
    blocks, marks = comp_ref.shape
    devices = out_ref.shape[0] // chunk
    shift = marks.bit_length() - 1
    part = marks // WAYS
    low_bits = part.bit_length() - 1
    pairs = (
        (dest_hbm, dest_ref),
        (cell_hbm, cell_ref),
        (comp_hbm, comp_ref),
        (strain_hbm, strain_ref),
        (live_hbm, live_ref),
    )
    loads = [pltpu.make_async_copy(*pair, load_sem.at[k]) for k, pair in enumerate(pairs)]
    for load in loads:
        load.start()
    out_ref[...] = jnp.zeros_like(out_ref)
    loads[0].wait()
    loads[1].wait()

    owner_ids = lax.broadcasted_iota(jnp.int32, (devices, marks), 0)
    rank_ids = lax.broadcasted_iota(jnp.int32, (slots, marks), 0)
    square = (marks, marks)
    before = lax.broadcasted_iota(jnp.int32, square, 0) < lax.broadcasted_iota(jnp.int32, square, 1)
    before = jnp.where(before, 1.0, 0.0).astype(BF16)
    seen = jnp.zeros((devices, 1), F32)
    ids = jnp.zeros((devices, slots), F32)
    for k in range(blocks // marks):
        dest = dest_ref[k : k + 1, :]
        mine = owner_ids == dest
        hot = jnp.where(mine, 1.0, 0.0)
        earlier = jnp.dot(hot.astype(BF16), before, preferred_element_type=F32) + seen
        rank = jnp.sum(jnp.where(mine, earlier, 0.0), axis=0, keepdims=True).astype(jnp.int32)
        seen = seen + jnp.sum(hot, axis=1, keepdims=True)
        line_ref[k : k + 1, :] = dest * chunk + rank
        column = (cell_ref[k * marks : (k + 1) * marks, :] >> shift).astype(F32).T[0:1] + 1.0
        spot = jnp.where(rank_ids == rank, 1.0, 0.0).astype(BF16)
        for piece in split(column):
            weighted = jnp.where(mine, piece, 0.0).astype(BF16)
            ids = ids + lax.dot_general(weighted, spot, BY_LANES, preferred_element_type=F32)
    places = pltpu.make_async_copy(line_ref, place_ref, place_sem)
    places.start()
    ids = ids - 1.0
    for owner in range(devices):
        at = owner * chunk + 3 * slots
        out_ref[at : at + 1, 0:slots] = ids[owner : owner + 1, :]
    for load in loads[2:]:
        load.wait()

    fine_ids = lax.broadcasted_iota(jnp.int32, (part, marks), 0).astype(F32).astype(BF16)
    row_ids = lax.broadcasted_iota(jnp.int32, (8, marks), 0)
    lane_ids = lax.broadcasted_iota(jnp.int32, (8, marks), 1)
    halves = [row_ids < 4, row_ids >= 4]
    spans = [(lane_ids >> low_bits) == ((row_ids + w) & (WAYS - 1)) for w in range(WAYS)]

    def depth_sums(group):
        rows = pl.ds(pl.multiple_of(group * 8, 8), 8)
        comp = comp_ref[rows, :]
        strain = strain_ref[rows, :]
        weight = live_ref[rows, :].astype(F32)
        soften = strain / (1.0 + strain)
        logv = weight * (LOG_HIGH * comp + LOG_LOW * (1.0 - comp) - WEAKENING * soften)
        rho = weight * (1.0 + DENSITY_JUMP * comp - SOFTENING * soften)
        pieces = [*split(logv), *split(rho), weight]
        depth = cell_ref[rows, :] & (marks - 1)
        coarse = ((depth >> low_bits) - row_ids) & (WAYS - 1)
        fine = (depth & (part - 1)).astype(F32)
        left, right = [], []
        for half in halves:
            lines = []
            for w in range(WAYS):
                mask = (coarse == w) & half
                lines += [jnp.where(mask, piece, 0.0) for piece in pieces]
            left.append(jnp.concatenate(lines, axis=0).astype(BF16))
        for first in (0, 4):
            lines = []
            for b in range(first, first + 4):
                line = jnp.broadcast_to(fine[b : b + 1, :], (16, marks)).astype(BF16)
                line = jnp.concatenate([line] * (part // 16), axis=0)
                lines.append(jnp.where(fine_ids == line, BF16(1.0), BF16(0.0)))
            right.append(jnp.concatenate(lines, axis=0))
        sums = lax.dot_general(
            jnp.concatenate(left, axis=1),
            jnp.concatenate(right, axis=1),
            BY_LANES,
            preferred_element_type=F32,
        )

        def piece_sum(w, p):
            first = (w * len(pieces) + p) * 8
            return sums[first : first + 8]

        results = []
        for numbers in ((0, 1), (2, 3), (4,)):
            total = None
            for w in range(WAYS):
                value = piece_sum(w, numbers[0])
                if len(numbers) > 1:
                    value = value + piece_sum(w, numbers[1])
                if w:
                    value = pltpu.roll(value, part * w, 1)
                total = value if total is None else jnp.where(spans[w], value, total)
            results.append(total)
        return results

    def batch(step, g, f):
        first = (step & 1) * (24 * BATCH) + g * 24 + f * 8
        return pl.ds(pl.multiple_of(first, 8), 8)

    def put(step):
        for g in range(BATCH):
            for f, value in enumerate(depth_sums(step * BATCH + g)):
                sums_ref[batch(step, g, f), :] = value

    def place(step):
        for g in range(BATCH):
            group = step * BATCH + g
            values = [sums_ref[batch(step, g, f), :] for f in range(3)]
            for k in range(8):
                at = place_ref[group // 16, (group % 16) * 8 + k]
                for f in range(3):
                    out_ref[pl.ds(at + f * slots, 1), :] = values[f][k : k + 1]

    steps = blocks // 8 // BATCH
    put(0)
    places.wait()

    def step(i, carry):
        place(i - 1)
        put(i)
        return carry

    lax.fori_loop(1, steps, step, 0)
    place(steps - 1)


def average_kernel(
    slots,
    chunk,
    bricks,
    recv_ref,
    old_ref,
    logvisc_ref,
    density_ref,
    visc_ref,
    force_ref,
    x_low_ref,
    x_high_ref,
    y_low_ref,
    y_high_ref,
    hot_ref,
    value_ref,
):
    size_x, size_y = bricks
    columns, depth = old_ref.shape
    total = hot_ref.shape[1]
    per = depth // slots
    lanes = lax.broadcasted_iota(jnp.int32, (1, depth), 1)
    column_ids = lax.broadcasted_iota(jnp.int32, (columns, depth), 0).astype(F32)
    for part in range(total // depth):
        span = slice(part * depth, (part + 1) * depth)
        ids = jnp.full((1, depth), -1.0, F32)
        for k in range(per):
            first = (part * per + k) * chunk
            line = recv_ref[first + 3 * slots : first + 3 * slots + 1, :]
            if k:
                line = pltpu.roll(line, k * slots, 1)
            ids = jnp.where((lanes >= k * slots) & (lanes < (k + 1) * slots), line, ids)
        hot_ref[:, span] = jnp.where(column_ids == ids, 1.0, 0.0).astype(BF16)
        for v in range(3):
            block = jnp.concatenate(
                [
                    recv_ref[pl.ds((part * per + k) * chunk + v * slots, slots), :]
                    for k in range(per)
                ],
                axis=0,
            )
            high, low = split(block)
            value_ref[span, pl.ds(2 * v * depth, depth)] = high.astype(BF16)
            if v < 2:
                value_ref[span, pl.ds((2 * v + 1) * depth, depth)] = low.astype(BF16)
    for tile in range(columns // depth):
        span = slice(tile * depth, (tile + 1) * depth)
        sums = jnp.dot(hot_ref[span, :], value_ref[...], preferred_element_type=F32)
        sum_logv = sums[:, 0:depth] + sums[:, depth : 2 * depth]
        sum_rho = sums[:, 2 * depth : 3 * depth] + sums[:, 3 * depth : 4 * depth]
        count = sums[:, 4 * depth : 5 * depth] + 1.0
        logvisc = (sum_logv + old_ref[span, :]) / count
        density = (sum_rho + 1.0) / count
        logvisc_ref[span, :] = logvisc
        density_ref[span, :] = density
        visc_ref[span, :] = jnp.exp(logvisc)
        force_ref[span, :] = GRAVITY * (1.0 - density)
    near = size_y
    x_low_ref[0 : 2 * near, :] = visc_ref[0 : 2 * near, :]
    x_low_ref[2 * near : 3 * near, :] = force_ref[0:near, :]
    x_high_ref[0 : 2 * near, :] = visc_ref[columns - 2 * near : columns, :]
    x_high_ref[2 * near : 3 * near, :] = force_ref[columns - near : columns, :]
    y_low_ref[...] = jnp.zeros_like(y_low_ref)
    y_high_ref[...] = jnp.zeros_like(y_high_ref)
    for ref, first, second in ((y_low_ref, 0, 1), (y_high_ref, size_y - 1, size_y - 2)):
        ref[NEAR : NEAR + size_x, :] = visc_ref[pl.ds(first, size_x, stride=size_y), :]
        ref[FAR : FAR + size_x, :] = visc_ref[pl.ds(second, size_x, stride=size_y), :]
        ref[LINE : LINE + size_x, :] = force_ref[pl.ds(first, size_x, stride=size_y), :]


def smooth_kernel(
    bricks,
    visc_ref,
    force_ref,
    vel_ref,
    vx_low_ref,
    vx_high_ref,
    vy_low_ref,
    vy_high_ref,
    x_low_ref,
    x_high_ref,
    y_low_ref,
    y_high_ref,
    out_ref,
    wide_visc,
    wide_vel,
    wide_next,
    coeff_ref,
):
    size_x, size_y = bricks
    cells, depth = visc_ref.shape
    pitch = size_y + 16
    lanes = lax.broadcasted_iota(jnp.int32, (1, depth), 1)

    def place(ref, offset, core, low, high, near_low, near_high):
        for plane in range(2):
            ref[pl.ds(offset + plane * pitch + 8, size_y), :] = low(plane)
            ref[pl.ds(offset + (size_x + 2 + plane) * pitch + 8, size_y), :] = high(plane)
        for plane in range(size_x):
            ref[pl.ds(offset + (plane + 2) * pitch + 8, size_y), :] = core(plane)
        planes = size_x + 2
        ref[pl.ds(offset + pitch + 7, planes, stride=pitch), :] = near_low
        ref[pl.ds(offset + pitch + 8 + size_y, planes, stride=pitch), :] = near_high

    def block(ref, first, count):
        return ref[pl.ds(first, count), :]

    place(
        wide_visc,
        0,
        lambda p: block(visc_ref, p * size_y, size_y),
        lambda p: block(x_low_ref, p * size_y, size_y),
        lambda p: block(x_high_ref, p * size_y, size_y),
        block(y_low_ref, NEAR - 1, size_x + 2),
        block(y_high_ref, NEAR - 1, size_x + 2),
    )
    field = (size_x + 4) * pitch
    field_next = (size_x + 2) * pitch
    for c in range(3):
        place(
            wide_vel,
            c * field,
            lambda p: block(vel_ref, c * cells + p * size_y, size_y),
            lambda p: block(vx_low_ref, (2 * c + p) * size_y, size_y),
            lambda p: block(vx_high_ref, (2 * c + p) * size_y, size_y),
            block(vy_low_ref, c * LINE + NEAR - 1, size_x + 2),
            block(vy_high_ref, c * LINE + NEAR - 1, size_x + 2),
        )

    def factors(visc, beside, force):
        up = jnp.where(lanes == depth - 1, 0.0, pltpu.roll(visc, depth - 1, 1))
        down = jnp.where(lanes == 0, 0.0, pltpu.roll(visc, 1, 1))
        faces = [visc + other for other in (*beside, up, down)]
        total = ((faces[0] + faces[1]) + (faces[2] + faces[3])) + (faces[4] + faces[5])
        scale = RELAX / total
        faces = [face * scale for face in faces]
        faces[4] = jnp.where(lanes == depth - 1, 0.0, faces[4])
        faces[5] = jnp.where(lanes == 0, 0.0, faces[5])
        return faces, 2.0 * force * scale

    def relax(faces, push, vel, beside):
        up = pltpu.roll(vel, depth - 1, 1)
        down = pltpu.roll(vel, 1, 1)
        terms = [face * other for face, other in zip(faces, (*beside, up, down))]
        result = ((terms[0] + terms[1]) + (terms[2] + terms[3])) + (terms[4] + terms[5])
        result = result + (1.0 - RELAX) * vel
        return result if push is None else result + push

    def around(ref, first):
        return (
            ref[pl.ds(first + pitch, size_y), :],
            ref[pl.ds(first - pitch, size_y), :],
            ref[pl.ds(first + 1, size_y), :],
            ref[pl.ds(first - 1, size_y), :],
        )

    def first_sweep(plane, force):
        at = (plane + 2) * pitch + 8
        faces, push = factors(wide_visc[pl.ds(at, size_y), :], around(wide_visc, at), force)
        results = []
        for c in range(3):
            vel = wide_vel[pl.ds(c * field + at, size_y), :]
            beside = around(wide_vel, c * field + at)
            results.append(relax(faces, push if c == 2 else None, vel, beside))
        return faces, push, results

    def put(plane, results):
        for c in range(3):
            at = c * field_next + (plane + 1) * pitch + 8
            wide_next[pl.ds(at, size_y), :] = results[c]

    for plane, ref in ((-1, x_low_ref), (size_x, x_high_ref)):
        _, _, results = first_sweep(plane, ref[pl.ds(2 * size_y, size_y), :])
        inside = wide_visc[pl.ds((plane + 2) * pitch + 8, size_y), :] > 0.0
        put(plane, [jnp.where(inside, value, 0.0) for value in results])

    for row, near_row, visc_lines, vel_lines in (
        (7, 0, y_low_ref, vy_low_ref),
        (8 + size_y, size_y - 1, y_high_ref, vy_high_ref),
    ):

        def around_line(ref, first, inner):
            return (
                ref[pl.ds(first + NEAR + 1, size_x), :],
                ref[pl.ds(first + NEAR - 1, size_x), :],
                inner,
                ref[pl.ds(first + FAR, size_x), :],
            )

        inner = visc_ref[pl.ds(near_row, size_x, stride=size_y), :]
        visc = visc_lines[pl.ds(NEAR, size_x), :]
        faces, push = factors(
            visc,
            around_line(visc_lines, 0, inner),
            visc_lines[pl.ds(LINE, size_x), :],
        )
        for c in range(3):
            inner = vel_ref[pl.ds(c * cells + near_row, size_x, stride=size_y), :]
            value = relax(
                faces,
                push if c == 2 else None,
                vel_lines[pl.ds(c * LINE + NEAR, size_x), :],
                around_line(vel_lines, c * LINE, inner),
            )
            value = jnp.where(visc > 0.0, value, 0.0)
            at = c * field_next + pitch + row
            wide_next[pl.ds(at, size_x, stride=pitch), :] = value

    for plane in range(size_x):
        faces, push, results = first_sweep(plane, force_ref[pl.ds(plane * size_y, size_y), :])
        put(plane, results)
        for k, value in enumerate((*faces, push)):
            coeff_ref[pl.ds(k * cells + plane * size_y, size_y), :] = value

    for plane in range(size_x):
        faces = [coeff_ref[pl.ds(k * cells + plane * size_y, size_y), :] for k in range(6)]
        push = coeff_ref[pl.ds(6 * cells + plane * size_y, size_y), :]
        for c in range(3):
            at = c * field_next + (plane + 1) * pitch + 8
            vel = wide_next[pl.ds(at, size_y), :]
            value = relax(faces, push if c == 2 else None, vel, around(wide_next, at))
            out_ref[pl.ds(c * cells + plane * size_y, size_y), :] = value


def corner_kernel(bricks, first_in, last_in, x_low_ref, x_high_ref, first_ref, last_ref):
    size_x, size_y = bricks
    for ref, near in ((first_ref, 0), (last_ref, size_y - 1)):
        ref[NEAR - 1 : NEAR, :] = x_low_ref[size_y + near : size_y + near + 1, :]
        ref[NEAR + size_x : NEAR + size_x + 1, :] = x_high_ref[near : near + 1, :]


def limit(mebibytes):
    return pltpu.CompilerParams(vmem_limit_bytes=mebibytes << 20)


def in_hbm(value):
    return pltpu.with_memory_space_constraint(value, pltpu.HBM)


def shifted(value, axis, step):
    count = lax.axis_size(axis)
    pairs = [(i, i + step) for i in range(count) if 0 <= i + step < count]
    return lax.ppermute(value, axis, pairs)


def per_device(
    marker_comp, marker_strain, marker_live, marker_cell, block_dest, old_logvisc, velocity
):
    count_x = lax.axis_size("gx")
    count_y = lax.axis_size("gy")
    devices = count_x * count_y
    blocks, marks = marker_comp.shape
    size_x, size_y, depth = old_logvisc.shape
    columns = size_x * size_y
    slots = 2 * blocks // devices
    chunk = 3 * slots + 1
    total = devices * slots
    lines = (blocks // marks, marks)

    payload = pl.pallas_call(
        functools.partial(pack_kernel, slots, chunk),
        out_shape=jax.ShapeDtypeStruct((devices * chunk, marks), F32),
        in_specs=[HBM] * 5,
        out_specs=VMEM,
        scratch_shapes=[
            pltpu.SMEM(lines, jnp.int32),
            pltpu.VMEM(lines, jnp.int32),
            pltpu.VMEM((48 * BATCH, marks), F32),
            pltpu.SemaphoreType.DMA,
            pltpu.VMEM(lines, jnp.int32),
            pltpu.VMEM((blocks, marks), F32),
            pltpu.VMEM((blocks, marks), F32),
            pltpu.VMEM((blocks, marks), jnp.int32),
            pltpu.VMEM((blocks, marks), jnp.int32),
            pltpu.SemaphoreType.DMA((5,)),
        ],
        compiler_params=limit(12),
        name="pack",
    )(
        in_hbm(block_dest.reshape(lines)),
        in_hbm(marker_comp),
        in_hbm(marker_strain),
        in_hbm(marker_live),
        in_hbm(marker_cell),
    )
    payload = payload.reshape(devices * chunk, 1, marks)
    received = lax.all_to_all(payload, BOTH, split_axis=0, concat_axis=0, tiled=True)
    received = received.reshape(devices * chunk, marks)

    def x_planes(first):
        return velocity[:, first : first + 2].reshape(6 * size_y, depth)

    vx_low = shifted(x_planes(size_x - 2), "gx", 1)
    vx_high = shifted(x_planes(0), "gx", -1)

    def vel_lines(near, far):
        blank = jnp.zeros((3, 7, depth), F32)
        low = vx_low.reshape(3, 2, size_y, depth)[:, 1, near][:, None]
        high = vx_high.reshape(3, 2, size_y, depth)[:, 0, near][:, None]
        parts = [blank, low, velocity[:, :, near], high, blank, velocity[:, :, far]]
        return jnp.concatenate(parts, axis=1).reshape(3 * LINE, depth)

    vy_low = shifted(vel_lines(size_y - 1, size_y - 2), "gy", 1)
    vy_high = shifted(vel_lines(0, 1), "gy", -1)
    received, vx_low, vx_high, vy_low, vy_high = lax.optimization_barrier(
        (received, vx_low, vx_high, vy_low, vy_high)
    )

    field = jax.ShapeDtypeStruct((columns, depth), F32)
    x_side = jax.ShapeDtypeStruct((3 * size_y, depth), F32)
    y_side = jax.ShapeDtypeStruct((LINE + size_x, depth), F32)
    logvisc, density, visc, force, x_first, x_last, y_first, y_last = pl.pallas_call(
        functools.partial(average_kernel, slots, chunk, (size_x, size_y)),
        out_shape=(field, field, field, field, x_side, x_side, y_side, y_side),
        in_specs=[VMEM, VMEM],
        out_specs=(VMEM,) * 8,
        scratch_shapes=[pltpu.VMEM((columns, total), BF16), pltpu.VMEM((total, 5 * depth), BF16)],
        compiler_params=limit(16),
        name="average",
    )(received, old_logvisc.reshape(columns, depth))

    x_low = shifted(x_last, "gx", 1)
    x_high = shifted(x_first, "gx", -1)
    y_first, y_last = pl.pallas_call(
        functools.partial(corner_kernel, (size_x, size_y)),
        out_shape=(y_side, y_side),
        in_specs=[VMEM] * 4,
        out_specs=(VMEM, VMEM),
        input_output_aliases={0: 0, 1: 1},
        compiler_params=limit(4),
        name="corners",
    )(y_first, y_last, x_low, x_high)
    y_low = shifted(y_last, "gy", 1)
    y_high = shifted(y_first, "gy", -1)

    pitch = size_y + 16
    smoothed = pl.pallas_call(
        functools.partial(smooth_kernel, (size_x, size_y)),
        out_shape=jax.ShapeDtypeStruct((3 * columns, depth), F32),
        in_specs=[VMEM] * 11,
        out_specs=VMEM,
        scratch_shapes=[
            pltpu.VMEM(((size_x + 4) * pitch, depth), F32),
            pltpu.VMEM((3 * (size_x + 4) * pitch, depth), F32),
            pltpu.VMEM((3 * (size_x + 2) * pitch, depth), F32),
            pltpu.VMEM((7 * columns, depth), F32),
        ],
        compiler_params=limit(24),
        name="smooth",
    )(
        visc,
        force,
        velocity.reshape(3 * columns, depth),
        vx_low,
        vx_high,
        vy_low,
        vy_high,
        x_low,
        x_high,
        y_low,
        y_high,
    )
    return (
        logvisc.reshape(old_logvisc.shape),
        density.reshape(old_logvisc.shape),
        smoothed.reshape(velocity.shape),
    )


def solution(mesh):
    return jax.shard_map(
        per_device,
        mesh=mesh,
        in_specs=(
            P(("gx", "gy"), None),
            P(("gx", "gy"), None),
            P(("gx", "gy"), None),
            P(("gx", "gy"), None),
            P(("gx", "gy"), None),
            P("gx", "gy", None),
            P(None, "gx", "gy", None),
        ),
        out_specs=(P("gx", "gy", None), P("gx", "gy", None), P(None, "gx", "gy", None)),
        check_vma=False,
    )
```

```python
import functools

import jax
import jax.numpy as jnp
from jax import lax
from jax.experimental import pallas as pl
from jax.experimental.pallas import tpu as pltpu
from jax.sharding import PartitionSpec as P

LOG_HIGH = 1.5
LOG_LOW = -1.0
WEAKENING = 1.0
DENSITY_JUMP = 0.4
SOFTENING = 0.1
GRAVITY = 10.0
RELAX = 0.8
BOTH = ("gx", "gy")
F32 = jnp.float32
BF16 = jnp.bfloat16
VMEM = pl.BlockSpec(memory_space=pltpu.VMEM)
SMEM = pl.BlockSpec(memory_space=pltpu.SMEM)
HBM = pl.BlockSpec(memory_space=pltpu.HBM)
BY_LANES = (((1,), (1,)), ((), ()))
WAYS = 4
BATCH = 32
NEAR = 8
FAR = 32
LINE = 48


def split(values):
    high = values.astype(BF16).astype(F32)
    return high, values - high


def pack_kernel(
    slots,
    chunk,
    dest_hbm,
    comp_hbm,
    strain_hbm,
    live_hbm,
    cell_hbm,
    out_ref,
    place_ref,
    line_ref,
    sums_ref,
    place_sem,
    dest_ref,
    comp_ref,
    strain_ref,
    live_ref,
    cell_ref,
    load_sem,
):
    blocks, marks = comp_ref.shape
    devices = out_ref.shape[0] // chunk
    shift = marks.bit_length() - 1
    part = marks // WAYS
    low_bits = part.bit_length() - 1
    pairs = (
        (dest_hbm, dest_ref),
        (cell_hbm, cell_ref),
        (comp_hbm, comp_ref),
        (strain_hbm, strain_ref),
        (live_hbm, live_ref),
    )
    loads = [pltpu.make_async_copy(*pair, load_sem.at[k]) for k, pair in enumerate(pairs)]
    for load in loads:
        load.start()
    out_ref[...] = jnp.zeros_like(out_ref)
    loads[0].wait()
    loads[1].wait()

    owner_ids = lax.broadcasted_iota(jnp.int32, (devices, marks), 0)
    rank_ids = lax.broadcasted_iota(jnp.int32, (slots, marks), 0)
    square = (marks, marks)
    before = lax.broadcasted_iota(jnp.int32, square, 0) < lax.broadcasted_iota(jnp.int32, square, 1)
    before = jnp.where(before, 1.0, 0.0).astype(BF16)
    seen = jnp.zeros((devices, 1), F32)
    ids = jnp.zeros((devices, slots), F32)
    for k in range(blocks // marks):
        dest = dest_ref[k : k + 1, :]
        mine = owner_ids == dest
        hot = jnp.where(mine, 1.0, 0.0)
        earlier = jnp.dot(hot.astype(BF16), before, preferred_element_type=F32) + seen
        rank = jnp.sum(jnp.where(mine, earlier, 0.0), axis=0, keepdims=True).astype(jnp.int32)
        seen = seen + jnp.sum(hot, axis=1, keepdims=True)
        line_ref[k : k + 1, :] = dest * chunk + rank
        column = (cell_ref[k * marks : (k + 1) * marks, :] >> shift).astype(F32).T[0:1] + 1.0
        spot = jnp.where(rank_ids == rank, 1.0, 0.0).astype(BF16)
        for piece in split(column):
            weighted = jnp.where(mine, piece, 0.0).astype(BF16)
            ids = ids + lax.dot_general(weighted, spot, BY_LANES, preferred_element_type=F32)
    places = pltpu.make_async_copy(line_ref, place_ref, place_sem)
    places.start()
    ids = ids - 1.0
    for owner in range(devices):
        at = owner * chunk + 3 * slots
        out_ref[at : at + 1, 0:slots] = ids[owner : owner + 1, :]
    for load in loads[2:]:
        load.wait()

    fine_ids = lax.broadcasted_iota(jnp.int32, (part, marks), 0).astype(F32).astype(BF16)
    row_ids = lax.broadcasted_iota(jnp.int32, (8, marks), 0)
    lane_ids = lax.broadcasted_iota(jnp.int32, (8, marks), 1)
    halves = [row_ids < 4, row_ids >= 4]
    spans = [(lane_ids >> low_bits) == ((row_ids + w) & (WAYS - 1)) for w in range(WAYS)]

    def depth_sums(group):
        rows = pl.ds(pl.multiple_of(group * 8, 8), 8)
        comp = comp_ref[rows, :]
        strain = strain_ref[rows, :]
        weight = live_ref[rows, :].astype(F32)
        soften = strain / (1.0 + strain)
        logv = weight * (LOG_HIGH * comp + LOG_LOW * (1.0 - comp) - WEAKENING * soften)
        rho = weight * (1.0 + DENSITY_JUMP * comp - SOFTENING * soften)
        pieces = [*split(logv), *split(rho), weight]
        depth = cell_ref[rows, :] & (marks - 1)
        coarse = ((depth >> low_bits) - row_ids) & (WAYS - 1)
        fine = (depth & (part - 1)).astype(F32)
        left, right = [], []
        for half in halves:
            lines = []
            for w in range(WAYS):
                mask = (coarse == w) & half
                lines += [jnp.where(mask, piece, 0.0) for piece in pieces]
            left.append(jnp.concatenate(lines, axis=0).astype(BF16))
        for first in (0, 4):
            lines = []
            for b in range(first, first + 4):
                line = jnp.broadcast_to(fine[b : b + 1, :], (16, marks)).astype(BF16)
                line = jnp.concatenate([line] * (part // 16), axis=0)
                lines.append(jnp.where(fine_ids == line, BF16(1.0), BF16(0.0)))
            right.append(jnp.concatenate(lines, axis=0))
        sums = lax.dot_general(
            jnp.concatenate(left, axis=1),
            jnp.concatenate(right, axis=1),
            BY_LANES,
            preferred_element_type=F32,
        )

        def piece_sum(w, p):
            first = (w * len(pieces) + p) * 8
            return sums[first : first + 8]

        results = []
        for numbers in ((0, 1), (2, 3), (4,)):
            total = None
            for w in range(WAYS):
                value = piece_sum(w, numbers[0])
                if len(numbers) > 1:
                    value = value + piece_sum(w, numbers[1])
                if w:
                    value = pltpu.roll(value, part * w, 1)
                total = value if total is None else jnp.where(spans[w], value, total)
            results.append(total)
        return results

    def batch(step, g, f):
        first = (step & 1) * (24 * BATCH) + g * 24 + f * 8
        return pl.ds(pl.multiple_of(first, 8), 8)

    def put(step):
        for g in range(BATCH):
            for f, value in enumerate(depth_sums(step * BATCH + g)):
                sums_ref[batch(step, g, f), :] = value

    def place(step):
        for g in range(BATCH):
            group = step * BATCH + g
            values = [sums_ref[batch(step, g, f), :] for f in range(3)]
            for k in range(8):
                at = place_ref[group // 16, (group % 16) * 8 + k]
                for f in range(3):
                    out_ref[pl.ds(at + f * slots, 1), :] = values[f][k : k + 1]

    steps = blocks // 8 // BATCH
    put(0)
    places.wait()

    def step(i, carry):
        place(i - 1)
        put(i)
        return carry

    lax.fori_loop(1, steps, step, 0)
    place(steps - 1)


def parities():
    return lax.axis_index("gx") & 1, lax.axis_index("gy") & 1


def average_kernel(
    slots,
    chunk,
    bricks,
    recv_ref,
    old_ref,
    logvisc_ref,
    density_ref,
    visc_ref,
    force_ref,
    x_even_ref,
    x_odd_ref,
    y_even_ref,
    y_odd_ref,
    hot_ref,
    value_ref,
):
    size_x, size_y = bricks
    columns, depth = old_ref.shape
    total = hot_ref.shape[1]
    per = depth // slots
    lanes = lax.broadcasted_iota(jnp.int32, (1, depth), 1)
    column_ids = lax.broadcasted_iota(jnp.int32, (columns, depth), 0).astype(F32)
    for part in range(total // depth):
        span = slice(part * depth, (part + 1) * depth)
        ids = jnp.full((1, depth), -1.0, F32)
        for k in range(per):
            first = (part * per + k) * chunk
            line = recv_ref[first + 3 * slots : first + 3 * slots + 1, :]
            if k:
                line = pltpu.roll(line, k * slots, 1)
            ids = jnp.where((lanes >= k * slots) & (lanes < (k + 1) * slots), line, ids)
        hot_ref[:, span] = jnp.where(column_ids == ids, 1.0, 0.0).astype(BF16)
        for v in range(3):
            block = jnp.concatenate(
                [
                    recv_ref[pl.ds((part * per + k) * chunk + v * slots, slots), :]
                    for k in range(per)
                ],
                axis=0,
            )
            high, low = split(block)
            value_ref[span, pl.ds(2 * v * depth, depth)] = high.astype(BF16)
            if v < 2:
                value_ref[span, pl.ds((2 * v + 1) * depth, depth)] = low.astype(BF16)
    for tile in range(columns // depth):
        span = slice(tile * depth, (tile + 1) * depth)
        sums = jnp.dot(hot_ref[span, :], value_ref[...], preferred_element_type=F32)
        sum_logv = sums[:, 0:depth] + sums[:, depth : 2 * depth]
        sum_rho = sums[:, 2 * depth : 3 * depth] + sums[:, 3 * depth : 4 * depth]
        count = sums[:, 4 * depth : 5 * depth] + 1.0
        logvisc = (sum_logv + old_ref[span, :]) / count
        density = (sum_rho + 1.0) / count
        logvisc_ref[span, :] = logvisc
        density_ref[span, :] = density
        visc_ref[span, :] = jnp.exp(logvisc)
        force_ref[span, :] = GRAVITY * (1.0 - density)
    odd_x, odd_y = parities()
    for ref, first in ((x_even_ref, odd_x == 1), (x_odd_ref, odd_x == 0)):
        start = jnp.where(first, 0, columns - 2 * size_y)
        ref[0 : 2 * size_y, :] = visc_ref[pl.ds(pl.multiple_of(start, 8), 2 * size_y), :]
        start = jnp.where(first, 0, columns - size_y)
        ref[2 * size_y :, :] = force_ref[pl.ds(pl.multiple_of(start, 8), size_y), :]
    for ref, first in ((y_even_ref, odd_y == 1), (y_odd_ref, odd_y == 0)):
        near = jnp.where(first, 0, size_y - 1)
        far = jnp.where(first, 1, size_y - 2)
        ref[...] = jnp.zeros_like(ref)
        ref[NEAR : NEAR + size_x, :] = visc_ref[pl.ds(near, size_x, stride=size_y), :]
        ref[FAR : FAR + size_x, :] = visc_ref[pl.ds(far, size_x, stride=size_y), :]
        ref[LINE : LINE + size_x, :] = force_ref[pl.ds(near, size_x, stride=size_y), :]


def smooth_kernel(
    bricks,
    visc_ref,
    force_ref,
    vel_ref,
    vx_low_ref,
    vx_high_ref,
    vy_low_ref,
    vy_high_ref,
    x_even_ref,
    x_odd_ref,
    y_even_ref,
    y_odd_ref,
    out_ref,
    wide_visc,
    wide_vel,
    wide_next,
    coeff_ref,
):
    size_x, size_y = bricks
    cells, depth = visc_ref.shape
    pitch = size_y + 16
    lanes = lax.broadcasted_iota(jnp.int32, (1, depth), 1)

    field = (size_x + 4) * pitch
    field_next = (size_x + 2) * pitch
    odd_x, odd_y = parities()

    def x_side(is_low):
        return jnp.where(is_low, -1, size_x)

    def y_row(is_low):
        return jnp.where(is_low, 7, 8 + size_y)

    def place(ref, offset, source, first):
        for plane in range(size_x):
            at = offset + (plane + 2) * pitch + 8
            ref[pl.ds(at, size_y), :] = source[pl.ds(first + plane * size_y, size_y), :]

    def place_x(ref, offset, source, first, is_low):
        base = offset + jnp.where(is_low, 0, (size_x + 2) * pitch) + 8
        for plane in range(2):
            at = pl.multiple_of(base + plane * pitch, 8)
            ref[pl.ds(at, size_y), :] = source[pl.ds(first + plane * size_y, size_y), :]

    def place_y(ref, offset, source, first, row):
        span = pl.ds(offset + pitch + row, size_x + 2, stride=pitch)
        ref[span, :] = source[pl.ds(first + NEAR - 1, size_x + 2), :]

    place(wide_visc, 0, visc_ref, 0)
    place_x(wide_visc, 0, x_even_ref, 0, odd_x == 1)
    place_x(wide_visc, 0, x_odd_ref, 0, odd_x == 0)
    place_y(wide_visc, 0, y_even_ref, 0, y_row(odd_y == 1))
    place_y(wide_visc, 0, y_odd_ref, 0, y_row(odd_y == 0))
    for c in range(3):
        place(wide_vel, c * field, vel_ref, c * cells)
        place_x(wide_vel, c * field, vx_low_ref, 2 * c * size_y, True)
        place_x(wide_vel, c * field, vx_high_ref, 2 * c * size_y, False)
        place_y(wide_vel, c * field, vy_low_ref, c * LINE, 7)
        place_y(wide_vel, c * field, vy_high_ref, c * LINE, 8 + size_y)

    def factors(visc, beside, force):
        up = jnp.where(lanes == depth - 1, 0.0, pltpu.roll(visc, depth - 1, 1))
        down = jnp.where(lanes == 0, 0.0, pltpu.roll(visc, 1, 1))
        faces = [visc + other for other in (*beside, up, down)]
        total = ((faces[0] + faces[1]) + (faces[2] + faces[3])) + (faces[4] + faces[5])
        scale = RELAX / total
        faces = [face * scale for face in faces]
        faces[4] = jnp.where(lanes == depth - 1, 0.0, faces[4])
        faces[5] = jnp.where(lanes == 0, 0.0, faces[5])
        return faces, 2.0 * force * scale

    def relax(faces, push, vel, beside):
        up = pltpu.roll(vel, depth - 1, 1)
        down = pltpu.roll(vel, 1, 1)
        terms = [face * other for face, other in zip(faces, (*beside, up, down))]
        result = ((terms[0] + terms[1]) + (terms[2] + terms[3])) + (terms[4] + terms[5])
        result = result + (1.0 - RELAX) * vel
        return result if push is None else result + push

    def around(ref, first):
        return (
            ref[pl.ds(first + pitch, size_y), :],
            ref[pl.ds(first - pitch, size_y), :],
            ref[pl.ds(first + 1, size_y), :],
            ref[pl.ds(first - 1, size_y), :],
        )

    def first_sweep(plane, force):
        at = pl.multiple_of((plane + 2) * pitch + 8, 8)
        faces, push = factors(wide_visc[pl.ds(at, size_y), :], around(wide_visc, at), force)
        results = []
        for c in range(3):
            vel = wide_vel[pl.ds(c * field + at, size_y), :]
            beside = around(wide_vel, c * field + at)
            results.append(relax(faces, push if c == 2 else None, vel, beside))
        return faces, push, results

    def put(plane, results):
        for c in range(3):
            at = pl.multiple_of(c * field_next + (plane + 1) * pitch + 8, 8)
            wide_next[pl.ds(at, size_y), :] = results[c]

    for plane, ref in ((x_side(odd_x == 1), x_even_ref), (x_side(odd_x == 0), x_odd_ref)):
        _, _, results = first_sweep(plane, ref[pl.ds(2 * size_y, size_y), :])
        inside = ref[pl.ds(jnp.where(plane < 0, size_y, 0), size_y), :] > 0.0
        put(plane, [jnp.where(inside, value, 0.0) for value in results])

    def y_lines(is_low, ref):
        near = jnp.where(is_low, 0, size_y - 1)
        return y_row(is_low), near, is_low, ref

    for row, near_row, is_low, visc_lines in (
        y_lines(odd_y == 1, y_even_ref),
        y_lines(odd_y == 0, y_odd_ref),
    ):

        def vel_line(first, count):
            span = pl.ds(first, count)
            return jnp.where(is_low, vy_low_ref[span, :], vy_high_ref[span, :])

        def visc_line(first, count):
            return visc_lines[pl.ds(first, count), :]

        def around_line(line, first, inner):
            return (
                line(first + NEAR + 1, size_x),
                line(first + NEAR - 1, size_x),
                inner,
                line(first + FAR, size_x),
            )

        inner = visc_ref[pl.ds(near_row, size_x, stride=size_y), :]
        visc = visc_line(NEAR, size_x)
        faces, push = factors(
            visc,
            around_line(visc_line, 0, inner),
            visc_line(LINE, size_x),
        )
        for c in range(3):
            inner = vel_ref[pl.ds(c * cells + near_row, size_x, stride=size_y), :]
            value = relax(
                faces,
                push if c == 2 else None,
                vel_line(c * LINE + NEAR, size_x),
                around_line(vel_line, c * LINE, inner),
            )
            value = jnp.where(visc > 0.0, value, 0.0)
            at = c * field_next + pitch + row
            wide_next[pl.ds(at, size_x, stride=pitch), :] = value

    for plane in range(size_x):
        faces, push, results = first_sweep(plane, force_ref[pl.ds(plane * size_y, size_y), :])
        put(plane, results)
        for k, value in enumerate((*faces, push)):
            coeff_ref[pl.ds(k * cells + plane * size_y, size_y), :] = value

    for plane in range(size_x):
        faces = [coeff_ref[pl.ds(k * cells + plane * size_y, size_y), :] for k in range(6)]
        push = coeff_ref[pl.ds(6 * cells + plane * size_y, size_y), :]
        for c in range(3):
            at = c * field_next + (plane + 1) * pitch + 8
            vel = wide_next[pl.ds(at, size_y), :]
            value = relax(faces, push if c == 2 else None, vel, around(wide_next, at))
            out_ref[pl.ds(c * cells + plane * size_y, size_y), :] = value


def corner_kernel(
    bricks, even_in, odd_in, x_even_ref, x_odd_ref, y_even_ref, y_odd_ref
):
    size_x, size_y = bricks
    odd_x, odd_y = parities()
    swapped = odd_x == 1
    for ref, first in ((y_even_ref, odd_y == 1), (y_odd_ref, odd_y == 0)):
        near = jnp.where(first, 0, size_y - 1)
        low, high = pl.ds(size_y + near, 1), pl.ds(near, 1)
        ref[NEAR - 1 : NEAR, :] = jnp.where(swapped, x_even_ref[low, :], x_odd_ref[low, :])
        high = jnp.where(swapped, x_odd_ref[high, :], x_even_ref[high, :])
        ref[NEAR + size_x : NEAR + size_x + 1, :] = high


def limit(mebibytes):
    return pltpu.CompilerParams(vmem_limit_bytes=mebibytes << 20)


def in_hbm(value):
    return pltpu.with_memory_space_constraint(value, pltpu.HBM)


def shifted(value, axis, step):
    count = lax.axis_size(axis)
    pairs = [(i, i + step) for i in range(count) if 0 <= i + step < count]
    return lax.ppermute(value, axis, pairs)


def swapped(value, axis, first):
    count = lax.axis_size(axis)
    pairs = [(i, i + 1) for i in range(first, count - 1, 2)]
    return lax.ppermute(value, axis, pairs + [(b, a) for a, b in pairs])


def per_device(
    marker_comp, marker_strain, marker_live, marker_cell, block_dest, old_logvisc, velocity
):
    count_x = lax.axis_size("gx")
    count_y = lax.axis_size("gy")
    devices = count_x * count_y
    blocks, marks = marker_comp.shape
    size_x, size_y, depth = old_logvisc.shape
    columns = size_x * size_y
    slots = 2 * blocks // devices
    chunk = 3 * slots + 1
    total = devices * slots
    lines = (blocks // marks, marks)

    payload = pl.pallas_call(
        functools.partial(pack_kernel, slots, chunk),
        out_shape=jax.ShapeDtypeStruct((devices * chunk, marks), F32),
        in_specs=[HBM] * 5,
        out_specs=VMEM,
        scratch_shapes=[
            pltpu.SMEM(lines, jnp.int32),
            pltpu.VMEM(lines, jnp.int32),
            pltpu.VMEM((48 * BATCH, marks), F32),
            pltpu.SemaphoreType.DMA,
            pltpu.VMEM(lines, jnp.int32),
            pltpu.VMEM((blocks, marks), F32),
            pltpu.VMEM((blocks, marks), F32),
            pltpu.VMEM((blocks, marks), jnp.int32),
            pltpu.VMEM((blocks, marks), jnp.int32),
            pltpu.SemaphoreType.DMA((5,)),
        ],
        compiler_params=limit(12),
        name="pack",
    )(
        in_hbm(block_dest.reshape(lines)),
        in_hbm(marker_comp),
        in_hbm(marker_strain),
        in_hbm(marker_live),
        in_hbm(marker_cell),
    )
    payload = payload.reshape(devices * chunk, 1, marks)
    received = lax.all_to_all(payload, BOTH, split_axis=0, concat_axis=0, tiled=True)
    received = received.reshape(devices * chunk, marks)

    def x_planes(first):
        return velocity[:, first : first + 2].reshape(6 * size_y, depth)

    vx_low = shifted(x_planes(size_x - 2), "gx", 1)
    vx_high = shifted(x_planes(0), "gx", -1)

    def vel_lines(near, far):
        blank = jnp.zeros((3, 7, depth), F32)
        low = vx_low.reshape(3, 2, size_y, depth)[:, 1, near][:, None]
        high = vx_high.reshape(3, 2, size_y, depth)[:, 0, near][:, None]
        parts = [blank, low, velocity[:, :, near], high, blank, velocity[:, :, far]]
        return jnp.concatenate(parts, axis=1).reshape(3 * LINE, depth)

    vy_low = shifted(vel_lines(size_y - 1, size_y - 2), "gy", 1)
    vy_high = shifted(vel_lines(0, 1), "gy", -1)
    received, vx_low, vx_high, vy_low, vy_high = lax.optimization_barrier(
        (received, vx_low, vx_high, vy_low, vy_high)
    )

    field = jax.ShapeDtypeStruct((columns, depth), F32)
    x_side = jax.ShapeDtypeStruct((3 * size_y, depth), F32)
    y_side = jax.ShapeDtypeStruct((LINE + size_x, depth), F32)
    logvisc, density, visc, force, x_even, x_odd, y_even, y_odd = pl.pallas_call(
        functools.partial(average_kernel, slots, chunk, (size_x, size_y)),
        out_shape=(field, field, field, field, x_side, x_side, y_side, y_side),
        in_specs=[VMEM, VMEM],
        out_specs=(VMEM,) * 8,
        scratch_shapes=[pltpu.VMEM((columns, total), BF16), pltpu.VMEM((total, 5 * depth), BF16)],
        compiler_params=limit(16),
        name="average",
    )(received, old_logvisc.reshape(columns, depth))

    x_even = swapped(x_even, "gx", 0)
    x_odd = swapped(x_odd, "gx", 1)
    y_even, y_odd = pl.pallas_call(
        functools.partial(corner_kernel, (size_x, size_y)),
        out_shape=(y_side, y_side),
        in_specs=[VMEM] * 4,
        out_specs=(VMEM, VMEM),
        input_output_aliases={0: 0, 1: 1},
        compiler_params=limit(4),
        name="corners",
    )(y_even, y_odd, x_even, x_odd)
    y_even = swapped(y_even, "gy", 0)
    y_odd = swapped(y_odd, "gy", 1)

    pitch = size_y + 16
    smoothed = pl.pallas_call(
        functools.partial(smooth_kernel, (size_x, size_y)),
        out_shape=jax.ShapeDtypeStruct((3 * columns, depth), F32),
        in_specs=[VMEM] * 11,
        out_specs=VMEM,
        scratch_shapes=[
            pltpu.VMEM(((size_x + 4) * pitch, depth), F32),
            pltpu.VMEM((3 * (size_x + 4) * pitch, depth), F32),
            pltpu.VMEM((3 * (size_x + 2) * pitch, depth), F32),
            pltpu.VMEM((7 * columns, depth), F32),
        ],
        compiler_params=limit(24),
        name="smooth",
    )(
        visc,
        force,
        velocity.reshape(3 * columns, depth),
        vx_low,
        vx_high,
        vy_low,
        vy_high,
        x_even,
        x_odd,
        y_even,
        y_odd,
    )
    return (
        logvisc.reshape(old_logvisc.shape),
        density.reshape(old_logvisc.shape),
        smoothed.reshape(velocity.shape),
    )


def solution(mesh):
    return jax.shard_map(
        per_device,
        mesh=mesh,
        in_specs=(
            P(("gx", "gy"), None),
            P(("gx", "gy"), None),
            P(("gx", "gy"), None),
            P(("gx", "gy"), None),
            P(("gx", "gy"), None),
            P("gx", "gy", None),
            P(None, "gx", "gy", None),
        ),
        out_specs=(P("gx", "gy", None), P("gx", "gy", None), P(None, "gx", "gy", None)),
        check_vma=False,
    )
```

```python
import functools

import jax
import jax.numpy as jnp
from jax import lax
from jax.experimental import pallas as pl
from jax.experimental.pallas import tpu as pltpu
from jax.sharding import PartitionSpec as P

LOG_HIGH = 1.5
LOG_LOW = -1.0
WEAKENING = 1.0
DENSITY_JUMP = 0.4
SOFTENING = 0.1
GRAVITY = 10.0
RELAX = 0.8
BOTH = ("gx", "gy")
F32 = jnp.float32
BF16 = jnp.bfloat16
VMEM = pl.BlockSpec(memory_space=pltpu.VMEM)
SMEM = pl.BlockSpec(memory_space=pltpu.SMEM)
HBM = pl.BlockSpec(memory_space=pltpu.HBM)
BY_LANES = (((1,), (1,)), ((), ()))
WAYS = 4
BATCH = 32
CORNERS = 8


def split(values):
    high = values.astype(BF16).astype(F32)
    return high, values - high


def pack_kernel(
    slots,
    chunk,
    dest_hbm,
    comp_hbm,
    strain_hbm,
    live_hbm,
    cell_hbm,
    out_ref,
    place_ref,
    line_ref,
    sums_ref,
    place_sem,
    dest_ref,
    comp_ref,
    strain_ref,
    live_ref,
    cell_ref,
    load_sem,
):
    blocks, marks = comp_ref.shape
    devices = out_ref.shape[0] // chunk
    shift = marks.bit_length() - 1
    part = marks // WAYS
    low_bits = part.bit_length() - 1
    pairs = (
        (dest_hbm, dest_ref),
        (cell_hbm, cell_ref),
        (comp_hbm, comp_ref),
        (strain_hbm, strain_ref),
        (live_hbm, live_ref),
    )
    loads = [pltpu.make_async_copy(*pair, load_sem.at[k]) for k, pair in enumerate(pairs)]
    for load in loads:
        load.start()
    out_ref[...] = jnp.zeros_like(out_ref)
    loads[0].wait()
    loads[1].wait()

    owner_ids = lax.broadcasted_iota(jnp.int32, (devices, marks), 0)
    rank_ids = lax.broadcasted_iota(jnp.int32, (slots, marks), 0)
    square = (marks, marks)
    before = lax.broadcasted_iota(jnp.int32, square, 0) < lax.broadcasted_iota(jnp.int32, square, 1)
    before = jnp.where(before, 1.0, 0.0).astype(BF16)
    seen = jnp.zeros((devices, 1), F32)
    ids = jnp.zeros((devices, slots), F32)
    for k in range(blocks // marks):
        dest = dest_ref[k : k + 1, :]
        mine = owner_ids == dest
        hot = jnp.where(mine, 1.0, 0.0)
        earlier = jnp.dot(hot.astype(BF16), before, preferred_element_type=F32) + seen
        rank = jnp.sum(jnp.where(mine, earlier, 0.0), axis=0, keepdims=True).astype(jnp.int32)
        seen = seen + jnp.sum(hot, axis=1, keepdims=True)
        line_ref[k : k + 1, :] = dest * chunk + rank
        column = (cell_ref[k * marks : (k + 1) * marks, :] >> shift).astype(F32).T[0:1] + 1.0
        spot = jnp.where(rank_ids == rank, 1.0, 0.0).astype(BF16)
        for piece in split(column):
            weighted = jnp.where(mine, piece, 0.0).astype(BF16)
            ids = ids + lax.dot_general(weighted, spot, BY_LANES, preferred_element_type=F32)
    places = pltpu.make_async_copy(line_ref, place_ref, place_sem)
    places.start()
    ids = ids - 1.0
    for owner in range(devices):
        at = owner * chunk + 3 * slots
        out_ref[at : at + 1, 0:slots] = ids[owner : owner + 1, :]
    for load in loads[2:]:
        load.wait()

    fine_ids = lax.broadcasted_iota(jnp.int32, (part, marks), 0).astype(F32).astype(BF16)
    row_ids = lax.broadcasted_iota(jnp.int32, (8, marks), 0)
    lane_ids = lax.broadcasted_iota(jnp.int32, (8, marks), 1)
    halves = [row_ids < 4, row_ids >= 4]
    spans = [(lane_ids >> low_bits) == ((row_ids + w) & (WAYS - 1)) for w in range(WAYS)]

    def depth_sums(group):
        rows = pl.ds(pl.multiple_of(group * 8, 8), 8)
        comp = comp_ref[rows, :]
        strain = strain_ref[rows, :]
        weight = live_ref[rows, :].astype(F32)
        soften = strain / (1.0 + strain)
        logv = weight * (LOG_HIGH * comp + LOG_LOW * (1.0 - comp) - WEAKENING * soften)
        rho = weight * (1.0 + DENSITY_JUMP * comp - SOFTENING * soften)
        pieces = [*split(logv), *split(rho), weight]
        depth = cell_ref[rows, :] & (marks - 1)
        coarse = ((depth >> low_bits) - row_ids) & (WAYS - 1)
        fine = (depth & (part - 1)).astype(F32)
        left, right = [], []
        for half in halves:
            lines = []
            for w in range(WAYS):
                mask = (coarse == w) & half
                lines += [jnp.where(mask, piece, 0.0) for piece in pieces]
            left.append(jnp.concatenate(lines, axis=0).astype(BF16))
        for first in (0, 4):
            lines = []
            for b in range(first, first + 4):
                line = jnp.broadcast_to(fine[b : b + 1, :], (16, marks)).astype(BF16)
                line = jnp.concatenate([line] * (part // 16), axis=0)
                lines.append(jnp.where(fine_ids == line, BF16(1.0), BF16(0.0)))
            right.append(jnp.concatenate(lines, axis=0))
        sums = lax.dot_general(
            jnp.concatenate(left, axis=1),
            jnp.concatenate(right, axis=1),
            BY_LANES,
            preferred_element_type=F32,
        )

        def piece_sum(w, p):
            first = (w * len(pieces) + p) * 8
            return sums[first : first + 8]

        results = []
        for numbers in ((0, 1), (2, 3), (4,)):
            total = None
            for w in range(WAYS):
                value = piece_sum(w, numbers[0])
                if len(numbers) > 1:
                    value = value + piece_sum(w, numbers[1])
                if w:
                    value = pltpu.roll(value, part * w, 1)
                total = value if total is None else jnp.where(spans[w], value, total)
            results.append(total)
        return results

    def batch(step, g, f):
        first = (step & 1) * (24 * BATCH) + g * 24 + f * 8
        return pl.ds(pl.multiple_of(first, 8), 8)

    def put(step):
        for g in range(BATCH):
            for f, value in enumerate(depth_sums(step * BATCH + g)):
                sums_ref[batch(step, g, f), :] = value

    def place(step):
        for g in range(BATCH):
            group = step * BATCH + g
            values = [sums_ref[batch(step, g, f), :] for f in range(3)]
            for k in range(8):
                at = place_ref[group // 16, (group % 16) * 8 + k]
                for f in range(3):
                    out_ref[pl.ds(at + f * slots, 1), :] = values[f][k : k + 1]

    steps = blocks // 8 // BATCH
    put(0)
    places.wait()

    def step(i, carry):
        place(i - 1)
        put(i)
        return carry

    lax.fori_loop(1, steps, step, 0)
    place(steps - 1)


def parities():
    return lax.axis_index("gx") & 1, lax.axis_index("gy") & 1


def at_end(axis):
    place, last = lax.axis_index(axis), lax.axis_size(axis) - 1
    return (place == 0) | (place == last) if last % 2 else place == 0


def boundary_columns(size_x, size_y):
    return (
        (0, 2 * size_y, 1),
        ((size_x - 2) * size_y, 2 * size_y, 1),
        (0, size_x, size_y),
        (1, size_x, size_y),
        (size_y - 1, size_x, size_y),
        (size_y - 2, size_x, size_y),
    )


def averages(sums, depth, old):
    sum_logv = sums[:, 0:depth] + sums[:, depth : 2 * depth]
    sum_rho = sums[:, 2 * depth : 3 * depth] + sums[:, 3 * depth : 4 * depth]
    count = sums[:, 4 * depth : 5 * depth] + 1.0
    return (sum_logv + old) / count, (sum_rho + 1.0) / count


def edge_kernel(
    slots,
    chunk,
    bricks,
    recv_ref,
    old_ref,
    vy_low_ref,
    vy_high_ref,
    wide_in,
    x_even_ref,
    x_odd_ref,
    y_even_ref,
    y_odd_ref,
    value_ref,
    ids_ref,
    wide_ref,
    hot_ref,
    visc_ref,
    force_ref,
):
    size_x, size_y = bricks
    depth = old_ref.shape[1]
    total = value_ref.shape[0]
    per = depth // slots
    lanes = lax.broadcasted_iota(jnp.int32, (1, depth), 1)
    runs = boundary_columns(size_x, size_y)
    wide = Wide(bricks)
    for c in range(3):
        for ref, near, far in ((vy_low_ref, -1, -2), (vy_high_ref, size_y, size_y + 1)):
            for k, row in enumerate((near, far)):
                wide_ref[wide.line(c, row), :] = ref[pl.ds((2 * c + k) * size_x, size_x), :]
    names = []
    for first, count, stride in runs:
        names.append(lax.broadcasted_iota(jnp.int32, (count, depth), 0) * stride + first)
    names = jnp.concatenate(names, axis=0).astype(F32)
    for part in range(total // depth):
        span = slice(part * depth, (part + 1) * depth)
        ids = jnp.full((1, depth), -1.0, F32)
        for k in range(per):
            first = (part * per + k) * chunk
            line = recv_ref[first + 3 * slots : first + 3 * slots + 1, :]
            if k:
                line = pltpu.roll(line, k * slots, 1)
            ids = jnp.where((lanes >= k * slots) & (lanes < (k + 1) * slots), line, ids)
        ids_ref[part : part + 1, :] = ids
        hot_ref[:, span] = jnp.where(names == ids, 1.0, 0.0).astype(BF16)
        for v in range(3):
            lines = []
            for k in range(per):
                lines.append(recv_ref[pl.ds((part * per + k) * chunk + v * slots, slots), :])
            high, low = split(jnp.concatenate(lines, axis=0))
            value_ref[span, pl.ds(2 * v * depth, depth)] = high.astype(BF16)
            if v < 2:
                value_ref[span, pl.ds((2 * v + 1) * depth, depth)] = low.astype(BF16)
    sums = jnp.dot(hot_ref[...], value_ref[...], preferred_element_type=F32)
    old = []
    for first, count, stride in runs:
        old.append(old_ref[pl.ds(first, count, stride=stride) if stride > 1 else pl.ds(first, count), :])
    logvisc, density = averages(sums, depth, jnp.concatenate(old, axis=0))
    visc_ref[...] = jnp.exp(logvisc)
    force_ref[...] = GRAVITY * (1.0 - density)
    odd_x, odd_y = parities()
    for ref, is_first in ((y_even_ref, odd_y == 1), (y_odd_ref, odd_y == 0)):
        start = pl.multiple_of(jnp.where(is_first, 4 * size_y, 4 * size_y + 2 * size_x), 8)
        ref[0 : 2 * size_x, :] = visc_ref[pl.ds(start, 2 * size_x), :]
        ref[2 * size_x :, :] = force_ref[pl.ds(start, size_x), :]
    for ref, is_first in ((x_even_ref, odd_x == 1), (x_odd_ref, odd_x == 0)):
        start = pl.multiple_of(jnp.where(is_first, 0, 2 * size_y), 8)
        ref[0 : 2 * size_y, :] = visc_ref[pl.ds(start, 2 * size_y), :]
        start = pl.multiple_of(jnp.where(is_first, 0, 3 * size_y), 8)
        ref[2 * size_y : 3 * size_y, :] = force_ref[pl.ds(start, size_y), :]
        ref[3 * size_y :, :] = jnp.zeros((CORNERS, depth), F32)

    @pl.when(at_end("gx"))
    def _():
        x_odd_ref[...] = jnp.zeros_like(x_odd_ref)

    @pl.when(at_end("gy"))
    def _():
        y_odd_ref[...] = jnp.zeros_like(y_odd_ref)


def factors(visc, beside, force):
    depth = visc.shape[1]
    lanes = lax.broadcasted_iota(jnp.int32, (1, depth), 1)
    up = jnp.where(lanes == depth - 1, 0.0, pltpu.roll(visc, depth - 1, 1))
    down = jnp.where(lanes == 0, 0.0, pltpu.roll(visc, 1, 1))
    faces = [visc + other for other in (*beside, up, down)]
    total = ((faces[0] + faces[1]) + (faces[2] + faces[3])) + (faces[4] + faces[5])
    scale = RELAX / total
    faces = [face * scale for face in faces]
    faces[4] = jnp.where(lanes == depth - 1, 0.0, faces[4])
    faces[5] = jnp.where(lanes == 0, 0.0, faces[5])
    return faces, 2.0 * force * scale


def relax(faces, push, vel, beside):
    depth = vel.shape[1]
    up = pltpu.roll(vel, depth - 1, 1)
    down = pltpu.roll(vel, 1, 1)
    terms = [face * other for face, other in zip(faces, (*beside, up, down))]
    result = ((terms[0] + terms[1]) + (terms[2] + terms[3])) + (terms[4] + terms[5])
    result = result + (1.0 - RELAX) * vel
    return result if push is None else result + push


class Wide:
    def __init__(self, bricks):
        self.size_x, self.size_y = bricks
        self.pitch = self.size_y + 16
        self.cells = self.size_x * self.size_y
        self.field = (self.size_x + 4) * self.pitch

    def plane(self, field, plane, dx=0, dy=0, row=0, rows=None):
        at = field * self.field + (plane + 2 + dx) * self.pitch + 8 + row
        if dy == 0 and row == 0 and not isinstance(at, int):
            at = pl.multiple_of(at, 8)
        return pl.ds(at + dy, rows or self.size_y)

    def cell(self, field, plane, row):
        return pl.ds(field * self.field + (plane + 2) * self.pitch + 8 + row, 1)

    def line(self, field, row, dx=0):
        at = field * self.field + (2 + dx) * self.pitch + 8 + row
        return pl.ds(at, self.size_x, stride=self.pitch)

    def around(self, ref, field, plane, **tile):
        steps = ((1, 0), (-1, 0), (0, 1), (0, -1))
        return tuple(ref[self.plane(field, plane, dx=dx, dy=dy, **tile), :] for dx, dy in steps)

    def core(self, plane, field=0, row=0, rows=None):
        return pl.ds(field * self.cells + plane * self.size_y + row, rows or self.size_y)

    def first_sweep(self, visc_ref, vel_ref, plane, force, **tile):
        visc = visc_ref[self.plane(0, plane, **tile), :]
        faces, push = factors(visc, self.around(visc_ref, 0, plane, **tile), force)
        results = []
        for c in range(3):
            vel = vel_ref[self.plane(c, plane, **tile), :]
            beside = self.around(vel_ref, c, plane, **tile)
            results.append(relax(faces, push if c == 2 else None, vel, beside))
        return faces, push, results

    def around_line(self, ref, field, row):
        places = (
            self.line(field, row, dx=1),
            self.line(field, row, dx=-1),
            self.line(field, row + 1),
            self.line(field, row - 1),
        )
        return tuple(ref[place, :] for place in places)

    def first_ring(self, visc_ref, vel_ref, next_ref, plane, force, **tile):
        _, _, results = self.first_sweep(visc_ref, vel_ref, plane, force, **tile)
        inside = visc_ref[self.plane(0, plane, **tile), :] > 0.0
        for c in range(3):
            next_ref[self.plane(c, plane, **tile), :] = jnp.where(inside, results[c], 0.0)

    def first_core(self, visc_ref, vel_ref, force_ref, next_ref, coeff_ref, plane, **tile):
        force = force_ref[self.core(plane, **tile), :]
        faces, push, results = self.first_sweep(visc_ref, vel_ref, plane, force, **tile)
        for c in range(3):
            next_ref[self.plane(c, plane, **tile), :] = results[c]
        for k, value in enumerate((*faces, push)):
            coeff_ref[self.core(plane, k, **tile), :] = value

    def second_sweep(self, coeff_ref, next_ref, last_ref, plane, **tile):
        faces = [coeff_ref[self.core(plane, k, **tile), :] for k in range(6)]
        push = coeff_ref[self.core(plane, 6, **tile), :]
        for c in range(3):
            beside = self.around(next_ref, c, plane, **tile)
            vel = next_ref[self.plane(c, plane, **tile), :]
            value = relax(faces, push if c == 2 else None, vel, beside)
            last_ref[self.core(plane, c, **tile), :] = value


def widen_kernel(bricks, vel_ref, vx_low_ref, vx_high_ref, wide_ref):
    size_x = bricks[0]
    wide = Wide(bricks)
    for c in range(3):
        for plane in range(size_x):
            wide_ref[wide.plane(c, plane), :] = vel_ref[wide.core(plane, c), :]
        for plane in range(2):
            wide_ref[wide.plane(c, plane - 2), :] = vx_low_ref[wide.core(2 * c + plane), :]
            wide_ref[wide.plane(c, size_x + plane), :] = vx_high_ref[wide.core(2 * c + plane), :]


def interior_kernel(
    bricks,
    value_ref,
    ids_ref,
    old_ref,
    logvisc_ref,
    density_ref,
    force_ref,
    visc_ref,
    hot_ref,
):
    size_y = bricks[1]
    wide = Wide(bricks)
    columns, depth = old_ref.shape
    names = lax.broadcasted_iota(jnp.int32, (columns, depth), 0).astype(F32)
    for part in range(value_ref.shape[0] // depth):
        hot = jnp.where(names == ids_ref[part : part + 1, :], 1.0, 0.0)
        hot_ref[:, part * depth : (part + 1) * depth] = hot.astype(BF16)
    for tile in range(columns // depth):
        span = slice(tile * depth, (tile + 1) * depth)
        sums = jnp.dot(hot_ref[span, :], value_ref[...], preferred_element_type=F32)
        logvisc, density = averages(sums, depth, old_ref[span, :])
        visc = jnp.exp(logvisc)
        logvisc_ref[span, :] = logvisc
        density_ref[span, :] = density
        force_ref[span, :] = GRAVITY * (1.0 - density)
        for k in range(depth // size_y):
            plane = tile * (depth // size_y) + k
            visc_ref[wide.plane(0, plane), :] = visc[k * size_y : (k + 1) * size_y]


def sweep_kernel(
    bricks,
    visc_in,
    force_ref,
    wide_ref,
    y_even_ref,
    y_odd_ref,
    visc_ref,
    next_ref,
    coeff_ref,
    last_ref,
):
    size_x, size_y = bricks
    wide = Wide(bricks)
    odd_y = parities()[1]
    rows = ((odd_y == 1, y_even_ref), (odd_y == 0, y_odd_ref))
    for is_low, ref in rows:
        row = jnp.where(is_low, -1, size_y)
        visc_ref[wide.line(0, row), :] = ref[pl.ds(0, size_x), :]
        outer = jnp.where(is_low, -2, size_y + 1)
        visc_ref[wide.line(0, outer), :] = ref[pl.ds(size_x, size_x), :]
    for is_low, ref in rows:
        row = jnp.where(is_low, -1, size_y)
        visc = ref[pl.ds(0, size_x), :]
        force = ref[pl.ds(2 * size_x, size_x), :]
        faces, push = factors(visc, wide.around_line(visc_ref, 0, row), force)
        for c in range(3):
            vel = wide_ref[wide.line(c, row), :]
            beside = wide.around_line(wide_ref, c, row)
            value = relax(faces, push if c == 2 else None, vel, beside)
            next_ref[wide.line(c, row), :] = jnp.where(visc > 0.0, value, 0.0)
    for plane in range(1, size_x - 1):
        wide.first_core(visc_ref, wide_ref, force_ref, next_ref, coeff_ref, plane)
    for plane in range(2, size_x - 2):
        wide.second_sweep(coeff_ref, next_ref, last_ref, plane)


def finish_kernel(
    bricks,
    visc_in,
    next_in,
    coeff_in,
    last_in,
    wide_in,
    force_ref,
    x_even_ref,
    x_odd_ref,
    y_even_ref,
    y_odd_ref,
    out_ref,
    visc_ref,
    next_ref,
    coeff_ref,
    last_ref,
    wide_ref,
    sems,
):
    size_x, size_y = bricks
    wide = Wide(bricks)
    odd_x, odd_y = parities()
    whole = last_ref.reshape(3, size_x, size_y, last_ref.shape[1])
    copies = []
    for k, (first, stop) in enumerate(((2, size_x - 2), (0, 2), (size_x - 2, size_x))):
        at = (slice(None), slice(first, stop))
        copies.append(pltpu.make_async_copy(whole.at[at], out_ref.at[at], sems.at[k]))
    copies[0].start()

    sides = ((odd_x == 1, x_even_ref), (odd_x == 0, x_odd_ref))
    for is_low, ref in sides:
        first = jnp.where(is_low, -2, size_x)
        for k in range(2):
            visc_ref[wide.plane(0, first + k), :] = ref[pl.ds(k * size_y, size_y), :]
        plane = jnp.where(is_low, -1, size_x)
        for k, row in enumerate((-1, size_y)):
            at = 3 * size_y + 4 * k
            visc_ref[wide.cell(0, plane, row), :] = ref[at : at + 1, :]
            for c in range(3):
                wide_ref[wide.cell(c, plane, row), :] = ref[at + 1 + c : at + 2 + c, :]

    for plane in (0, size_x - 1):
        wide.first_core(visc_ref, wide_ref, force_ref, next_ref, coeff_ref, plane)
        at = slice(2 * size_x + plane, 2 * size_x + plane + 1)
        forces = (y_even_ref[at, :], y_odd_ref[at, :])
        for row, is_even in ((-1, odd_y == 1), (size_y, odd_y == 0)):
            force = jnp.where(is_even, *forces)
            wide.first_ring(visc_ref, wide_ref, next_ref, plane, force, row=row, rows=1)
    for is_low, ref in sides:
        plane = jnp.where(is_low, -1, size_x)
        force = ref[pl.ds(2 * size_y, size_y), :]
        wide.first_ring(visc_ref, wide_ref, next_ref, plane, force)

    for plane in (0, 1, size_x - 2, size_x - 1):
        wide.second_sweep(coeff_ref, next_ref, last_ref, plane)
        if plane == 1:
            copies[1].start()
    copies[2].start()
    for copy in copies:
        copy.wait()


def corner_kernel(
    bricks, even_in, odd_in, y_even_ref, y_odd_ref, wide_ref, x_even_ref, x_odd_ref
):
    size_x, size_y = bricks
    wide = Wide(bricks)
    odd_x, odd_y = parities()
    for ref, is_first in ((x_even_ref, odd_x == 1), (x_odd_ref, odd_x == 0)):
        near = jnp.where(is_first, 0, size_x - 1)
        pair = (y_even_ref[pl.ds(near, 1), :], y_odd_ref[pl.ds(near, 1), :])
        for k, row in enumerate((-1, size_y)):
            at = 3 * size_y + 4 * k
            ref[at : at + 1, :] = jnp.where(odd_y == 1 - k, *pair)
            for c in range(3):
                ref[at + 1 + c : at + 2 + c, :] = wide_ref[wide.cell(c, near, row), :]

    @pl.when(at_end("gx"))
    def _():
        x_odd_ref[3 * size_y :, :] = jnp.zeros((CORNERS, x_odd_ref.shape[1]), F32)


def limit(mebibytes):
    return pltpu.CompilerParams(vmem_limit_bytes=mebibytes << 20)


def in_hbm(value):
    return pltpu.with_memory_space_constraint(value, pltpu.HBM)


def shifted(value, axis, step):
    count = lax.axis_size(axis)
    pairs = [(i, i + step) for i in range(count) if 0 <= i + step < count]
    return lax.ppermute(value, axis, pairs)


def swapped(value, axis, first):
    counts = {name: lax.axis_size(name) for name in BOTH}
    other = BOTH[1 - BOTH.index(axis)]
    pairs = []
    for i in range(counts[axis]):
        for j in range(counts[other]):
            partner, beside = i + 1 - 2 * ((i + first) % 2), j
            if not 0 <= partner < counts[axis]:
                partner, beside = i, j ^ 1
                if first == 0 or beside >= counts[other]:
                    continue
            ends = ((i, j), (partner, beside))
            if axis == BOTH[1]:
                ends = tuple(end[::-1] for end in ends)
            pairs.append(tuple(x * counts["gy"] + y for x, y in ends))
    return lax.ppermute(value, BOTH, pairs)


def per_device(
    marker_comp, marker_strain, marker_live, marker_cell, block_dest, old_logvisc, velocity
):
    count_x = lax.axis_size("gx")
    count_y = lax.axis_size("gy")
    devices = count_x * count_y
    blocks, marks = marker_comp.shape
    size_x, size_y, depth = old_logvisc.shape
    columns = size_x * size_y
    slots = 2 * blocks // devices
    chunk = 3 * slots + 1
    total = devices * slots
    lines = (blocks // marks, marks)

    payload = pl.pallas_call(
        functools.partial(pack_kernel, slots, chunk),
        out_shape=jax.ShapeDtypeStruct((devices * chunk, marks), F32),
        in_specs=[HBM] * 5,
        out_specs=VMEM,
        scratch_shapes=[
            pltpu.SMEM(lines, jnp.int32),
            pltpu.VMEM(lines, jnp.int32),
            pltpu.VMEM((48 * BATCH, marks), F32),
            pltpu.SemaphoreType.DMA,
            pltpu.VMEM(lines, jnp.int32),
            pltpu.VMEM((blocks, marks), F32),
            pltpu.VMEM((blocks, marks), F32),
            pltpu.VMEM((blocks, marks), jnp.int32),
            pltpu.VMEM((blocks, marks), jnp.int32),
            pltpu.SemaphoreType.DMA((5,)),
        ],
        compiler_params=limit(12),
        name="pack",
    )(
        in_hbm(block_dest.reshape(lines)),
        in_hbm(marker_comp),
        in_hbm(marker_strain),
        in_hbm(marker_live),
        in_hbm(marker_cell),
    )
    payload = payload.reshape(devices * chunk, 1, marks)
    received = lax.all_to_all(payload, BOTH, split_axis=0, concat_axis=0, tiled=True)
    received = received.reshape(devices * chunk, marks)

    def y_lines(near, far):
        pair = jnp.concatenate([velocity[:, :, near], velocity[:, :, far]], axis=1)
        return pair.reshape(6 * size_x, depth)

    def x_planes(first):
        return velocity[:, first : first + 2].reshape(6 * size_y, depth)

    vy_low = shifted(y_lines(size_y - 1, size_y - 2), "gy", 1)
    vy_high = shifted(y_lines(0, 1), "gy", -1)
    vx_low = shifted(x_planes(size_x - 2), "gx", 1)
    vx_high = shifted(x_planes(0), "gx", -1)

    bricks = (size_x, size_y)
    wide = Wide(bricks)

    def shape(rows, width=depth, kind=F32):
        return jax.ShapeDtypeStruct((rows, width), kind)

    wide_vel = pl.pallas_call(
        functools.partial(widen_kernel, bricks),
        out_shape=shape(3 * wide.field),
        in_specs=[VMEM] * 3,
        out_specs=VMEM,
        compiler_params=limit(8),
        name="widen",
    )(velocity.reshape(3 * columns, depth), vx_low, vx_high)
    received, wide_vel = lax.optimization_barrier((received, wide_vel))

    edge = 4 * (size_x + size_y)
    x_side, y_side = shape(3 * size_y + CORNERS), shape(3 * size_x)
    old = old_logvisc.reshape(columns, depth)
    x_even, x_odd, y_even, y_odd, values, ids, wide_vel = pl.pallas_call(
        functools.partial(edge_kernel, slots, chunk, bricks),
        out_shape=(
            *(x_side, x_side, y_side, y_side),
            shape(total, 5 * depth, BF16),
            shape(total // depth),
            shape(3 * wide.field),
        ),
        in_specs=[VMEM] * 5,
        out_specs=(VMEM,) * 7,
        input_output_aliases={4: 6},
        scratch_shapes=[
            pltpu.VMEM((edge, total), BF16),
            pltpu.VMEM((edge, depth), F32),
            pltpu.VMEM((edge, depth), F32),
        ],
        compiler_params=limit(16),
        name="edge",
    )(received, old, vy_low, vy_high, wide_vel)
    logvisc, density, force, visc = pl.pallas_call(
        functools.partial(interior_kernel, bricks),
        out_shape=(*(shape(columns),) * 3, shape(wide.field)),
        in_specs=[VMEM] * 3,
        out_specs=(VMEM,) * 4,
        scratch_shapes=[pltpu.VMEM((columns, total), BF16)],
        compiler_params=limit(16),
        name="interior",
    )(values, ids, old)
    y_even = swapped(y_even, "gy", 0)
    y_odd = swapped(y_odd, "gy", 1)
    y_even, y_odd, visc, force = lax.optimization_barrier((y_even, y_odd, visc, force))
    x_even, x_odd = pl.pallas_call(
        functools.partial(corner_kernel, bricks),
        out_shape=(x_side, x_side),
        in_specs=[VMEM] * 5,
        out_specs=(VMEM, VMEM),
        input_output_aliases={0: 0, 1: 1},
        compiler_params=limit(4),
        name="corners",
    )(x_even, x_odd, y_even, y_odd, wide_vel)
    visc, wide_next, coeff, last = pl.pallas_call(
        functools.partial(sweep_kernel, bricks),
        out_shape=(
            shape(wide.field),
            shape(3 * wide.field),
            shape(7 * columns),
            shape(3 * columns),
        ),
        in_specs=[VMEM] * 5,
        out_specs=(VMEM,) * 4,
        input_output_aliases={0: 0},
        compiler_params=limit(12),
        name="sweep",
    )(visc, force, wide_vel, y_even, y_odd)
    x_even = swapped(x_even, "gx", 0)
    x_odd = swapped(x_odd, "gx", 1)
    smoothed = pl.pallas_call(
        functools.partial(finish_kernel, bricks),
        out_shape=(
            jax.ShapeDtypeStruct(velocity.shape, F32),
            shape(wide.field),
            shape(3 * wide.field),
            shape(7 * columns),
            shape(3 * columns),
            shape(3 * wide.field),
        ),
        in_specs=[VMEM] * 10,
        out_specs=(HBM, *(VMEM,) * 5),
        scratch_shapes=[pltpu.SemaphoreType.DMA((3,))],
        input_output_aliases={0: 1, 1: 2, 2: 3, 3: 4, 4: 5},
        compiler_params=limit(12),
        name="finish",
    )(
        visc,
        wide_next,
        coeff,
        last,
        wide_vel,
        force,
        x_even,
        x_odd,
        y_even,
        y_odd,
    )[0]
    return (
        logvisc.reshape(old_logvisc.shape),
        density.reshape(old_logvisc.shape),
        smoothed,
    )


def solution(mesh):
    return jax.shard_map(
        per_device,
        mesh=mesh,
        in_specs=(
            P(("gx", "gy"), None),
            P(("gx", "gy"), None),
            P(("gx", "gy"), None),
            P(("gx", "gy"), None),
            P(("gx", "gy"), None),
            P("gx", "gy", None),
            P(None, "gx", "gy", None),
        ),
        out_specs=(P("gx", "gy", None), P("gx", "gy", None), P(None, "gx", "gy", None)),
        check_vma=False,
    )
```

```python
import functools

import jax
import jax.numpy as jnp
from jax import lax
from jax.experimental import pallas as pl
from jax.experimental.pallas import tpu as pltpu
from jax.sharding import PartitionSpec as P

LOG_HIGH = 1.5
LOG_LOW = -1.0
WEAKENING = 1.0
DENSITY_JUMP = 0.4
SOFTENING = 0.1
GRAVITY = 10.0
RELAX = 0.8
BOTH = ("gx", "gy")
F32 = jnp.float32
BF16 = jnp.bfloat16
VMEM = pl.BlockSpec(memory_space=pltpu.VMEM)
SMEM = pl.BlockSpec(memory_space=pltpu.SMEM)
HBM = pl.BlockSpec(memory_space=pltpu.HBM)
BY_LANES = (((1,), (1,)), ((), ()))
WAYS = 4
BATCH = 32
CORNERS = 8


def split(values):
    high = values.astype(BF16).astype(F32)
    return high, values - high


class Depth:
    def __init__(self, marks):
        self.marks = marks
        self.shift = marks.bit_length() - 1
        self.part = marks // WAYS
        self.low_bits = self.part.bit_length() - 1
        ids = lax.broadcasted_iota(jnp.int32, (self.part, marks), 0)
        self.fine_ids = ids.astype(F32).astype(BF16)
        self.row_ids = lax.broadcasted_iota(jnp.int32, (8, marks), 0)
        lane_ids = lax.broadcasted_iota(jnp.int32, (8, marks), 1)
        self.halves = [self.row_ids < 4, self.row_ids >= 4]
        self.spans = [
            (lane_ids >> self.low_bits) == ((self.row_ids + w) & (WAYS - 1)) for w in range(WAYS)
        ]

    def sums(self, fields, cell):
        marks, part = self.marks, self.part
        pieces = [piece for field in fields for piece in field]
        depth = cell & (marks - 1)
        coarse = ((depth >> self.low_bits) - self.row_ids) & (WAYS - 1)
        fine = (depth & (part - 1)).astype(F32)
        left, right = [], []
        for half in self.halves:
            lines = []
            for w in range(WAYS):
                mask = (coarse == w) & half
                lines += [jnp.where(mask, piece, 0.0) for piece in pieces]
            left.append(jnp.concatenate(lines, axis=0).astype(BF16))
        for first in (0, 4):
            lines = []
            for b in range(first, first + 4):
                line = jnp.broadcast_to(fine[b : b + 1, :], (16, marks)).astype(BF16)
                line = jnp.concatenate([line] * (part // 16), axis=0)
                lines.append(jnp.where(self.fine_ids == line, BF16(1.0), BF16(0.0)))
            right.append(jnp.concatenate(lines, axis=0))
        sums = lax.dot_general(
            jnp.concatenate(left, axis=1),
            jnp.concatenate(right, axis=1),
            BY_LANES,
            preferred_element_type=F32,
        )
        results, number = [], 0
        for field in fields:
            total = None
            for w in range(WAYS):
                rows = [(w * len(pieces) + number + p) * 8 for p in range(len(field))]
                value = sums[rows[0] : rows[0] + 8]
                for row in rows[1:]:
                    value = value + sums[row : row + 8]
                if w:
                    value = pltpu.roll(value, part * w, 1)
                total = value if total is None else jnp.where(self.spans[w], value, total)
            results.append(total)
            number += len(field)
        return results


def placed(blocks, count, compute, places, place_ref, sums_ref, out_ref, slots):
    def batch(step, g, f):
        first = ((step & 1) * BATCH + g) * (8 * count) + f * 8
        return pl.ds(pl.multiple_of(first, 8), 8)

    def put(step):
        for g in range(BATCH):
            rows = pl.ds(pl.multiple_of((step * BATCH + g) * 8, 8), 8)
            for f, value in enumerate(compute(rows)):
                sums_ref[batch(step, g, f), :] = value

    def place(step):
        for g in range(BATCH):
            group = step * BATCH + g
            values = [sums_ref[batch(step, g, f), :] for f in range(count)]
            for k in range(8):
                at = place_ref[group // 16, (group % 16) * 8 + k]
                for f in range(count):
                    out_ref[pl.ds(at + f * slots, 1), :] = values[f][k : k + 1]

    put(0)
    places.wait()

    def step(i, carry):
        place(i - 1)
        put(i)
        return carry

    steps = blocks // 8 // BATCH
    lax.fori_loop(1, steps, step, 0)
    place(steps - 1)


def count_kernel(slots, chunk, counts, dest_hbm, live_hbm, cell_hbm, *refs):
    size_x, size_y = counts
    plane_refs = refs[:size_y]
    (
        line_ref,
        ids_ref,
        rows_ref,
        place_ref,
        spot_ref,
        sums_ref,
        place_sem,
        dest_ref,
        live_ref,
        cell_ref,
        load_sem,
    ) = refs[size_y:]
    blocks, marks = live_ref.shape
    devices = size_x * size_y
    depth = Depth(marks)
    pairs = ((dest_hbm, dest_ref), (cell_hbm, cell_ref), (live_hbm, live_ref))
    loads = [pltpu.make_async_copy(*pair, load_sem.at[k]) for k, pair in enumerate(pairs)]
    for load in loads:
        load.start()
    rows_ref[...] = jnp.zeros_like(rows_ref)
    loads[0].wait()

    owner_ids = lax.broadcasted_iota(jnp.int32, (devices, marks), 0)
    rank_ids = lax.broadcasted_iota(jnp.int32, (slots, marks), 0)
    square = (marks, marks)
    before = lax.broadcasted_iota(jnp.int32, square, 0) < lax.broadcasted_iota(jnp.int32, square, 1)
    before = jnp.where(before, 1.0, 0.0).astype(BF16)
    seen = jnp.zeros((devices, 1), F32)
    owned, ranks = [], []
    own_y = lax.axis_index("gy")
    for k in range(blocks // marks):
        dest = dest_ref[k : k + 1, :]
        mine = owner_ids == dest
        hot = jnp.where(mine, 1.0, 0.0)
        earlier = jnp.dot(hot.astype(BF16), before, preferred_element_type=F32) + seen
        rank = jnp.sum(jnp.where(mine, earlier, 0.0), axis=0, keepdims=True).astype(jnp.int32)
        seen = seen + jnp.sum(hot, axis=1, keepdims=True)
        line_ref[k : k + 1, :] = dest * chunk + rank
        across = (dest & (size_y - 1)) ^ own_y
        along = dest >> (size_y.bit_length() - 1)
        spot_ref[k : k + 1, :] = (across * size_x + along) * slots + rank
        owned.append(mine)
        ranks.append(rank)
    places = pltpu.make_async_copy(spot_ref, place_ref, place_sem)
    places.start()
    for load in loads[1:]:
        load.wait()
    ids = jnp.zeros((devices, slots), F32)
    for k, (mine, rank) in enumerate(zip(owned, ranks)):
        column = cell_ref[k * marks : (k + 1) * marks, :] >> depth.shift
        column = column.astype(F32).T[0:1] + 1.0
        spot = jnp.where(rank_ids == rank, 1.0, 0.0).astype(BF16)
        for piece in split(column):
            weighted = jnp.where(mine, piece, 0.0).astype(BF16)
            ids = ids + lax.dot_general(weighted, spot, BY_LANES, preferred_element_type=F32)
    ids_ref[...] = jnp.zeros_like(ids_ref)
    ids_ref[:, 0:slots] = ids - 1.0

    def compute(rows):
        weight = live_ref[rows, :].astype(F32)
        return depth.sums([(weight,)], cell_ref[rows, :])

    placed(blocks, 1, compute, places, place_ref, sums_ref, rows_ref, slots)
    for k, ref in enumerate(plane_refs):
        ref[...] = rows_ref[pl.ds(k * size_x * slots, size_x * slots), :]


def pack_kernel(
    slots,
    chunk,
    comp_hbm,
    strain_hbm,
    live_hbm,
    cell_hbm,
    line_ref,
    ids_ref,
    out_ref,
    place_ref,
    sums_ref,
    place_sem,
    comp_ref,
    strain_ref,
    live_ref,
    cell_ref,
    load_sem,
):
    blocks, marks = comp_ref.shape
    devices = out_ref.shape[0] // chunk
    depth = Depth(marks)
    pairs = (
        (comp_hbm, comp_ref),
        (strain_hbm, strain_ref),
        (live_hbm, live_ref),
        (cell_hbm, cell_ref),
    )
    loads = [pltpu.make_async_copy(*pair, load_sem.at[k]) for k, pair in enumerate(pairs)]
    for load in loads:
        load.start()
    places = pltpu.make_async_copy(line_ref, place_ref, place_sem)
    places.start()
    out_ref[...] = jnp.zeros_like(out_ref)
    for owner in range(devices):
        at = owner * chunk + 2 * slots
        out_ref[at : at + 1, :] = ids_ref[owner : owner + 1, :]
    for load in loads:
        load.wait()

    def compute(rows):
        comp = comp_ref[rows, :]
        strain = strain_ref[rows, :]
        weight = live_ref[rows, :].astype(F32)
        soften = strain / (1.0 + strain)
        logv = weight * (LOG_HIGH * comp + LOG_LOW * (1.0 - comp) - WEAKENING * soften)
        rho = weight * (1.0 + DENSITY_JUMP * comp - SOFTENING * soften)
        return depth.sums([split(logv), split(rho)], cell_ref[rows, :])

    placed(blocks, 2, compute, places, place_ref, sums_ref, out_ref, slots)


def regroup_kernel(slots, counts, *refs):
    size_x, size_y = counts
    own_x = lax.axis_index("gx")
    for k, out_ref in enumerate(refs[size_y:]):
        at = pl.multiple_of((own_x ^ k) * slots, 8)
        for j, ref in enumerate(refs[:size_y]):
            out_ref[j * slots : (j + 1) * slots, :] = ref[pl.ds(at, slots), :]


def gather_kernel(slots, counts, *refs):
    size_x, size_y = counts
    own_x, own_y = lax.axis_index("gx"), lax.axis_index("gy")
    out_ref = refs[size_x]
    for k, ref in enumerate(refs[:size_x]):
        for j in range(size_y):
            at = pl.multiple_of(((own_x ^ k) * size_y + (own_y ^ j)) * slots, 8)
            out_ref[pl.ds(at, slots), :] = ref[j * slots : (j + 1) * slots, :]


def parities():
    return lax.axis_index("gx") & 1, lax.axis_index("gy") & 1


def at_end(axis):
    place, last = lax.axis_index(axis), lax.axis_size(axis) - 1
    return (place == 0) | (place == last) if last % 2 else place == 0


def boundary_columns(size_x, size_y):
    return tuple((first, size_x, size_y) for first in (0, 1, size_y - 1, size_y - 2))


def averages(sums, depth, old):
    sum_logv = sums[:, 0:depth] + sums[:, depth : 2 * depth]
    sum_rho = sums[:, 2 * depth : 3 * depth] + sums[:, 3 * depth : 4 * depth]
    count = sums[:, 4 * depth : 5 * depth] + 1.0
    return (sum_logv + old) / count, (sum_rho + 1.0) / count


def edge_kernel(
    slots,
    chunk,
    bricks,
    recv_ref,
    count_ref,
    old_ref,
    y_even_ref,
    y_odd_ref,
    value_ref,
    ids_ref,
    hot_ref,
    visc_ref,
    force_ref,
):
    size_x, size_y = bricks
    depth = old_ref.shape[1]
    total = value_ref.shape[0]
    per = depth // slots
    lanes = lax.broadcasted_iota(jnp.int32, (1, depth), 1)
    runs = boundary_columns(size_x, size_y)
    names = []
    for first, count, stride in runs:
        names.append(lax.broadcasted_iota(jnp.int32, (count, depth), 0) * stride + first)
    names = jnp.concatenate(names, axis=0).astype(F32)
    for part in range(total // depth):
        span = slice(part * depth, (part + 1) * depth)
        ids = jnp.full((1, depth), -1.0, F32)
        for k in range(per):
            first = (part * per + k) * chunk
            line = recv_ref[first + 2 * slots : first + 2 * slots + 1, :]
            if k:
                line = pltpu.roll(line, k * slots, 1)
            ids = jnp.where((lanes >= k * slots) & (lanes < (k + 1) * slots), line, ids)
        ids_ref[part : part + 1, :] = ids
        hot_ref[:, span] = jnp.where(names == ids, 1.0, 0.0).astype(BF16)
        for v in range(2):
            lines = []
            for k in range(per):
                lines.append(recv_ref[pl.ds((part * per + k) * chunk + v * slots, slots), :])
            high, low = split(jnp.concatenate(lines, axis=0))
            value_ref[span, pl.ds(2 * v * depth, depth)] = high.astype(BF16)
            value_ref[span, pl.ds((2 * v + 1) * depth, depth)] = low.astype(BF16)
        value_ref[span, pl.ds(4 * depth, depth)] = count_ref[span, :].astype(BF16)
    sums = jnp.dot(hot_ref[...], value_ref[...], preferred_element_type=F32)
    old = []
    for first, count, stride in runs:
        old.append(old_ref[pl.ds(first, count, stride=stride), :])
    logvisc, density = averages(sums, depth, jnp.concatenate(old, axis=0))
    visc_ref[...] = jnp.exp(logvisc)
    force_ref[...] = GRAVITY * (1.0 - density)
    odd_y = parities()[1]
    for ref, is_first in ((y_even_ref, odd_y == 1), (y_odd_ref, odd_y == 0)):
        start = pl.multiple_of(jnp.where(is_first, 0, 2 * size_x), 8)
        ref[0 : 2 * size_x, :] = visc_ref[pl.ds(start, 2 * size_x), :]
        ref[2 * size_x :, :] = force_ref[pl.ds(start, size_x), :]

    @pl.when(at_end("gy"))
    def _():
        y_odd_ref[...] = jnp.zeros_like(y_odd_ref)


def factors(visc, beside, force):
    depth = visc.shape[1]
    lanes = lax.broadcasted_iota(jnp.int32, (1, depth), 1)
    up = jnp.where(lanes == depth - 1, 0.0, pltpu.roll(visc, depth - 1, 1))
    down = jnp.where(lanes == 0, 0.0, pltpu.roll(visc, 1, 1))
    faces = [visc + other for other in (*beside, up, down)]
    total = ((faces[0] + faces[1]) + (faces[2] + faces[3])) + (faces[4] + faces[5])
    scale = RELAX / total
    faces = [face * scale for face in faces]
    faces[4] = jnp.where(lanes == depth - 1, 0.0, faces[4])
    faces[5] = jnp.where(lanes == 0, 0.0, faces[5])
    return faces, 2.0 * force * scale


def relax(faces, push, vel, beside):
    depth = vel.shape[1]
    up = pltpu.roll(vel, depth - 1, 1)
    down = pltpu.roll(vel, 1, 1)
    terms = [face * other for face, other in zip(faces, (*beside, up, down))]
    result = ((terms[0] + terms[1]) + (terms[2] + terms[3])) + (terms[4] + terms[5])
    result = result + (1.0 - RELAX) * vel
    return result if push is None else result + push


class Wide:
    def __init__(self, bricks):
        self.size_x, self.size_y = bricks
        self.pitch = self.size_y + 16
        self.cells = self.size_x * self.size_y
        self.field = (self.size_x + 4) * self.pitch

    def plane(self, field, plane, dx=0, dy=0, row=0, rows=None):
        at = field * self.field + (plane + 2 + dx) * self.pitch + 8 + row
        if dy == 0 and row == 0 and not isinstance(at, int):
            at = pl.multiple_of(at, 8)
        return pl.ds(at + dy, rows or self.size_y)

    def cell(self, field, plane, row):
        return pl.ds(field * self.field + (plane + 2) * self.pitch + 8 + row, 1)

    def line(self, field, row, dx=0):
        at = field * self.field + (2 + dx) * self.pitch + 8 + row
        return pl.ds(at, self.size_x, stride=self.pitch)

    def around(self, ref, field, plane, **tile):
        steps = ((1, 0), (-1, 0), (0, 1), (0, -1))
        return tuple(ref[self.plane(field, plane, dx=dx, dy=dy, **tile), :] for dx, dy in steps)

    def core(self, plane, field=0, row=0, rows=None):
        return pl.ds(field * self.cells + plane * self.size_y + row, rows or self.size_y)

    def first_sweep(self, visc_ref, vel_ref, plane, force, **tile):
        visc = visc_ref[self.plane(0, plane, **tile), :]
        faces, push = factors(visc, self.around(visc_ref, 0, plane, **tile), force)
        results = []
        for c in range(3):
            vel = vel_ref[self.plane(c, plane, **tile), :]
            beside = self.around(vel_ref, c, plane, **tile)
            results.append(relax(faces, push if c == 2 else None, vel, beside))
        return faces, push, results

    def around_line(self, ref, field, row):
        places = (
            self.line(field, row, dx=1),
            self.line(field, row, dx=-1),
            self.line(field, row + 1),
            self.line(field, row - 1),
        )
        return tuple(ref[place, :] for place in places)

    def first_ring(self, visc_ref, vel_ref, next_ref, plane, force, **tile):
        _, _, results = self.first_sweep(visc_ref, vel_ref, plane, force, **tile)
        inside = visc_ref[self.plane(0, plane, **tile), :] > 0.0
        for c in range(3):
            next_ref[self.plane(c, plane, **tile), :] = jnp.where(inside, results[c], 0.0)

    def first_core(self, visc_ref, vel_ref, force_ref, next_ref, coeff_ref, plane, **tile):
        force = force_ref[self.core(plane, **tile), :]
        faces, push, results = self.first_sweep(visc_ref, vel_ref, plane, force, **tile)
        for c in range(3):
            next_ref[self.plane(c, plane, **tile), :] = results[c]
        for k, value in enumerate((*faces, push)):
            coeff_ref[self.core(plane, k, **tile), :] = value

    def second_sweep(self, coeff_ref, next_ref, last_ref, plane, **tile):
        faces = [coeff_ref[self.core(plane, k, **tile), :] for k in range(6)]
        push = coeff_ref[self.core(plane, 6, **tile), :]
        for c in range(3):
            beside = self.around(next_ref, c, plane, **tile)
            vel = next_ref[self.plane(c, plane, **tile), :]
            value = relax(faces, push if c == 2 else None, vel, beside)
            last_ref[self.core(plane, c, **tile), :] = value


def widen_kernel(bricks, vel_ref, vx_low_ref, vx_high_ref, wide_ref):
    size_x = bricks[0]
    wide = Wide(bricks)
    for c in range(3):
        for plane in range(size_x):
            wide_ref[wide.plane(c, plane), :] = vel_ref[wide.core(plane, c), :]
        for plane in range(2):
            wide_ref[wide.plane(c, plane - 2), :] = vx_low_ref[wide.core(2 * c + plane), :]
            wide_ref[wide.plane(c, size_x + plane), :] = vx_high_ref[wide.core(2 * c + plane), :]


def interior_kernel(
    bricks,
    value_ref,
    ids_ref,
    old_ref,
    logvisc_ref,
    density_ref,
    force_ref,
    visc_ref,
    x_even_ref,
    x_odd_ref,
    hot_ref,
):
    size_x, size_y = bricks
    wide = Wide(bricks)
    columns, depth = old_ref.shape
    names = lax.broadcasted_iota(jnp.int32, (columns, depth), 0).astype(F32)
    for part in range(value_ref.shape[0] // depth):
        hot = jnp.where(names == ids_ref[part : part + 1, :], 1.0, 0.0)
        hot_ref[:, part * depth : (part + 1) * depth] = hot.astype(BF16)
    for tile in range(columns // depth):
        span = slice(tile * depth, (tile + 1) * depth)
        sums = jnp.dot(hot_ref[span, :], value_ref[...], preferred_element_type=F32)
        logvisc, density = averages(sums, depth, old_ref[span, :])
        visc = jnp.exp(logvisc)
        logvisc_ref[span, :] = logvisc
        density_ref[span, :] = density
        force_ref[span, :] = GRAVITY * (1.0 - density)
        for k in range(depth // size_y):
            plane = tile * (depth // size_y) + k
            visc_ref[wide.plane(0, plane), :] = visc[k * size_y : (k + 1) * size_y]
    odd_x = parities()[0]
    for ref, is_first in ((x_even_ref, odd_x == 1), (x_odd_ref, odd_x == 0)):
        first = jnp.where(is_first, 0, size_x - 2)
        for k in range(2):
            ref[k * size_y : (k + 1) * size_y, :] = visc_ref[wide.plane(0, first + k), :]
        start = pl.multiple_of(jnp.where(is_first, 0, columns - size_y), 8)
        ref[2 * size_y : 3 * size_y, :] = force_ref[pl.ds(start, size_y), :]
        ref[3 * size_y :, :] = jnp.zeros((CORNERS, depth), F32)

    @pl.when(at_end("gx"))
    def _():
        x_odd_ref[...] = jnp.zeros_like(x_odd_ref)


def sweep_kernel(
    bricks,
    visc_in,
    wide_in,
    force_ref,
    vy_low_ref,
    vy_high_ref,
    y_even_ref,
    y_odd_ref,
    visc_ref,
    wide_ref,
    next_ref,
    coeff_ref,
    last_ref,
):
    size_x, size_y = bricks
    wide = Wide(bricks)
    for c in range(3):
        for ref, near, far in ((vy_low_ref, -1, -2), (vy_high_ref, size_y, size_y + 1)):
            for k, row in enumerate((near, far)):
                wide_ref[wide.line(c, row), :] = ref[pl.ds((2 * c + k) * size_x, size_x), :]
    odd_y = parities()[1]
    rows = ((odd_y == 1, y_even_ref), (odd_y == 0, y_odd_ref))
    for is_low, ref in rows:
        row = jnp.where(is_low, -1, size_y)
        visc_ref[wide.line(0, row), :] = ref[pl.ds(0, size_x), :]
        outer = jnp.where(is_low, -2, size_y + 1)
        visc_ref[wide.line(0, outer), :] = ref[pl.ds(size_x, size_x), :]
    for is_low, ref in rows:
        row = jnp.where(is_low, -1, size_y)
        visc = ref[pl.ds(0, size_x), :]
        force = ref[pl.ds(2 * size_x, size_x), :]
        faces, push = factors(visc, wide.around_line(visc_ref, 0, row), force)
        for c in range(3):
            vel = wide_ref[wide.line(c, row), :]
            beside = wide.around_line(wide_ref, c, row)
            value = relax(faces, push if c == 2 else None, vel, beside)
            next_ref[wide.line(c, row), :] = jnp.where(visc > 0.0, value, 0.0)
    for plane in range(1, size_x - 1):
        wide.first_core(visc_ref, wide_ref, force_ref, next_ref, coeff_ref, plane)
    for plane in range(2, size_x - 2):
        wide.second_sweep(coeff_ref, next_ref, last_ref, plane)


def finish_kernel(
    bricks,
    visc_in,
    next_in,
    coeff_in,
    last_in,
    wide_in,
    force_ref,
    x_even_ref,
    x_odd_ref,
    y_even_ref,
    y_odd_ref,
    out_ref,
    visc_ref,
    next_ref,
    coeff_ref,
    last_ref,
    wide_ref,
    sems,
):
    size_x, size_y = bricks
    wide = Wide(bricks)
    odd_x, odd_y = parities()
    whole = last_ref.reshape(3, size_x, size_y, last_ref.shape[1])
    copies = []
    for k, (first, stop) in enumerate(((2, size_x - 2), (0, 2), (size_x - 2, size_x))):
        at = (slice(None), slice(first, stop))
        copies.append(pltpu.make_async_copy(whole.at[at], out_ref.at[at], sems.at[k]))
    copies[0].start()

    sides = ((odd_x == 1, x_even_ref), (odd_x == 0, x_odd_ref))
    for is_low, ref in sides:
        first = jnp.where(is_low, -2, size_x)
        for k in range(2):
            visc_ref[wide.plane(0, first + k), :] = ref[pl.ds(k * size_y, size_y), :]
        plane = jnp.where(is_low, -1, size_x)
        for k, row in enumerate((-1, size_y)):
            at = 3 * size_y + 4 * k
            visc_ref[wide.cell(0, plane, row), :] = ref[at : at + 1, :]
            for c in range(3):
                wide_ref[wide.cell(c, plane, row), :] = ref[at + 1 + c : at + 2 + c, :]

    for plane in (0, size_x - 1):
        wide.first_core(visc_ref, wide_ref, force_ref, next_ref, coeff_ref, plane)
        at = slice(2 * size_x + plane, 2 * size_x + plane + 1)
        forces = (y_even_ref[at, :], y_odd_ref[at, :])
        for row, is_even in ((-1, odd_y == 1), (size_y, odd_y == 0)):
            force = jnp.where(is_even, *forces)
            wide.first_ring(visc_ref, wide_ref, next_ref, plane, force, row=row, rows=1)
    for is_low, ref in sides:
        plane = jnp.where(is_low, -1, size_x)
        force = ref[pl.ds(2 * size_y, size_y), :]
        wide.first_ring(visc_ref, wide_ref, next_ref, plane, force)

    for plane in (0, 1, size_x - 2, size_x - 1):
        wide.second_sweep(coeff_ref, next_ref, last_ref, plane)
        if plane == 1:
            copies[1].start()
    copies[2].start()
    for copy in copies:
        copy.wait()


def corner_kernel(
    bricks,
    even_in,
    odd_in,
    y_even_ref,
    y_odd_ref,
    vy_low_ref,
    vy_high_ref,
    x_even_ref,
    x_odd_ref,
):
    size_x, size_y = bricks
    odd_x, odd_y = parities()
    for ref, is_first in ((x_even_ref, odd_x == 1), (x_odd_ref, odd_x == 0)):
        near = jnp.where(is_first, 0, size_x - 1)
        pair = (y_even_ref[pl.ds(near, 1), :], y_odd_ref[pl.ds(near, 1), :])
        for k, lines_ref in enumerate((vy_low_ref, vy_high_ref)):
            at = 3 * size_y + 4 * k
            ref[at : at + 1, :] = jnp.where(odd_y == 1 - k, *pair)
            for c in range(3):
                ref[at + 1 + c : at + 2 + c, :] = lines_ref[pl.ds(2 * c * size_x + near, 1), :]

    @pl.when(at_end("gx"))
    def _():
        x_odd_ref[3 * size_y :, :] = jnp.zeros((CORNERS, x_odd_ref.shape[1]), F32)


def limit(mebibytes):
    return pltpu.CompilerParams(vmem_limit_bytes=mebibytes << 20)


def in_hbm(value):
    return pltpu.with_memory_space_constraint(value, pltpu.HBM)


def shifted(value, axis, step):
    count = lax.axis_size(axis)
    pairs = [(i, i + step) for i in range(count) if 0 <= i + step < count]
    return lax.ppermute(value, axis, pairs)


def swapped(value, axis, first):
    counts = {name: lax.axis_size(name) for name in BOTH}
    other = BOTH[1 - BOTH.index(axis)]
    pairs = []
    for i in range(counts[axis]):
        for j in range(counts[other]):
            partner, beside = i + 1 - 2 * ((i + first) % 2), j
            if not 0 <= partner < counts[axis]:
                partner, beside = i, j ^ 1
                if first == 0 or beside >= counts[other]:
                    continue
            ends = ((i, j), (partner, beside))
            if axis == BOTH[1]:
                ends = tuple(end[::-1] for end in ends)
            pairs.append(tuple(x * counts["gy"] + y for x, y in ends))
    return lax.ppermute(value, BOTH, pairs)


def crossed(value, axis, bits):
    pairs = [(i, i ^ bits) for i in range(lax.axis_size(axis))]
    return lax.ppermute(value, axis, pairs)


def per_device(
    marker_comp, marker_strain, marker_live, marker_cell, block_dest, old_logvisc, velocity
):
    count_x = lax.axis_size("gx")
    count_y = lax.axis_size("gy")
    devices = count_x * count_y
    blocks, marks = marker_comp.shape
    size_x, size_y, depth = old_logvisc.shape
    columns = size_x * size_y
    slots = 2 * blocks // devices
    chunk = 2 * slots + 1
    total = devices * slots
    lines = (blocks // marks, marks)
    counts = (count_x, count_y)

    def shape(rows, width=depth, kind=F32):
        return jax.ShapeDtypeStruct((rows, width), kind)

    def buffers(kinds):
        return [pltpu.VMEM((blocks, marks), kind) for kind in kinds]

    live, cell = in_hbm(marker_live), in_hbm(marker_cell)
    *planes, places, ids = pl.pallas_call(
        functools.partial(count_kernel, slots, chunk, counts),
        out_shape=(
            *(shape(count_x * slots),) * count_y,
            shape(*lines, jnp.int32),
            shape(devices),
        ),
        in_specs=[HBM] * 3,
        out_specs=(VMEM,) * (count_y + 2),
        scratch_shapes=[
            pltpu.VMEM((total, marks), F32),
            pltpu.SMEM(lines, jnp.int32),
            pltpu.VMEM(lines, jnp.int32),
            pltpu.VMEM((16 * BATCH, marks), F32),
            pltpu.SemaphoreType.DMA,
            pltpu.VMEM(lines, jnp.int32),
            *buffers((jnp.int32, jnp.int32)),
            pltpu.SemaphoreType.DMA((3,)),
        ],
        compiler_params=limit(12),
        name="count",
    )(in_hbm(block_dest.reshape(lines)), live, cell)
    for k in range(1, count_y):
        planes[k] = crossed(planes[k], "gy", k)
    payload = pl.pallas_call(
        functools.partial(pack_kernel, slots, chunk),
        out_shape=shape(devices * chunk),
        in_specs=[HBM] * 4 + [VMEM] * 2,
        out_specs=VMEM,
        scratch_shapes=[
            pltpu.SMEM(lines, jnp.int32),
            pltpu.VMEM((32 * BATCH, marks), F32),
            pltpu.SemaphoreType.DMA,
            *buffers((F32, F32, jnp.int32, jnp.int32)),
            pltpu.SemaphoreType.DMA((4,)),
        ],
        compiler_params=limit(12),
        cost_estimate=pl.CostEstimate(flops=10**11, bytes_accessed=1, transcendentals=0),
        name="pack",
    )(in_hbm(marker_comp), in_hbm(marker_strain), live, cell, places, ids)
    payload = payload.reshape(devices * chunk, 1, marks)
    received = lax.all_to_all(payload, BOTH, split_axis=0, concat_axis=0, tiled=True)
    received = received.reshape(devices * chunk, marks)

    messages = pl.pallas_call(
        functools.partial(regroup_kernel, slots, counts),
        out_shape=(shape(count_y * slots),) * count_x,
        in_specs=[VMEM] * count_y,
        out_specs=(VMEM,) * count_x,
        compiler_params=limit(4),
        cost_estimate=pl.CostEstimate(flops=10**11, bytes_accessed=1, transcendentals=0),
        name="regroup",
    )(*planes)
    messages, velocity = lax.optimization_barrier((messages, velocity))
    messages = [crossed(m, "gx", k) if k else m for k, m in enumerate(messages)]
    gathered = pl.pallas_call(
        functools.partial(gather_kernel, slots, counts),
        out_shape=shape(total),
        in_specs=[VMEM] * count_x,
        out_specs=VMEM,
        compiler_params=limit(4),
        name="gather",
    )(*messages)

    def y_lines(near, far):
        pair = jnp.concatenate([velocity[:, :, near], velocity[:, :, far]], axis=1)
        return pair.reshape(6 * size_x, depth)

    def x_planes(first):
        return velocity[:, first : first + 2].reshape(6 * size_y, depth)

    vy_low = shifted(y_lines(size_y - 1, size_y - 2), "gy", 1)
    vy_high = shifted(y_lines(0, 1), "gy", -1)
    vx_low = shifted(x_planes(size_x - 2), "gx", 1)
    vx_high = shifted(x_planes(0), "gx", -1)

    bricks = (size_x, size_y)
    wide = Wide(bricks)

    wide_vel = pl.pallas_call(
        functools.partial(widen_kernel, bricks),
        out_shape=shape(3 * wide.field),
        in_specs=[VMEM] * 3,
        out_specs=VMEM,
        compiler_params=limit(8),
        name="widen",
    )(velocity.reshape(3 * columns, depth), vx_low, vx_high)
    received, wide_vel, gathered = lax.optimization_barrier((received, wide_vel, gathered))

    edge = 4 * size_x
    x_side, y_side = shape(3 * size_y + CORNERS), shape(3 * size_x)
    old = old_logvisc.reshape(columns, depth)
    y_even, y_odd, values, ids = pl.pallas_call(
        functools.partial(edge_kernel, slots, chunk, bricks),
        out_shape=(
            *(y_side, y_side),
            shape(total, 5 * depth, BF16),
            shape(total // depth),
        ),
        in_specs=[VMEM] * 3,
        out_specs=(VMEM,) * 4,
        scratch_shapes=[
            pltpu.VMEM((edge, total), BF16),
            pltpu.VMEM((edge, depth), F32),
            pltpu.VMEM((edge, depth), F32),
        ],
        compiler_params=limit(16),
        cost_estimate=pl.CostEstimate(flops=1, bytes_accessed=1, transcendentals=0),
        name="edge",
    )(received, gathered, old)
    logvisc, density, force, visc, x_even, x_odd = pl.pallas_call(
        functools.partial(interior_kernel, bricks),
        out_shape=(*(shape(columns),) * 3, shape(wide.field), x_side, x_side),
        in_specs=[VMEM] * 3,
        out_specs=(VMEM,) * 6,
        scratch_shapes=[pltpu.VMEM((columns, total), BF16)],
        compiler_params=limit(16),
        cost_estimate=pl.CostEstimate(flops=1, bytes_accessed=1, transcendentals=0),
        name="interior",
    )(values, ids, old)
    y_even = swapped(y_even, "gy", 0)
    y_odd = swapped(y_odd, "gy", 1)
    y_even, y_odd, visc, force, x_even, x_odd = lax.optimization_barrier(
        (y_even, y_odd, visc, force, x_even, x_odd)
    )
    x_even, x_odd = pl.pallas_call(
        functools.partial(corner_kernel, bricks),
        out_shape=(x_side, x_side),
        in_specs=[VMEM] * 6,
        out_specs=(VMEM, VMEM),
        input_output_aliases={0: 0, 1: 1},
        compiler_params=limit(4),
        name="corners",
    )(x_even, x_odd, y_even, y_odd, vy_low, vy_high)
    visc, wide_vel, wide_next, coeff, last = pl.pallas_call(
        functools.partial(sweep_kernel, bricks),
        out_shape=(
            shape(wide.field),
            shape(3 * wide.field),
            shape(3 * wide.field),
            shape(7 * columns),
            shape(3 * columns),
        ),
        in_specs=[VMEM] * 7,
        out_specs=(VMEM,) * 5,
        input_output_aliases={0: 0, 1: 1},
        compiler_params=limit(12),
        name="sweep",
    )(visc, wide_vel, force, vy_low, vy_high, y_even, y_odd)
    x_even = swapped(x_even, "gx", 0)
    x_odd = swapped(x_odd, "gx", 1)
    smoothed = pl.pallas_call(
        functools.partial(finish_kernel, bricks),
        out_shape=(
            jax.ShapeDtypeStruct(velocity.shape, F32),
            shape(wide.field),
            shape(3 * wide.field),
            shape(7 * columns),
            shape(3 * columns),
            shape(3 * wide.field),
        ),
        in_specs=[VMEM] * 10,
        out_specs=(HBM, *(VMEM,) * 5),
        scratch_shapes=[pltpu.SemaphoreType.DMA((3,))],
        input_output_aliases={0: 1, 1: 2, 2: 3, 3: 4, 4: 5},
        compiler_params=limit(12),
        name="finish",
    )(
        visc,
        wide_next,
        coeff,
        last,
        wide_vel,
        force,
        x_even,
        x_odd,
        y_even,
        y_odd,
    )[0]
    return (
        logvisc.reshape(old_logvisc.shape),
        density.reshape(old_logvisc.shape),
        smoothed,
    )


def solution(mesh):
    return jax.shard_map(
        per_device,
        mesh=mesh,
        in_specs=(
            P(("gx", "gy"), None),
            P(("gx", "gy"), None),
            P(("gx", "gy"), None),
            P(("gx", "gy"), None),
            P(("gx", "gy"), None),
            P("gx", "gy", None),
            P(None, "gx", "gy", None),
        ),
        out_specs=(P("gx", "gy", None), P("gx", "gy", None), P(None, "gx", "gy", None)),
        check_vma=False,
    )
```

```python
import functools

import jax
import jax.numpy as jnp
from jax import lax
from jax.experimental import pallas as pl
from jax.experimental.pallas import tpu as pltpu
from jax.sharding import PartitionSpec as P

LOG_HIGH = 1.5
LOG_LOW = -1.0
WEAKENING = 1.0
DENSITY_JUMP = 0.4
SOFTENING = 0.1
GRAVITY = 10.0
RELAX = 0.8
BOTH = ("gx", "gy")
F32 = jnp.float32
BF16 = jnp.bfloat16
VMEM = pl.BlockSpec(memory_space=pltpu.VMEM)
SMEM = pl.BlockSpec(memory_space=pltpu.SMEM)
HBM = pl.BlockSpec(memory_space=pltpu.HBM)
BY_LANES = (((1,), (1,)), ((), ()))
WAYS = 4
BATCH = 32
CORNERS = 8


def split(values):
    high = values.astype(BF16).astype(F32)
    return high, values - high


class Depth:
    def __init__(self, marks):
        self.marks = marks
        self.shift = marks.bit_length() - 1
        self.part = marks // WAYS
        self.low_bits = self.part.bit_length() - 1
        ids = lax.broadcasted_iota(jnp.int32, (self.part, marks), 0)
        self.fine_ids = ids.astype(F32).astype(BF16)
        self.row_ids = lax.broadcasted_iota(jnp.int32, (8, marks), 0)
        lane_ids = lax.broadcasted_iota(jnp.int32, (8, marks), 1)
        self.halves = [self.row_ids < 4, self.row_ids >= 4]
        self.spans = [
            (lane_ids >> self.low_bits) == ((self.row_ids + w) & (WAYS - 1)) for w in range(WAYS)
        ]

    def sums(self, fields, cell):
        marks, part = self.marks, self.part
        pieces = [piece for field in fields for piece in field]
        depth = cell & (marks - 1)
        coarse = ((depth >> self.low_bits) - self.row_ids) & (WAYS - 1)
        fine = (depth & (part - 1)).astype(F32)
        left, right = [], []
        for half in self.halves:
            lines = []
            for w in range(WAYS):
                mask = (coarse == w) & half
                lines += [jnp.where(mask, piece, 0.0) for piece in pieces]
            left.append(jnp.concatenate(lines, axis=0).astype(BF16))
        for first in (0, 4):
            lines = []
            for b in range(first, first + 4):
                line = jnp.broadcast_to(fine[b : b + 1, :], (16, marks)).astype(BF16)
                line = jnp.concatenate([line] * (part // 16), axis=0)
                lines.append(jnp.where(self.fine_ids == line, BF16(1.0), BF16(0.0)))
            right.append(jnp.concatenate(lines, axis=0))
        sums = lax.dot_general(
            jnp.concatenate(left, axis=1),
            jnp.concatenate(right, axis=1),
            BY_LANES,
            preferred_element_type=F32,
        )
        results, number = [], 0
        for field in fields:
            total = None
            for w in range(WAYS):
                rows = [(w * len(pieces) + number + p) * 8 for p in range(len(field))]
                value = sums[rows[0] : rows[0] + 8]
                for row in rows[1:]:
                    value = value + sums[row : row + 8]
                if w:
                    value = pltpu.roll(value, part * w, 1)
                total = value if total is None else jnp.where(self.spans[w], value, total)
            results.append(total)
            number += len(field)
        return results


def placed(blocks, count, compute, places, place_ref, sums_ref, out_ref, slots):
    def batch(step, g, f):
        first = ((step & 1) * BATCH + g) * (8 * count) + f * 8
        return pl.ds(pl.multiple_of(first, 8), 8)

    def put(step):
        for g in range(BATCH):
            rows = pl.ds(pl.multiple_of((step * BATCH + g) * 8, 8), 8)
            for f, value in enumerate(compute(rows)):
                sums_ref[batch(step, g, f), :] = value

    def place(step):
        for g in range(BATCH):
            group = step * BATCH + g
            values = [sums_ref[batch(step, g, f), :] for f in range(count)]
            for k in range(8):
                at = place_ref[group // 16, (group % 16) * 8 + k]
                for f in range(count):
                    out_ref[pl.ds(at + f * slots, 1), :] = values[f][k : k + 1]

    put(0)
    places.wait()

    def step(i, carry):
        place(i - 1)
        put(i)
        return carry

    steps = blocks // 8 // BATCH
    lax.fori_loop(1, steps, step, 0)
    place(steps - 1)


def count_kernel(slots, chunk, counts, dest_hbm, live_hbm, cell_hbm, *refs):
    size_x, size_y = counts
    plane_refs = refs[:size_y]
    (
        line_ref,
        rows_ref,
        ids_ref,
        place_ref,
        spot_ref,
        sums_ref,
        place_sem,
        dest_ref,
        live_ref,
        cell_ref,
        load_sem,
    ) = refs[size_y:]
    blocks, marks = live_ref.shape
    devices = size_x * size_y
    depth = Depth(marks)
    pairs = ((dest_hbm, dest_ref), (cell_hbm, cell_ref), (live_hbm, live_ref))
    loads = [pltpu.make_async_copy(*pair, load_sem.at[k]) for k, pair in enumerate(pairs)]
    for load in loads:
        load.start()
    rows_ref[...] = jnp.zeros_like(rows_ref)
    loads[0].wait()

    owner_ids = lax.broadcasted_iota(jnp.int32, (devices, marks), 0)
    rank_ids = lax.broadcasted_iota(jnp.int32, (slots, marks), 0)
    square = (marks, marks)
    before = lax.broadcasted_iota(jnp.int32, square, 0) < lax.broadcasted_iota(jnp.int32, square, 1)
    before = jnp.where(before, 1.0, 0.0).astype(BF16)
    seen = jnp.zeros((devices, 1), F32)
    owned, ranks = [], []
    own_y = lax.axis_index("gy")
    for k in range(blocks // marks):
        dest = dest_ref[k : k + 1, :]
        mine = owner_ids == dest
        hot = jnp.where(mine, 1.0, 0.0)
        earlier = jnp.dot(hot.astype(BF16), before, preferred_element_type=F32) + seen
        rank = jnp.sum(jnp.where(mine, earlier, 0.0), axis=0, keepdims=True).astype(jnp.int32)
        seen = seen + jnp.sum(hot, axis=1, keepdims=True)
        line_ref[k : k + 1, :] = dest * chunk + rank
        across = (dest & (size_y - 1)) ^ own_y
        along = dest >> (size_y.bit_length() - 1)
        spot_ref[k : k + 1, :] = (across * size_x + along) * slots + rank
        owned.append(mine)
        ranks.append(rank)
    places = pltpu.make_async_copy(spot_ref, place_ref, place_sem)
    places.start()
    for load in loads[1:]:
        load.wait()
    ids = jnp.zeros((devices, slots), F32)
    for k, (mine, rank) in enumerate(zip(owned, ranks)):
        column = cell_ref[k * marks : (k + 1) * marks, :] >> depth.shift
        column = column.astype(F32).T[0:1] + 1.0
        spot = jnp.where(rank_ids == rank, 1.0, 0.0).astype(BF16)
        for piece in split(column):
            weighted = jnp.where(mine, piece, 0.0).astype(BF16)
            ids = ids + lax.dot_general(weighted, spot, BY_LANES, preferred_element_type=F32)
    ids = ids - 1.0
    for owner in range(devices):
        across, along = owner % size_y, owner // size_y
        at = pl.ds((across ^ own_y) * size_x + along, 1)
        ids_ref[at, 0:slots] = ids[owner : owner + 1, :]

    def compute(rows):
        weight = live_ref[rows, :].astype(F32)
        return depth.sums([(weight,)], cell_ref[rows, :])

    placed(blocks, 1, compute, places, place_ref, sums_ref, rows_ref, slots)
    for k, ref in enumerate(plane_refs):
        ref[0 : size_x * slots, :] = rows_ref[pl.ds(k * size_x * slots, size_x * slots), :]
        ref[size_x * slots :, :] = ids_ref[pl.ds(k * size_x, size_x), :]


def pack_kernel(
    slots,
    chunk,
    comp_hbm,
    strain_hbm,
    live_hbm,
    cell_hbm,
    line_ref,
    out_hbm,
    out_ref,
    place_ref,
    sums_ref,
    place_sem,
    out_sem,
    comp_ref,
    strain_ref,
    live_ref,
    cell_ref,
    load_sem,
):
    blocks, marks = comp_ref.shape
    depth = Depth(marks)
    pairs = (
        (comp_hbm, comp_ref),
        (strain_hbm, strain_ref),
        (live_hbm, live_ref),
        (cell_hbm, cell_ref),
    )
    loads = [pltpu.make_async_copy(*pair, load_sem.at[k]) for k, pair in enumerate(pairs)]
    for load in loads:
        load.start()
    places = pltpu.make_async_copy(line_ref, place_ref, place_sem)
    places.start()
    out_ref[...] = jnp.zeros_like(out_ref)
    for load in loads:
        load.wait()

    def compute(rows):
        comp = comp_ref[rows, :]
        strain = strain_ref[rows, :]
        weight = live_ref[rows, :].astype(F32)
        soften = strain / (1.0 + strain)
        logv = weight * (LOG_HIGH * comp + LOG_LOW * (1.0 - comp) - WEAKENING * soften)
        rho = weight * (1.0 + DENSITY_JUMP * comp - SOFTENING * soften)
        return depth.sums([split(logv), split(rho)], cell_ref[rows, :])

    placed(blocks, 2, compute, places, place_ref, sums_ref, out_ref, slots)
    copy = pltpu.make_async_copy(out_ref.at[pl.ds(0, out_hbm.shape[0])], out_hbm, out_sem)
    copy.start()
    copy.wait()


def regroup_kernel(slots, counts, *refs):
    size_x, size_y = counts
    own_x = lax.axis_index("gx")
    for k, out_ref in enumerate(refs[size_y:]):
        at = pl.multiple_of((own_x ^ k) * slots, 8)
        for j, ref in enumerate(refs[:size_y]):
            out_ref[j * slots : (j + 1) * slots, :] = ref[pl.ds(at, slots), :]
            line = ref[pl.ds(size_x * slots + (own_x ^ k), 1), :]
            out_ref[size_y * slots + j : size_y * slots + j + 1, :] = line


def gather_kernel(slots, counts, *refs):
    size_x, size_y = counts
    own_x, own_y = lax.axis_index("gx"), lax.axis_index("gy")
    out_ref = refs[size_x]
    for k, ref in enumerate(refs[:size_x]):
        for j in range(size_y):
            source = (own_x ^ k) * size_y + (own_y ^ j)
            at = pl.multiple_of(source * slots, 8)
            out_ref[pl.ds(at, slots), :] = ref[j * slots : (j + 1) * slots, :]
            line = ref[size_y * slots + j : size_y * slots + j + 1, :]
            out_ref[pl.ds(size_x * size_y * slots + source, 1), :] = line


def parities():
    return lax.axis_index("gx") & 1, lax.axis_index("gy") & 1


def at_end(axis):
    place, last = lax.axis_index(axis), lax.axis_size(axis) - 1
    return (place == 0) | (place == last) if last % 2 else place == 0


def boundary_columns(size_x, size_y):
    return tuple((first, size_x, size_y) for first in (0, 1, size_y - 1, size_y - 2))


def averages(sums, depth, old):
    sum_logv = sums[:, 0:depth] + sums[:, depth : 2 * depth]
    sum_rho = sums[:, 2 * depth : 3 * depth] + sums[:, 3 * depth : 4 * depth]
    count = sums[:, 4 * depth : 5 * depth] + 1.0
    return (sum_logv + old) / count, (sum_rho + 1.0) / count


def edge_kernel(
    slots,
    chunk,
    bricks,
    recv_ref,
    count_ref,
    old_ref,
    vel_ref,
    y_even_ref,
    y_odd_ref,
    value_ref,
    ids_ref,
    hot_ref,
    visc_ref,
    force_ref,
):
    size_x, size_y = bricks
    depth = old_ref.shape[1]
    total = value_ref.shape[0]
    per = depth // slots
    lanes = lax.broadcasted_iota(jnp.int32, (1, depth), 1)
    runs = boundary_columns(size_x, size_y)
    names = []
    for first, count, stride in runs:
        names.append(lax.broadcasted_iota(jnp.int32, (count, depth), 0) * stride + first)
    names = jnp.concatenate(names, axis=0).astype(F32)
    for part in range(total // depth):
        span = slice(part * depth, (part + 1) * depth)
        ids = jnp.full((1, depth), -1.0, F32)
        for k in range(per):
            at = total + part * per + k
            line = count_ref[at : at + 1, :]
            if k:
                line = pltpu.roll(line, k * slots, 1)
            ids = jnp.where((lanes >= k * slots) & (lanes < (k + 1) * slots), line, ids)
        ids_ref[part : part + 1, :] = ids
        hot_ref[:, span] = jnp.where(names == ids, 1.0, 0.0).astype(BF16)
        for v in range(2):
            lines = []
            for k in range(per):
                lines.append(recv_ref[pl.ds((part * per + k) * chunk + v * slots, slots), :])
            high, low = split(jnp.concatenate(lines, axis=0))
            value_ref[span, pl.ds(2 * v * depth, depth)] = high.astype(BF16)
            value_ref[span, pl.ds((2 * v + 1) * depth, depth)] = low.astype(BF16)
        value_ref[span, pl.ds(4 * depth, depth)] = count_ref[span, :].astype(BF16)
    sums = jnp.dot(hot_ref[...], value_ref[...], preferred_element_type=F32)
    old = []
    for first, count, stride in runs:
        old.append(old_ref[pl.ds(first, count, stride=stride), :])
    logvisc, density = averages(sums, depth, jnp.concatenate(old, axis=0))
    visc_ref[...] = jnp.exp(logvisc)
    force_ref[...] = GRAVITY * (1.0 - density)
    odd_y = parities()[1]
    for ref, is_first in ((y_even_ref, odd_y == 1), (y_odd_ref, odd_y == 0)):
        start = pl.multiple_of(jnp.where(is_first, 0, 2 * size_x), 8)
        ref[0 : 2 * size_x, :] = visc_ref[pl.ds(start, 2 * size_x), :]
        ref[2 * size_x : 3 * size_x, :] = force_ref[pl.ds(start, size_x), :]
        wide = Wide(bricks)
        for c in range(3):
            for k in range(2):
                row = jnp.where(is_first, k, size_y - 1 - k)
                at = (3 + 2 * c + k) * size_x
                ref[at : at + size_x, :] = vel_ref[wide.line(c, row), :]

    @pl.when(at_end("gy"))
    def _():
        y_odd_ref[...] = jnp.zeros_like(y_odd_ref)


def factors(visc, beside, force):
    depth = visc.shape[1]
    lanes = lax.broadcasted_iota(jnp.int32, (1, depth), 1)
    up = jnp.where(lanes == depth - 1, 0.0, pltpu.roll(visc, depth - 1, 1))
    down = jnp.where(lanes == 0, 0.0, pltpu.roll(visc, 1, 1))
    faces = [visc + other for other in (*beside, up, down)]
    total = ((faces[0] + faces[1]) + (faces[2] + faces[3])) + (faces[4] + faces[5])
    scale = RELAX / total
    faces = [face * scale for face in faces]
    faces[4] = jnp.where(lanes == depth - 1, 0.0, faces[4])
    faces[5] = jnp.where(lanes == 0, 0.0, faces[5])
    return faces, 2.0 * force * scale


def relax(faces, push, vel, beside):
    depth = vel.shape[1]
    up = pltpu.roll(vel, depth - 1, 1)
    down = pltpu.roll(vel, 1, 1)
    terms = [face * other for face, other in zip(faces, (*beside, up, down))]
    result = ((terms[0] + terms[1]) + (terms[2] + terms[3])) + (terms[4] + terms[5])
    result = result + (1.0 - RELAX) * vel
    return result if push is None else result + push


class Wide:
    def __init__(self, bricks):
        self.size_x, self.size_y = bricks
        self.pitch = self.size_y + 16
        self.cells = self.size_x * self.size_y
        self.field = (self.size_x + 4) * self.pitch

    def plane(self, field, plane, dx=0, dy=0, row=0, rows=None):
        at = field * self.field + (plane + 2 + dx) * self.pitch + 8 + row
        if dy == 0 and row == 0 and not isinstance(at, int):
            at = pl.multiple_of(at, 8)
        return pl.ds(at + dy, rows or self.size_y)

    def cell(self, field, plane, row):
        return pl.ds(field * self.field + (plane + 2) * self.pitch + 8 + row, 1)

    def line(self, field, row, dx=0):
        at = field * self.field + (2 + dx) * self.pitch + 8 + row
        return pl.ds(at, self.size_x, stride=self.pitch)

    def around(self, ref, field, plane, **tile):
        steps = ((1, 0), (-1, 0), (0, 1), (0, -1))
        return tuple(ref[self.plane(field, plane, dx=dx, dy=dy, **tile), :] for dx, dy in steps)

    def core(self, plane, field=0, row=0, rows=None):
        return pl.ds(field * self.cells + plane * self.size_y + row, rows or self.size_y)

    def first_sweep(self, visc_ref, vel_ref, plane, force, **tile):
        visc = visc_ref[self.plane(0, plane, **tile), :]
        faces, push = factors(visc, self.around(visc_ref, 0, plane, **tile), force)
        results = []
        for c in range(3):
            vel = vel_ref[self.plane(c, plane, **tile), :]
            beside = self.around(vel_ref, c, plane, **tile)
            results.append(relax(faces, push if c == 2 else None, vel, beside))
        return faces, push, results

    def around_line(self, ref, field, row):
        places = (
            self.line(field, row, dx=1),
            self.line(field, row, dx=-1),
            self.line(field, row + 1),
            self.line(field, row - 1),
        )
        return tuple(ref[place, :] for place in places)

    def first_ring(self, visc_ref, vel_ref, next_ref, plane, force, **tile):
        _, _, results = self.first_sweep(visc_ref, vel_ref, plane, force, **tile)
        inside = visc_ref[self.plane(0, plane, **tile), :] > 0.0
        for c in range(3):
            next_ref[self.plane(c, plane, **tile), :] = jnp.where(inside, results[c], 0.0)

    def first_core(self, visc_ref, vel_ref, force_ref, next_ref, coeff_ref, plane, **tile):
        force = force_ref[self.core(plane, **tile), :]
        faces, push, results = self.first_sweep(visc_ref, vel_ref, plane, force, **tile)
        for c in range(3):
            next_ref[self.plane(c, plane, **tile), :] = results[c]
        for k, value in enumerate((*faces, push)):
            coeff_ref[self.core(plane, k, **tile), :] = value

    def second_sweep(self, coeff_ref, next_ref, last_ref, plane, **tile):
        faces = [coeff_ref[self.core(plane, k, **tile), :] for k in range(6)]
        push = coeff_ref[self.core(plane, 6, **tile), :]
        for c in range(3):
            beside = self.around(next_ref, c, plane, **tile)
            vel = next_ref[self.plane(c, plane, **tile), :]
            value = relax(faces, push if c == 2 else None, vel, beside)
            last_ref[self.core(plane, c, **tile), :] = value


def widen_kernel(bricks, vel_ref, vx_low_ref, vx_high_ref, wide_ref):
    size_x = bricks[0]
    wide = Wide(bricks)
    for c in range(3):
        for plane in range(size_x):
            wide_ref[wide.plane(c, plane), :] = vel_ref[wide.core(plane, c), :]
        for plane in range(2):
            wide_ref[wide.plane(c, plane - 2), :] = vx_low_ref[wide.core(2 * c + plane), :]
            wide_ref[wide.plane(c, size_x + plane), :] = vx_high_ref[wide.core(2 * c + plane), :]


def interior_kernel(
    bricks,
    value_ref,
    ids_ref,
    old_ref,
    logvisc_ref,
    density_ref,
    force_ref,
    visc_ref,
    x_even_ref,
    x_odd_ref,
    hot_ref,
):
    size_x, size_y = bricks
    wide = Wide(bricks)
    columns, depth = old_ref.shape
    names = lax.broadcasted_iota(jnp.int32, (columns, depth), 0).astype(F32)
    for part in range(value_ref.shape[0] // depth):
        hot = jnp.where(names == ids_ref[part : part + 1, :], 1.0, 0.0)
        hot_ref[:, part * depth : (part + 1) * depth] = hot.astype(BF16)
    for tile in range(columns // depth):
        span = slice(tile * depth, (tile + 1) * depth)
        sums = jnp.dot(hot_ref[span, :], value_ref[...], preferred_element_type=F32)
        logvisc, density = averages(sums, depth, old_ref[span, :])
        visc = jnp.exp(logvisc)
        logvisc_ref[span, :] = logvisc
        density_ref[span, :] = density
        force_ref[span, :] = GRAVITY * (1.0 - density)
        for k in range(depth // size_y):
            plane = tile * (depth // size_y) + k
            visc_ref[wide.plane(0, plane), :] = visc[k * size_y : (k + 1) * size_y]
    odd_x = parities()[0]
    for ref, is_first in ((x_even_ref, odd_x == 1), (x_odd_ref, odd_x == 0)):
        first = jnp.where(is_first, 0, size_x - 2)
        for k in range(2):
            ref[k * size_y : (k + 1) * size_y, :] = visc_ref[wide.plane(0, first + k), :]
        start = pl.multiple_of(jnp.where(is_first, 0, columns - size_y), 8)
        ref[2 * size_y : 3 * size_y, :] = force_ref[pl.ds(start, size_y), :]
        ref[3 * size_y :, :] = jnp.zeros((CORNERS, depth), F32)

    @pl.when(at_end("gx"))
    def _():
        x_odd_ref[...] = jnp.zeros_like(x_odd_ref)


def sweep_kernel(
    bricks,
    visc_in,
    wide_in,
    force_ref,
    y_even_ref,
    y_odd_ref,
    visc_ref,
    wide_ref,
    next_ref,
    coeff_ref,
    last_ref,
):
    size_x, size_y = bricks
    wide = Wide(bricks)
    odd_y = parities()[1]
    rows = ((odd_y == 1, y_even_ref), (odd_y == 0, y_odd_ref))
    for is_low, ref in rows:
        row = jnp.where(is_low, -1, size_y)
        visc_ref[wide.line(0, row), :] = ref[pl.ds(0, size_x), :]
        outer = jnp.where(is_low, -2, size_y + 1)
        visc_ref[wide.line(0, outer), :] = ref[pl.ds(size_x, size_x), :]
        for c in range(3):
            at = (3 + 2 * c) * size_x
            wide_ref[wide.line(c, row), :] = ref[pl.ds(at, size_x), :]
            wide_ref[wide.line(c, outer), :] = ref[pl.ds(at + size_x, size_x), :]
    for is_low, ref in rows:
        row = jnp.where(is_low, -1, size_y)
        visc = ref[pl.ds(0, size_x), :]
        force = ref[pl.ds(2 * size_x, size_x), :]
        faces, push = factors(visc, wide.around_line(visc_ref, 0, row), force)
        for c in range(3):
            vel = wide_ref[wide.line(c, row), :]
            beside = wide.around_line(wide_ref, c, row)
            value = relax(faces, push if c == 2 else None, vel, beside)
            next_ref[wide.line(c, row), :] = jnp.where(visc > 0.0, value, 0.0)
    for plane in range(1, size_x - 1):
        wide.first_core(visc_ref, wide_ref, force_ref, next_ref, coeff_ref, plane)
    for plane in range(2, size_x - 2):
        wide.second_sweep(coeff_ref, next_ref, last_ref, plane)


def finish_kernel(
    bricks,
    visc_in,
    next_in,
    coeff_in,
    last_in,
    wide_in,
    force_ref,
    x_even_ref,
    x_odd_ref,
    y_even_ref,
    y_odd_ref,
    out_ref,
    visc_ref,
    next_ref,
    coeff_ref,
    last_ref,
    wide_ref,
    sems,
):
    size_x, size_y = bricks
    wide = Wide(bricks)
    odd_x, odd_y = parities()
    whole = last_ref.reshape(3, size_x, size_y, last_ref.shape[1])
    copies = []
    for k, (first, stop) in enumerate(((2, size_x - 2), (0, 2), (size_x - 2, size_x))):
        at = (slice(None), slice(first, stop))
        copies.append(pltpu.make_async_copy(whole.at[at], out_ref.at[at], sems.at[k]))
    copies[0].start()

    sides = ((odd_x == 1, x_even_ref), (odd_x == 0, x_odd_ref))
    for is_low, ref in sides:
        first = jnp.where(is_low, -2, size_x)
        for k in range(2):
            visc_ref[wide.plane(0, first + k), :] = ref[pl.ds(k * size_y, size_y), :]
        plane = jnp.where(is_low, -1, size_x)
        for k, row in enumerate((-1, size_y)):
            at = 3 * size_y + 4 * k
            visc_ref[wide.cell(0, plane, row), :] = ref[at : at + 1, :]
            for c in range(3):
                wide_ref[wide.cell(c, plane, row), :] = ref[at + 1 + c : at + 2 + c, :]

    for plane in (0, size_x - 1):
        wide.first_core(visc_ref, wide_ref, force_ref, next_ref, coeff_ref, plane)
        at = slice(2 * size_x + plane, 2 * size_x + plane + 1)
        forces = (y_even_ref[at, :], y_odd_ref[at, :])
        for row, is_even in ((-1, odd_y == 1), (size_y, odd_y == 0)):
            force = jnp.where(is_even, *forces)
            wide.first_ring(visc_ref, wide_ref, next_ref, plane, force, row=row, rows=1)
    for is_low, ref in sides:
        plane = jnp.where(is_low, -1, size_x)
        force = ref[pl.ds(2 * size_y, size_y), :]
        wide.first_ring(visc_ref, wide_ref, next_ref, plane, force)

    for plane in (0, 1, size_x - 2, size_x - 1):
        wide.second_sweep(coeff_ref, next_ref, last_ref, plane)
        if plane == 1:
            copies[1].start()
    copies[2].start()
    for copy in copies:
        copy.wait()


def corner_kernel(
    bricks,
    even_in,
    odd_in,
    y_even_ref,
    y_odd_ref,
    x_even_ref,
    x_odd_ref,
):
    size_x, size_y = bricks
    odd_x, odd_y = parities()
    for ref, is_first in ((x_even_ref, odd_x == 1), (x_odd_ref, odd_x == 0)):
        near = jnp.where(is_first, 0, size_x - 1)
        for c, line in enumerate((0, 3, 5, 7)):
            row = pl.ds(line * size_x + near, 1)
            pair = (y_even_ref[row, :], y_odd_ref[row, :])
            for k in range(2):
                at = 3 * size_y + 4 * k + c
                ref[at : at + 1, :] = jnp.where(odd_y == 1 - k, *pair)

    @pl.when(at_end("gx"))
    def _():
        x_odd_ref[3 * size_y :, :] = jnp.zeros((CORNERS, x_odd_ref.shape[1]), F32)


def limit(mebibytes):
    return pltpu.CompilerParams(vmem_limit_bytes=mebibytes << 20)


def in_hbm(value):
    return pltpu.with_memory_space_constraint(value, pltpu.HBM)


def shifted(value, axis, step):
    count = lax.axis_size(axis)
    pairs = [(i, i + step) for i in range(count) if 0 <= i + step < count]
    return lax.ppermute(value, axis, pairs)


def swapped(value, axis, first):
    counts = {name: lax.axis_size(name) for name in BOTH}
    other = BOTH[1 - BOTH.index(axis)]
    pairs = []
    for i in range(counts[axis]):
        for j in range(counts[other]):
            partner, beside = i + 1 - 2 * ((i + first) % 2), j
            if not 0 <= partner < counts[axis]:
                partner, beside = i, j ^ 1
                if first == 0 or beside >= counts[other]:
                    continue
            ends = ((i, j), (partner, beside))
            if axis == BOTH[1]:
                ends = tuple(end[::-1] for end in ends)
            pairs.append(tuple(x * counts["gy"] + y for x, y in ends))
    return lax.ppermute(value, BOTH, pairs)


def crossed(value, axis, bits):
    pairs = [(i, i ^ bits) for i in range(lax.axis_size(axis))]
    return lax.ppermute(value, axis, pairs)


def per_device(
    marker_comp, marker_strain, marker_live, marker_cell, block_dest, old_logvisc, velocity
):
    count_x = lax.axis_size("gx")
    count_y = lax.axis_size("gy")
    devices = count_x * count_y
    blocks, marks = marker_comp.shape
    size_x, size_y, depth = old_logvisc.shape
    columns = size_x * size_y
    slots = 2 * blocks // devices
    chunk = 2 * slots
    total = devices * slots
    lines = (blocks // marks, marks)
    counts = (count_x, count_y)

    def shape(rows, width=depth, kind=F32):
        return jax.ShapeDtypeStruct((rows, width), kind)

    def buffers(kinds):
        return [pltpu.VMEM((blocks, marks), kind) for kind in kinds]

    live, cell = in_hbm(marker_live), in_hbm(marker_cell)
    spare = -(-count_y // 8) * 8
    *planes, places = pl.pallas_call(
        functools.partial(count_kernel, slots, chunk, counts),
        out_shape=(
            *(shape(count_x * (slots + 1)),) * count_y,
            shape(*lines, jnp.int32),
        ),
        in_specs=[HBM] * 3,
        out_specs=(VMEM,) * (count_y + 1),
        scratch_shapes=[
            pltpu.VMEM((total + 8, marks), F32),
            pltpu.VMEM((devices + 8, marks), F32),
            pltpu.SMEM(lines, jnp.int32),
            pltpu.VMEM(lines, jnp.int32),
            pltpu.VMEM((16 * BATCH, marks), F32),
            pltpu.SemaphoreType.DMA,
            pltpu.VMEM(lines, jnp.int32),
            *buffers((jnp.int32, jnp.int32)),
            pltpu.SemaphoreType.DMA((3,)),
        ],
        compiler_params=limit(12),
        name="count",
    )(in_hbm(block_dest.reshape(lines)), live, cell)
    for k in range(1, count_y):
        planes[k] = crossed(planes[k], "gy", k)
    payload = pl.pallas_call(
        functools.partial(pack_kernel, slots, chunk),
        out_shape=pltpu.HBM((devices * chunk, marks), F32),
        in_specs=[HBM] * 4 + [VMEM],
        out_specs=HBM,
        scratch_shapes=[
            pltpu.VMEM((devices * chunk + 8, marks), F32),
            pltpu.SMEM(lines, jnp.int32),
            pltpu.VMEM((32 * BATCH, marks), F32),
            pltpu.SemaphoreType.DMA,
            pltpu.SemaphoreType.DMA,
            *buffers((F32, F32, jnp.int32, jnp.int32)),
            pltpu.SemaphoreType.DMA((4,)),
        ],
        compiler_params=limit(12),
        cost_estimate=pl.CostEstimate(flops=10**11, bytes_accessed=1, transcendentals=0),
        name="pack",
    )(in_hbm(marker_comp), in_hbm(marker_strain), live, cell, places)
    payload = payload.reshape(devices * chunk, 1, marks)
    received = lax.all_to_all(payload, BOTH, split_axis=0, concat_axis=0, tiled=True)
    received = received.reshape(devices * chunk, marks)

    messages = pl.pallas_call(
        functools.partial(regroup_kernel, slots, counts),
        out_shape=(shape(count_y * slots + spare),) * count_x,
        in_specs=[VMEM] * count_y,
        out_specs=(VMEM,) * count_x,
        compiler_params=limit(4),
        cost_estimate=pl.CostEstimate(flops=10**11, bytes_accessed=1, transcendentals=0),
        name="regroup",
    )(*planes)
    messages, velocity = lax.optimization_barrier((messages, velocity))
    messages = [crossed(m, "gx", k) if k else m for k, m in enumerate(messages)]
    gathered = pl.pallas_call(
        functools.partial(gather_kernel, slots, counts),
        out_shape=shape(total + devices + 8),
        in_specs=[VMEM] * count_x,
        out_specs=VMEM,
        compiler_params=limit(4),
        name="gather",
    )(*messages)

    def x_planes(first):
        return velocity[:, first : first + 2].reshape(6 * size_y, depth)

    vx_low = shifted(x_planes(size_x - 2), "gx", 1)
    vx_high = shifted(x_planes(0), "gx", -1)

    bricks = (size_x, size_y)
    wide = Wide(bricks)

    wide_vel = pl.pallas_call(
        functools.partial(widen_kernel, bricks),
        out_shape=shape(3 * wide.field),
        in_specs=[VMEM] * 3,
        out_specs=VMEM,
        compiler_params=limit(8),
        name="widen",
    )(velocity.reshape(3 * columns, depth), vx_low, vx_high)
    received, wide_vel, gathered = lax.optimization_barrier((received, wide_vel, gathered))

    edge = 4 * size_x
    x_side, y_side = shape(3 * size_y + CORNERS), shape(9 * size_x)
    old = old_logvisc.reshape(columns, depth)
    y_even, y_odd, values, ids = pl.pallas_call(
        functools.partial(edge_kernel, slots, chunk, bricks),
        out_shape=(
            *(y_side, y_side),
            shape(total, 5 * depth, BF16),
            shape(total // depth),
        ),
        in_specs=[VMEM] * 4,
        out_specs=(VMEM,) * 4,
        scratch_shapes=[
            pltpu.VMEM((edge, total), BF16),
            pltpu.VMEM((edge, depth), F32),
            pltpu.VMEM((edge, depth), F32),
        ],
        compiler_params=limit(16),
        cost_estimate=pl.CostEstimate(flops=1, bytes_accessed=1, transcendentals=0),
        name="edge",
    )(received, gathered, old, wide_vel)
    logvisc, density, force, visc, x_even, x_odd = pl.pallas_call(
        functools.partial(interior_kernel, bricks),
        out_shape=(*(shape(columns),) * 3, shape(wide.field), x_side, x_side),
        in_specs=[VMEM] * 3,
        out_specs=(VMEM,) * 6,
        scratch_shapes=[pltpu.VMEM((columns, total), BF16)],
        compiler_params=limit(16),
        cost_estimate=pl.CostEstimate(flops=1, bytes_accessed=1, transcendentals=0),
        name="interior",
    )(values, ids, old)
    y_even = swapped(y_even, "gy", 0)
    y_odd = swapped(y_odd, "gy", 1)
    y_even, y_odd, visc, force, x_even, x_odd = lax.optimization_barrier(
        (y_even, y_odd, visc, force, x_even, x_odd)
    )
    x_even, x_odd = pl.pallas_call(
        functools.partial(corner_kernel, bricks),
        out_shape=(x_side, x_side),
        in_specs=[VMEM] * 4,
        out_specs=(VMEM, VMEM),
        input_output_aliases={0: 0, 1: 1},
        compiler_params=limit(4),
        name="corners",
    )(x_even, x_odd, y_even, y_odd)
    visc, wide_vel, wide_next, coeff, last = pl.pallas_call(
        functools.partial(sweep_kernel, bricks),
        out_shape=(
            shape(wide.field),
            shape(3 * wide.field),
            shape(3 * wide.field),
            shape(7 * columns),
            shape(3 * columns),
        ),
        in_specs=[VMEM] * 5,
        out_specs=(VMEM,) * 5,
        input_output_aliases={0: 0, 1: 1},
        compiler_params=limit(12),
        name="sweep",
    )(visc, wide_vel, force, y_even, y_odd)
    x_even = swapped(x_even, "gx", 0)
    x_odd = swapped(x_odd, "gx", 1)
    smoothed = pl.pallas_call(
        functools.partial(finish_kernel, bricks),
        out_shape=(
            jax.ShapeDtypeStruct(velocity.shape, F32),
            shape(wide.field),
            shape(3 * wide.field),
            shape(7 * columns),
            shape(3 * columns),
            shape(3 * wide.field),
        ),
        in_specs=[VMEM] * 10,
        out_specs=(HBM, *(VMEM,) * 5),
        scratch_shapes=[pltpu.SemaphoreType.DMA((3,))],
        input_output_aliases={0: 1, 1: 2, 2: 3, 3: 4, 4: 5},
        compiler_params=limit(12),
        name="finish",
    )(
        visc,
        wide_next,
        coeff,
        last,
        wide_vel,
        force,
        x_even,
        x_odd,
        y_even,
        y_odd,
    )[0]
    return (
        logvisc.reshape(old_logvisc.shape),
        density.reshape(old_logvisc.shape),
        smoothed,
    )


def solution(mesh):
    return jax.shard_map(
        per_device,
        mesh=mesh,
        in_specs=(
            P(("gx", "gy"), None),
            P(("gx", "gy"), None),
            P(("gx", "gy"), None),
            P(("gx", "gy"), None),
            P(("gx", "gy"), None),
            P("gx", "gy", None),
            P(None, "gx", "gy", None),
        ),
        out_specs=(P("gx", "gy", None), P("gx", "gy", None), P(None, "gx", "gy", None)),
        check_vma=False,
    )
```

```python
import functools

import jax
import jax.numpy as jnp
from jax import lax
from jax.experimental import pallas as pl
from jax.experimental.pallas import tpu as pltpu
from jax.sharding import PartitionSpec as P

LOG_HIGH = 1.5
LOG_LOW = -1.0
WEAKENING = 1.0
DENSITY_JUMP = 0.4
SOFTENING = 0.1
GRAVITY = 10.0
RELAX = 0.8
BOTH = ("gx", "gy")
F32 = jnp.float32
BF16 = jnp.bfloat16
VMEM = pl.BlockSpec(memory_space=pltpu.VMEM)
SMEM = pl.BlockSpec(memory_space=pltpu.SMEM)
HBM = pl.BlockSpec(memory_space=pltpu.HBM)
BY_LANES = (((1,), (1,)), ((), ()))
WAYS = 4
BATCH = 32
CORNERS = 8


def split(values):
    high = values.astype(BF16).astype(F32)
    return high, values - high


class Depth:
    def __init__(self, marks):
        self.marks = marks
        self.shift = marks.bit_length() - 1
        self.part = marks // WAYS
        self.low_bits = self.part.bit_length() - 1
        ids = lax.broadcasted_iota(jnp.int32, (self.part, marks), 0)
        self.fine_ids = ids.astype(F32).astype(BF16)
        self.row_ids = lax.broadcasted_iota(jnp.int32, (8, marks), 0)
        lane_ids = lax.broadcasted_iota(jnp.int32, (8, marks), 1)
        self.halves = [self.row_ids < 4, self.row_ids >= 4]
        self.spans = [
            (lane_ids >> self.low_bits) == ((self.row_ids + w) & (WAYS - 1)) for w in range(WAYS)
        ]

    def sums(self, fields, cell):
        marks, part = self.marks, self.part
        pieces = [piece for field in fields for piece in field]
        depth = cell & (marks - 1)
        coarse = ((depth >> self.low_bits) - self.row_ids) & (WAYS - 1)
        fine = (depth & (part - 1)).astype(F32)
        left, right = [], []
        for half in self.halves:
            lines = []
            for w in range(WAYS):
                mask = (coarse == w) & half
                lines += [jnp.where(mask, piece, 0.0) for piece in pieces]
            left.append(jnp.concatenate(lines, axis=0).astype(BF16))
        for first in (0, 4):
            lines = []
            for b in range(first, first + 4):
                line = jnp.broadcast_to(fine[b : b + 1, :], (16, marks)).astype(BF16)
                line = jnp.concatenate([line] * (part // 16), axis=0)
                lines.append(jnp.where(self.fine_ids == line, BF16(1.0), BF16(0.0)))
            right.append(jnp.concatenate(lines, axis=0))
        sums = lax.dot_general(
            jnp.concatenate(left, axis=1),
            jnp.concatenate(right, axis=1),
            BY_LANES,
            preferred_element_type=F32,
        )
        results, number = [], 0
        for field in fields:
            total = None
            for w in range(WAYS):
                rows = [(w * len(pieces) + number + p) * 8 for p in range(len(field))]
                value = sums[rows[0] : rows[0] + 8]
                for row in rows[1:]:
                    value = value + sums[row : row + 8]
                if w:
                    value = pltpu.roll(value, part * w, 1)
                total = value if total is None else jnp.where(self.spans[w], value, total)
            results.append(total)
            number += len(field)
        return results


def placed(blocks, count, compute, places, place_ref, sums_ref, out_ref, slots):
    def batch(step, g, f):
        first = ((step & 1) * BATCH + g) * (8 * count) + f * 8
        return pl.ds(pl.multiple_of(first, 8), 8)

    def put(step):
        for g in range(BATCH):
            rows = pl.ds(pl.multiple_of((step * BATCH + g) * 8, 8), 8)
            for f, value in enumerate(compute(rows)):
                sums_ref[batch(step, g, f), :] = value

    def place(step):
        for g in range(BATCH):
            group = step * BATCH + g
            values = [sums_ref[batch(step, g, f), :] for f in range(count)]
            for k in range(8):
                at = place_ref[group // 16, (group % 16) * 8 + k]
                for f in range(count):
                    out_ref[pl.ds(at + f * slots, 1), :] = values[f][k : k + 1]

    put(0)
    places.wait()

    def step(i, carry):
        place(i - 1)
        put(i)
        return carry

    steps = blocks // 8 // BATCH
    lax.fori_loop(1, steps, step, 0)
    place(steps - 1)


def count_kernel(
    slots, chunk, counts, dest_hbm, live_hbm, cell_hbm, comp_hbm, strain_hbm, *refs
):
    size_x, size_y = counts
    plane_refs = refs[:size_y]
    (
        line_ref,
        live_ref,
        cell_ref,
        comp_ref,
        strain_ref,
        rows_ref,
        ids_ref,
        place_ref,
        spot_ref,
        sums_ref,
        place_sem,
        dest_ref,
        load_sem,
    ) = refs[size_y:]
    blocks, marks = live_ref.shape
    devices = size_x * size_y
    depth = Depth(marks)
    pairs = (
        (dest_hbm, dest_ref),
        (cell_hbm, cell_ref),
        (live_hbm, live_ref),
        (comp_hbm, comp_ref),
        (strain_hbm, strain_ref),
    )
    loads = [pltpu.make_async_copy(*pair, load_sem.at[k]) for k, pair in enumerate(pairs)]
    for load in loads:
        load.start()
    rows_ref[...] = jnp.zeros_like(rows_ref)
    loads[0].wait()

    owner_ids = lax.broadcasted_iota(jnp.int32, (devices, marks), 0)
    rank_ids = lax.broadcasted_iota(jnp.int32, (slots, marks), 0)
    square = (marks, marks)
    before = lax.broadcasted_iota(jnp.int32, square, 0) < lax.broadcasted_iota(jnp.int32, square, 1)
    before = jnp.where(before, 1.0, 0.0).astype(BF16)
    seen = jnp.zeros((devices, 1), F32)
    owned, ranks = [], []
    own_y = lax.axis_index("gy")
    for k in range(blocks // marks):
        dest = dest_ref[k : k + 1, :]
        mine = owner_ids == dest
        hot = jnp.where(mine, 1.0, 0.0)
        earlier = jnp.dot(hot.astype(BF16), before, preferred_element_type=F32) + seen
        rank = jnp.sum(jnp.where(mine, earlier, 0.0), axis=0, keepdims=True).astype(jnp.int32)
        seen = seen + jnp.sum(hot, axis=1, keepdims=True)
        line_ref[k : k + 1, :] = dest * chunk + rank
        across = (dest & (size_y - 1)) ^ own_y
        along = dest >> (size_y.bit_length() - 1)
        spot_ref[k : k + 1, :] = (across * size_x + along) * slots + rank
        owned.append(mine)
        ranks.append(rank)
    places = pltpu.make_async_copy(spot_ref, place_ref, place_sem)
    places.start()
    for load in loads[1:3]:
        load.wait()
    ids = jnp.zeros((devices, slots), F32)
    for k, (mine, rank) in enumerate(zip(owned, ranks)):
        column = cell_ref[k * marks : (k + 1) * marks, :] >> depth.shift
        column = column.astype(F32).T[0:1] + 1.0
        spot = jnp.where(rank_ids == rank, 1.0, 0.0).astype(BF16)
        for piece in split(column):
            weighted = jnp.where(mine, piece, 0.0).astype(BF16)
            ids = ids + lax.dot_general(weighted, spot, BY_LANES, preferred_element_type=F32)
    ids = ids - 1.0
    for owner in range(devices):
        across, along = owner % size_y, owner // size_y
        at = pl.ds((across ^ own_y) * size_x + along, 1)
        ids_ref[at, 0:slots] = ids[owner : owner + 1, :]

    def compute(rows):
        weight = live_ref[rows, :].astype(F32)
        return depth.sums([(weight,)], cell_ref[rows, :])

    placed(blocks, 1, compute, places, place_ref, sums_ref, rows_ref, slots)
    for k, ref in enumerate(plane_refs):
        ref[0 : size_x * slots, :] = rows_ref[pl.ds(k * size_x * slots, size_x * slots), :]
        ref[size_x * slots :, :] = ids_ref[pl.ds(k * size_x, size_x), :]
    for load in loads[3:]:
        load.wait()


def pack_kernel(
    slots,
    comp_ref,
    strain_ref,
    live_ref,
    cell_ref,
    line_ref,
    out_hbm,
    out_ref,
    place_ref,
    sums_ref,
    place_sem,
    out_sem,
):
    blocks, marks = comp_ref.shape
    depth = Depth(marks)
    places = pltpu.make_async_copy(line_ref, place_ref, place_sem)
    places.start()
    out_ref[...] = jnp.zeros_like(out_ref)

    def compute(rows):
        comp = comp_ref[rows, :]
        strain = strain_ref[rows, :]
        weight = live_ref[rows, :].astype(F32)
        soften = strain / (1.0 + strain)
        logv = weight * (LOG_HIGH * comp + LOG_LOW * (1.0 - comp) - WEAKENING * soften)
        rho = weight * (1.0 + DENSITY_JUMP * comp - SOFTENING * soften)
        return depth.sums([split(logv), split(rho)], cell_ref[rows, :])

    placed(blocks, 2, compute, places, place_ref, sums_ref, out_ref, slots)
    copy = pltpu.make_async_copy(out_ref.at[pl.ds(0, out_hbm.shape[0])], out_hbm, out_sem)
    copy.start()
    copy.wait()


def regroup_kernel(slots, counts, *refs):
    size_x, size_y = counts
    own_x = lax.axis_index("gx")
    for k, out_ref in enumerate(refs[size_y:]):
        at = pl.multiple_of((own_x ^ k) * slots, 8)
        for j, ref in enumerate(refs[:size_y]):
            out_ref[j * slots : (j + 1) * slots, :] = ref[pl.ds(at, slots), :]
            line = ref[pl.ds(size_x * slots + (own_x ^ k), 1), :]
            out_ref[size_y * slots + j : size_y * slots + j + 1, :] = line


def gather_kernel(slots, counts, *refs):
    size_x, size_y = counts
    own_x, own_y = lax.axis_index("gx"), lax.axis_index("gy")
    out_ref = refs[size_x]
    for k, ref in enumerate(refs[:size_x]):
        for j in range(size_y):
            source = (own_x ^ k) * size_y + (own_y ^ j)
            at = pl.multiple_of(source * slots, 8)
            out_ref[pl.ds(at, slots), :] = ref[j * slots : (j + 1) * slots, :]
            line = ref[size_y * slots + j : size_y * slots + j + 1, :]
            out_ref[pl.ds(size_x * size_y * slots + source, 1), :] = line


def parities():
    return lax.axis_index("gx") & 1, lax.axis_index("gy") & 1


def at_end(axis):
    place, last = lax.axis_index(axis), lax.axis_size(axis) - 1
    return (place == 0) | (place == last) if last % 2 else place == 0


def boundary_columns(size_x, size_y):
    return tuple((first, size_x, size_y) for first in (0, 1, size_y - 1, size_y - 2))


def averages(sums, depth, old):
    sum_logv = sums[:, 0:depth] + sums[:, depth : 2 * depth]
    sum_rho = sums[:, 2 * depth : 3 * depth] + sums[:, 3 * depth : 4 * depth]
    count = sums[:, 4 * depth : 5 * depth] + 1.0
    return (sum_logv + old) / count, (sum_rho + 1.0) / count


def edge_kernel(
    slots,
    chunk,
    bricks,
    recv_ref,
    count_ref,
    old_ref,
    vel_ref,
    y_even_ref,
    y_odd_ref,
    value_ref,
    ids_ref,
    hot_ref,
    visc_ref,
    force_ref,
):
    size_x, size_y = bricks
    depth = old_ref.shape[1]
    total = value_ref.shape[0]
    per = depth // slots
    lanes = lax.broadcasted_iota(jnp.int32, (1, depth), 1)
    runs = boundary_columns(size_x, size_y)
    names = []
    for first, count, stride in runs:
        names.append(lax.broadcasted_iota(jnp.int32, (count, depth), 0) * stride + first)
    names = jnp.concatenate(names, axis=0).astype(F32)
    for part in range(total // depth):
        span = slice(part * depth, (part + 1) * depth)
        ids = jnp.full((1, depth), -1.0, F32)
        for k in range(per):
            at = total + part * per + k
            line = count_ref[at : at + 1, :]
            if k:
                line = pltpu.roll(line, k * slots, 1)
            ids = jnp.where((lanes >= k * slots) & (lanes < (k + 1) * slots), line, ids)
        ids_ref[part : part + 1, :] = ids
        hot_ref[:, span] = jnp.where(names == ids, 1.0, 0.0).astype(BF16)
        for v in range(2):
            lines = []
            for k in range(per):
                lines.append(recv_ref[pl.ds((part * per + k) * chunk + v * slots, slots), :])
            high, low = split(jnp.concatenate(lines, axis=0))
            value_ref[span, pl.ds(2 * v * depth, depth)] = high.astype(BF16)
            value_ref[span, pl.ds((2 * v + 1) * depth, depth)] = low.astype(BF16)
        value_ref[span, pl.ds(4 * depth, depth)] = count_ref[span, :].astype(BF16)
    sums = jnp.dot(hot_ref[...], value_ref[...], preferred_element_type=F32)
    old = []
    for first, count, stride in runs:
        old.append(old_ref[pl.ds(first, count, stride=stride), :])
    logvisc, density = averages(sums, depth, jnp.concatenate(old, axis=0))
    visc_ref[...] = jnp.exp(logvisc)
    force_ref[...] = GRAVITY * (1.0 - density)
    odd_y = parities()[1]
    for ref, is_first in ((y_even_ref, odd_y == 1), (y_odd_ref, odd_y == 0)):
        start = pl.multiple_of(jnp.where(is_first, 0, 2 * size_x), 8)
        ref[0 : 2 * size_x, :] = visc_ref[pl.ds(start, 2 * size_x), :]
        ref[2 * size_x : 3 * size_x, :] = force_ref[pl.ds(start, size_x), :]
        wide = Wide(bricks)
        for c in range(3):
            for k in range(2):
                row = jnp.where(is_first, k, size_y - 1 - k)
                at = (3 + 2 * c + k) * size_x
                ref[at : at + size_x, :] = vel_ref[wide.line(c, row), :]

    @pl.when(at_end("gy"))
    def _():
        y_odd_ref[...] = jnp.zeros_like(y_odd_ref)


def factors(visc, beside, force):
    depth = visc.shape[1]
    lanes = lax.broadcasted_iota(jnp.int32, (1, depth), 1)
    up = jnp.where(lanes == depth - 1, 0.0, pltpu.roll(visc, depth - 1, 1))
    down = jnp.where(lanes == 0, 0.0, pltpu.roll(visc, 1, 1))
    faces = [visc + other for other in (*beside, up, down)]
    total = ((faces[0] + faces[1]) + (faces[2] + faces[3])) + (faces[4] + faces[5])
    scale = RELAX / total
    faces = [face * scale for face in faces]
    faces[4] = jnp.where(lanes == depth - 1, 0.0, faces[4])
    faces[5] = jnp.where(lanes == 0, 0.0, faces[5])
    return faces, 2.0 * force * scale


def relax(faces, push, vel, beside):
    depth = vel.shape[1]
    up = pltpu.roll(vel, depth - 1, 1)
    down = pltpu.roll(vel, 1, 1)
    terms = [face * other for face, other in zip(faces, (*beside, up, down))]
    result = ((terms[0] + terms[1]) + (terms[2] + terms[3])) + (terms[4] + terms[5])
    result = result + (1.0 - RELAX) * vel
    return result if push is None else result + push


class Wide:
    def __init__(self, bricks):
        self.size_x, self.size_y = bricks
        self.pitch = self.size_y + 16
        self.cells = self.size_x * self.size_y
        self.field = (self.size_x + 4) * self.pitch

    def plane(self, field, plane, dx=0, dy=0, row=0, rows=None):
        at = field * self.field + (plane + 2 + dx) * self.pitch + 8 + row
        if dy == 0 and row == 0 and not isinstance(at, int):
            at = pl.multiple_of(at, 8)
        return pl.ds(at + dy, rows or self.size_y)

    def cell(self, field, plane, row):
        return pl.ds(field * self.field + (plane + 2) * self.pitch + 8 + row, 1)

    def line(self, field, row, dx=0):
        at = field * self.field + (2 + dx) * self.pitch + 8 + row
        return pl.ds(at, self.size_x, stride=self.pitch)

    def around(self, ref, field, plane, **tile):
        steps = ((1, 0), (-1, 0), (0, 1), (0, -1))
        return tuple(ref[self.plane(field, plane, dx=dx, dy=dy, **tile), :] for dx, dy in steps)

    def core(self, plane, field=0, row=0, rows=None):
        return pl.ds(field * self.cells + plane * self.size_y + row, rows or self.size_y)

    def first_sweep(self, visc_ref, vel_ref, plane, force, **tile):
        visc = visc_ref[self.plane(0, plane, **tile), :]
        faces, push = factors(visc, self.around(visc_ref, 0, plane, **tile), force)
        results = []
        for c in range(3):
            vel = vel_ref[self.plane(c, plane, **tile), :]
            beside = self.around(vel_ref, c, plane, **tile)
            results.append(relax(faces, push if c == 2 else None, vel, beside))
        return faces, push, results

    def around_line(self, ref, field, row):
        places = (
            self.line(field, row, dx=1),
            self.line(field, row, dx=-1),
            self.line(field, row + 1),
            self.line(field, row - 1),
        )
        return tuple(ref[place, :] for place in places)

    def first_ring(self, visc_ref, vel_ref, next_ref, plane, force, **tile):
        _, _, results = self.first_sweep(visc_ref, vel_ref, plane, force, **tile)
        inside = visc_ref[self.plane(0, plane, **tile), :] > 0.0
        for c in range(3):
            next_ref[self.plane(c, plane, **tile), :] = jnp.where(inside, results[c], 0.0)

    def first_core(self, visc_ref, vel_ref, force_ref, next_ref, coeff_ref, plane, **tile):
        force = force_ref[self.core(plane, **tile), :]
        faces, push, results = self.first_sweep(visc_ref, vel_ref, plane, force, **tile)
        for c in range(3):
            next_ref[self.plane(c, plane, **tile), :] = results[c]
        for k, value in enumerate((*faces, push)):
            coeff_ref[self.core(plane, k, **tile), :] = value

    def second_sweep(self, coeff_ref, next_ref, last_ref, plane, **tile):
        faces = [coeff_ref[self.core(plane, k, **tile), :] for k in range(6)]
        push = coeff_ref[self.core(plane, 6, **tile), :]
        for c in range(3):
            beside = self.around(next_ref, c, plane, **tile)
            vel = next_ref[self.plane(c, plane, **tile), :]
            value = relax(faces, push if c == 2 else None, vel, beside)
            last_ref[self.core(plane, c, **tile), :] = value


def widen_kernel(bricks, vel_ref, vx_low_ref, vx_high_ref, wide_ref):
    size_x = bricks[0]
    wide = Wide(bricks)
    for c in range(3):
        for plane in range(size_x):
            wide_ref[wide.plane(c, plane), :] = vel_ref[wide.core(plane, c), :]
        for plane in range(2):
            wide_ref[wide.plane(c, plane - 2), :] = vx_low_ref[wide.core(2 * c + plane), :]
            wide_ref[wide.plane(c, size_x + plane), :] = vx_high_ref[wide.core(2 * c + plane), :]


def interior_kernel(
    bricks,
    value_ref,
    ids_ref,
    old_ref,
    logvisc_ref,
    density_ref,
    force_ref,
    visc_ref,
    x_even_ref,
    x_odd_ref,
    hot_ref,
):
    size_x, size_y = bricks
    wide = Wide(bricks)
    columns, depth = old_ref.shape
    names = lax.broadcasted_iota(jnp.int32, (columns, depth), 0).astype(F32)
    for part in range(value_ref.shape[0] // depth):
        hot = jnp.where(names == ids_ref[part : part + 1, :], 1.0, 0.0)
        hot_ref[:, part * depth : (part + 1) * depth] = hot.astype(BF16)
    for tile in range(columns // depth):
        span = slice(tile * depth, (tile + 1) * depth)
        sums = jnp.dot(hot_ref[span, :], value_ref[...], preferred_element_type=F32)
        logvisc, density = averages(sums, depth, old_ref[span, :])
        visc = jnp.exp(logvisc)
        logvisc_ref[span, :] = logvisc
        density_ref[span, :] = density
        force_ref[span, :] = GRAVITY * (1.0 - density)
        for k in range(depth // size_y):
            plane = tile * (depth // size_y) + k
            visc_ref[wide.plane(0, plane), :] = visc[k * size_y : (k + 1) * size_y]
    odd_x = parities()[0]
    for ref, is_first in ((x_even_ref, odd_x == 1), (x_odd_ref, odd_x == 0)):
        first = jnp.where(is_first, 0, size_x - 2)
        for k in range(2):
            ref[k * size_y : (k + 1) * size_y, :] = visc_ref[wide.plane(0, first + k), :]
        start = pl.multiple_of(jnp.where(is_first, 0, columns - size_y), 8)
        ref[2 * size_y : 3 * size_y, :] = force_ref[pl.ds(start, size_y), :]
        ref[3 * size_y :, :] = jnp.zeros((CORNERS, depth), F32)

    @pl.when(at_end("gx"))
    def _():
        x_odd_ref[...] = jnp.zeros_like(x_odd_ref)


def sweep_kernel(
    bricks,
    visc_in,
    wide_in,
    force_ref,
    y_even_ref,
    y_odd_ref,
    visc_ref,
    wide_ref,
    next_ref,
    coeff_ref,
    last_ref,
):
    size_x, size_y = bricks
    wide = Wide(bricks)
    odd_y = parities()[1]
    rows = ((odd_y == 1, y_even_ref), (odd_y == 0, y_odd_ref))
    for is_low, ref in rows:
        row = jnp.where(is_low, -1, size_y)
        visc_ref[wide.line(0, row), :] = ref[pl.ds(0, size_x), :]
        outer = jnp.where(is_low, -2, size_y + 1)
        visc_ref[wide.line(0, outer), :] = ref[pl.ds(size_x, size_x), :]
        for c in range(3):
            at = (3 + 2 * c) * size_x
            wide_ref[wide.line(c, row), :] = ref[pl.ds(at, size_x), :]
            wide_ref[wide.line(c, outer), :] = ref[pl.ds(at + size_x, size_x), :]
    for is_low, ref in rows:
        row = jnp.where(is_low, -1, size_y)
        visc = ref[pl.ds(0, size_x), :]
        force = ref[pl.ds(2 * size_x, size_x), :]
        faces, push = factors(visc, wide.around_line(visc_ref, 0, row), force)
        for c in range(3):
            vel = wide_ref[wide.line(c, row), :]
            beside = wide.around_line(wide_ref, c, row)
            value = relax(faces, push if c == 2 else None, vel, beside)
            next_ref[wide.line(c, row), :] = jnp.where(visc > 0.0, value, 0.0)
    for plane in range(1, size_x - 1):
        wide.first_core(visc_ref, wide_ref, force_ref, next_ref, coeff_ref, plane)
    for plane in range(2, size_x - 2):
        wide.second_sweep(coeff_ref, next_ref, last_ref, plane)


def finish_kernel(
    bricks,
    visc_in,
    next_in,
    coeff_in,
    last_in,
    wide_in,
    force_ref,
    x_even_ref,
    x_odd_ref,
    y_even_ref,
    y_odd_ref,
    out_ref,
    visc_ref,
    next_ref,
    coeff_ref,
    last_ref,
    wide_ref,
    sems,
):
    size_x, size_y = bricks
    wide = Wide(bricks)
    odd_x, odd_y = parities()
    whole = last_ref.reshape(3, size_x, size_y, last_ref.shape[1])
    copies = []
    for k, (first, stop) in enumerate(((2, size_x - 2), (0, 2), (size_x - 2, size_x))):
        at = (slice(None), slice(first, stop))
        copies.append(pltpu.make_async_copy(whole.at[at], out_ref.at[at], sems.at[k]))
    copies[0].start()

    sides = ((odd_x == 1, x_even_ref), (odd_x == 0, x_odd_ref))
    for is_low, ref in sides:
        first = jnp.where(is_low, -2, size_x)
        for k in range(2):
            visc_ref[wide.plane(0, first + k), :] = ref[pl.ds(k * size_y, size_y), :]
        plane = jnp.where(is_low, -1, size_x)
        for k, row in enumerate((-1, size_y)):
            at = 3 * size_y + 4 * k
            visc_ref[wide.cell(0, plane, row), :] = ref[at : at + 1, :]
            for c in range(3):
                wide_ref[wide.cell(c, plane, row), :] = ref[at + 1 + c : at + 2 + c, :]

    for plane in (0, size_x - 1):
        wide.first_core(visc_ref, wide_ref, force_ref, next_ref, coeff_ref, plane)
        at = slice(2 * size_x + plane, 2 * size_x + plane + 1)
        forces = (y_even_ref[at, :], y_odd_ref[at, :])
        for row, is_even in ((-1, odd_y == 1), (size_y, odd_y == 0)):
            force = jnp.where(is_even, *forces)
            wide.first_ring(visc_ref, wide_ref, next_ref, plane, force, row=row, rows=1)
    for is_low, ref in sides:
        plane = jnp.where(is_low, -1, size_x)
        force = ref[pl.ds(2 * size_y, size_y), :]
        wide.first_ring(visc_ref, wide_ref, next_ref, plane, force)

    for plane in (0, 1, size_x - 2, size_x - 1):
        wide.second_sweep(coeff_ref, next_ref, last_ref, plane)
        if plane == 1:
            copies[1].start()
    copies[2].start()
    for copy in copies:
        copy.wait()


def corner_kernel(
    bricks,
    even_in,
    odd_in,
    y_even_ref,
    y_odd_ref,
    x_even_ref,
    x_odd_ref,
):
    size_x, size_y = bricks
    odd_x, odd_y = parities()
    for ref, is_first in ((x_even_ref, odd_x == 1), (x_odd_ref, odd_x == 0)):
        near = jnp.where(is_first, 0, size_x - 1)
        for c, line in enumerate((0, 3, 5, 7)):
            row = pl.ds(line * size_x + near, 1)
            pair = (y_even_ref[row, :], y_odd_ref[row, :])
            for k in range(2):
                at = 3 * size_y + 4 * k + c
                ref[at : at + 1, :] = jnp.where(odd_y == 1 - k, *pair)

    @pl.when(at_end("gx"))
    def _():
        x_odd_ref[3 * size_y :, :] = jnp.zeros((CORNERS, x_odd_ref.shape[1]), F32)


def limit(mebibytes):
    return pltpu.CompilerParams(vmem_limit_bytes=mebibytes << 20)


def in_hbm(value):
    return pltpu.with_memory_space_constraint(value, pltpu.HBM)


def shifted(value, axis, step):
    count = lax.axis_size(axis)
    pairs = [(i, i + step) for i in range(count) if 0 <= i + step < count]
    return lax.ppermute(value, axis, pairs)


def swapped(value, axis, first):
    counts = {name: lax.axis_size(name) for name in BOTH}
    other = BOTH[1 - BOTH.index(axis)]
    pairs = []
    for i in range(counts[axis]):
        for j in range(counts[other]):
            partner, beside = i + 1 - 2 * ((i + first) % 2), j
            if not 0 <= partner < counts[axis]:
                partner, beside = i, j ^ 1
                if first == 0 or beside >= counts[other]:
                    continue
            ends = ((i, j), (partner, beside))
            if axis == BOTH[1]:
                ends = tuple(end[::-1] for end in ends)
            pairs.append(tuple(x * counts["gy"] + y for x, y in ends))
    return lax.ppermute(value, BOTH, pairs)


def crossed(value, axis, bits):
    pairs = [(i, i ^ bits) for i in range(lax.axis_size(axis))]
    return lax.ppermute(value, axis, pairs)


def per_device(
    marker_comp, marker_strain, marker_live, marker_cell, block_dest, old_logvisc, velocity
):
    count_x = lax.axis_size("gx")
    count_y = lax.axis_size("gy")
    devices = count_x * count_y
    blocks, marks = marker_comp.shape
    size_x, size_y, depth = old_logvisc.shape
    columns = size_x * size_y
    slots = 2 * blocks // devices
    chunk = 2 * slots
    total = devices * slots
    lines = (blocks // marks, marks)
    counts = (count_x, count_y)

    def shape(rows, width=depth, kind=F32):
        return jax.ShapeDtypeStruct((rows, width), kind)

    spare = -(-count_y // 8) * 8
    *planes, places, live, cell, comp, strain = pl.pallas_call(
        functools.partial(count_kernel, slots, chunk, counts),
        out_shape=(
            *(shape(count_x * (slots + 1)),) * count_y,
            shape(*lines, jnp.int32),
            *(shape(blocks, marks, jnp.int32),) * 2,
            *(shape(blocks, marks),) * 2,
        ),
        in_specs=[HBM] * 5,
        out_specs=(VMEM,) * (count_y + 5),
        scratch_shapes=[
            pltpu.VMEM((total + 8, marks), F32),
            pltpu.VMEM((devices + 8, marks), F32),
            pltpu.SMEM(lines, jnp.int32),
            pltpu.VMEM(lines, jnp.int32),
            pltpu.VMEM((16 * BATCH, marks), F32),
            pltpu.SemaphoreType.DMA,
            pltpu.VMEM(lines, jnp.int32),
            pltpu.SemaphoreType.DMA((5,)),
        ],
        compiler_params=limit(12),
        name="count",
    )(
        in_hbm(block_dest.reshape(lines)),
        in_hbm(marker_live),
        in_hbm(marker_cell),
        in_hbm(marker_comp),
        in_hbm(marker_strain),
    )
    for k in range(1, count_y):
        planes[k] = crossed(planes[k], "gy", k)
    payload = pl.pallas_call(
        functools.partial(pack_kernel, slots),
        out_shape=pltpu.HBM((devices * chunk, marks), F32),
        in_specs=[VMEM] * 5,
        out_specs=HBM,
        scratch_shapes=[
            pltpu.VMEM((devices * chunk + 8, marks), F32),
            pltpu.SMEM(lines, jnp.int32),
            pltpu.VMEM((32 * BATCH, marks), F32),
            pltpu.SemaphoreType.DMA,
            pltpu.SemaphoreType.DMA,
        ],
        compiler_params=limit(12),
        cost_estimate=pl.CostEstimate(flops=10**11, bytes_accessed=1, transcendentals=0),
        name="pack",
    )(comp, strain, live, cell, places)
    payload = payload.reshape(devices * chunk, 1, marks)
    received = lax.all_to_all(payload, BOTH, split_axis=0, concat_axis=0, tiled=True)
    received = received.reshape(devices * chunk, marks)

    messages = pl.pallas_call(
        functools.partial(regroup_kernel, slots, counts),
        out_shape=(shape(count_y * slots + spare),) * count_x,
        in_specs=[VMEM] * count_y,
        out_specs=(VMEM,) * count_x,
        compiler_params=limit(4),
        cost_estimate=pl.CostEstimate(flops=10**11, bytes_accessed=1, transcendentals=0),
        name="regroup",
    )(*planes)
    messages, velocity = lax.optimization_barrier((messages, velocity))
    messages = [crossed(m, "gx", k) if k else m for k, m in enumerate(messages)]
    gathered = pl.pallas_call(
        functools.partial(gather_kernel, slots, counts),
        out_shape=shape(total + devices + 8),
        in_specs=[VMEM] * count_x,
        out_specs=VMEM,
        compiler_params=limit(4),
        name="gather",
    )(*messages)

    def x_planes(first):
        return velocity[:, first : first + 2].reshape(6 * size_y, depth)

    vx_low = shifted(x_planes(size_x - 2), "gx", 1)
    vx_high = shifted(x_planes(0), "gx", -1)

    bricks = (size_x, size_y)
    wide = Wide(bricks)

    wide_vel = pl.pallas_call(
        functools.partial(widen_kernel, bricks),
        out_shape=shape(3 * wide.field),
        in_specs=[VMEM] * 3,
        out_specs=VMEM,
        compiler_params=limit(8),
        name="widen",
    )(velocity.reshape(3 * columns, depth), vx_low, vx_high)
    received, wide_vel, gathered = lax.optimization_barrier((received, wide_vel, gathered))

    edge = 4 * size_x
    x_side, y_side = shape(3 * size_y + CORNERS), shape(9 * size_x)
    old = old_logvisc.reshape(columns, depth)
    y_even, y_odd, values, ids = pl.pallas_call(
        functools.partial(edge_kernel, slots, chunk, bricks),
        out_shape=(
            *(y_side, y_side),
            shape(total, 5 * depth, BF16),
            shape(total // depth),
        ),
        in_specs=[VMEM] * 4,
        out_specs=(VMEM,) * 4,
        scratch_shapes=[
            pltpu.VMEM((edge, total), BF16),
            pltpu.VMEM((edge, depth), F32),
            pltpu.VMEM((edge, depth), F32),
        ],
        compiler_params=limit(16),
        cost_estimate=pl.CostEstimate(flops=1, bytes_accessed=1, transcendentals=0),
        name="edge",
    )(received, gathered, old, wide_vel)
    logvisc, density, force, visc, x_even, x_odd = pl.pallas_call(
        functools.partial(interior_kernel, bricks),
        out_shape=(*(shape(columns),) * 3, shape(wide.field), x_side, x_side),
        in_specs=[VMEM] * 3,
        out_specs=(VMEM,) * 6,
        scratch_shapes=[pltpu.VMEM((columns, total), BF16)],
        compiler_params=limit(16),
        cost_estimate=pl.CostEstimate(flops=1, bytes_accessed=1, transcendentals=0),
        name="interior",
    )(values, ids, old)
    y_even = swapped(y_even, "gy", 0)
    y_odd = swapped(y_odd, "gy", 1)
    y_even, y_odd, visc, force, x_even, x_odd = lax.optimization_barrier(
        (y_even, y_odd, visc, force, x_even, x_odd)
    )
    x_even, x_odd = pl.pallas_call(
        functools.partial(corner_kernel, bricks),
        out_shape=(x_side, x_side),
        in_specs=[VMEM] * 4,
        out_specs=(VMEM, VMEM),
        input_output_aliases={0: 0, 1: 1},
        compiler_params=limit(4),
        name="corners",
    )(x_even, x_odd, y_even, y_odd)
    visc, wide_vel, wide_next, coeff, last = pl.pallas_call(
        functools.partial(sweep_kernel, bricks),
        out_shape=(
            shape(wide.field),
            shape(3 * wide.field),
            shape(3 * wide.field),
            shape(7 * columns),
            shape(3 * columns),
        ),
        in_specs=[VMEM] * 5,
        out_specs=(VMEM,) * 5,
        input_output_aliases={0: 0, 1: 1},
        compiler_params=limit(12),
        name="sweep",
    )(visc, wide_vel, force, y_even, y_odd)
    x_even = swapped(x_even, "gx", 0)
    x_odd = swapped(x_odd, "gx", 1)
    smoothed = pl.pallas_call(
        functools.partial(finish_kernel, bricks),
        out_shape=(
            jax.ShapeDtypeStruct(velocity.shape, F32),
            shape(wide.field),
            shape(3 * wide.field),
            shape(7 * columns),
            shape(3 * columns),
            shape(3 * wide.field),
        ),
        in_specs=[VMEM] * 10,
        out_specs=(HBM, *(VMEM,) * 5),
        scratch_shapes=[pltpu.SemaphoreType.DMA((3,))],
        input_output_aliases={0: 1, 1: 2, 2: 3, 3: 4, 4: 5},
        compiler_params=limit(12),
        name="finish",
    )(
        visc,
        wide_next,
        coeff,
        last,
        wide_vel,
        force,
        x_even,
        x_odd,
        y_even,
        y_odd,
    )[0]
    return (
        logvisc.reshape(old_logvisc.shape),
        density.reshape(old_logvisc.shape),
        smoothed,
    )


def solution(mesh):
    return jax.shard_map(
        per_device,
        mesh=mesh,
        in_specs=(
            P(("gx", "gy"), None),
            P(("gx", "gy"), None),
            P(("gx", "gy"), None),
            P(("gx", "gy"), None),
            P(("gx", "gy"), None),
            P("gx", "gy", None),
            P(None, "gx", "gy", None),
        ),
        out_specs=(P("gx", "gy", None), P("gx", "gy", None), P(None, "gx", "gy", None)),
        check_vma=False,
    )
```
